128 devices in a mesh: section: 4 (over z), expert: 32 (over x, y, core).
Axes of the slice: x: 4, y: 4, z: 4, core: 2. Of those that a mesh axis runs over, the one named last changes fastest.
Arguments:
- tokens: bfloat16 [4096, 4096], P('expert'), may hold values from -6 to 6
- cotangent: bfloat16 [4096, 4096], P('expert'), may hold values from -6 to 6
- w_down: bfloat16 [4, 4096, 512], P('section', 'expert'), may hold values from -0.09375 to 0.09375
- w_up: bfloat16 [4, 512, 4096], P('section', 'expert'), may hold values from -0.25 to 0.25
- w_gate_up: bfloat16 [4, 32, 512, 2048], P('section', 'expert'), may hold values from -0.25 to 0.25
- w_out: bfloat16 [4, 32, 1024, 512], P('section', 'expert'), may hold values from -0.1875 to 0.1875
- routes: int32 [4, 4096, 2], P('section', 'expert'), may hold values from 0 to 31, all different within a row; in each aligned block of 128 rows (0 to 127, 128 to 255, ..., all dimensions but the last counted through in order) at most 12 rows name the same one
- gates: float32 [4, 4096, 2], P('section', 'expert'), may hold values from 0.3 to 1
- token_counts: int32 [4, 32], P('section', 'expert'), may hold values from 96 to 128, as said below
Outputs:
- layer_outputs: bfloat16 [4, 4096, 4096], P('section', 'expert')
- input_grads: bfloat16 [4, 4096, 4096], P('section', 'expert')
The draws below stay inside these ranges and needn't reach their ends.
Inputs may be any that keep to these rules, and one draw needn't show every extreme that they name: `routes`: A token's 2 experts differ. In each aligned block of 128 rows of a layer no expert is named by more than 12 rows. `token_counts`: in every layer some block has all 128 tokens live.
All inputs are finite; a program needn't handle non-finite values.
Results may differ from the reference program's by a relative error of at most 0.04.
Values may be sent and summed in bfloat16 or wider, within the bound.
A program may use at most 128 MiB of HBM per device.

```python
import math
import jax
import jax.numpy as jnp
import numpy as np
from jax import lax

D = 4096
L = 512
FFH = 1024
TOP = 2
TOK_DEV = 128
SECTIONS = 4
EXPERTS = 32
TOKENS = 4096
CAP = 12
N_EXPERT = 32


def draw_token_counts(key, part):
    key = jax.random.fold_in(key, 7)
    first_key, second_key = jax.random.split(key)
    values = jax.random.randint(first_key, (SECTIONS, N_EXPERT), 3 * TOK_DEV // 4, TOK_DEV + 1)
    picked = jax.random.randint(second_key, (SECTIONS, 1), 0, N_EXPERT)
    full = jnp.arange(N_EXPERT)[None, :] == picked
    return jnp.where(full, TOK_DEV, values).astype(jnp.int32)


def level_of(stream_key, extent, pieces, smallest, largest):
    def one(dim, parts):
        steps = jax.random.uniform(jax.random.fold_in(jax.random.fold_in(stream_key, 6), dim), (parts,), jnp.float32, smallest / len(pieces), largest / len(pieces))
        return jnp.repeat(jnp.exp(steps), extent[dim] // parts).reshape((-1,) + (1,) * (len(extent) - dim - 1))

    loudness = one(*pieces[0])
    for cut in pieces[1:]:
        loudness = loudness * one(*cut)
    return loudness


def assign_block(rng, own, number, rows, count, top, limit, lean):
    order = jax.random.permutation(rng, count)
    packed, ordinary = shares(count, rows * top, limit, lean, True), shares(count, rows * top, limit, lean, False)
    places = jnp.arange(count)

    def named(sizes, offset_by):
        used = int((sizes > 0).sum())
        fixed = max(1, used // 4)
        shifted = fixed + (places - fixed + offset_by * (used - fixed)) % max(1, count - fixed)
        return jnp.zeros((count,), jnp.int32).at[order[jnp.where(places < fixed, places, shifted)]].set(jnp.asarray(sizes, jnp.int32))

    sizes = jnp.where(number % 4 == 0, named(packed, number // 4), named(ordinary, number - number // 4 - 1))
    mixed = jax.random.permutation(jax.random.fold_in(own, 3), count)
    donor, taker = mixed[0:count // 2 * 2:2], mixed[1:count // 2 * 2:2]
    room = jnp.minimum(sizes[donor] - 1, limit - sizes[taker]) // 2
    room = jnp.where((donor == order[0]) | (taker == order[0]) | (sizes[taker] == 0), 0, jnp.maximum(room, 0))
    shifted = jax.random.randint(jax.random.fold_in(own, 4), (count // 2,), 0, 1 << 20) % (room + 1)
    sizes = sizes.at[donor].add(-shifted).at[taker].add(shifted)
    members = jnp.searchsorted(jnp.cumsum(sizes), jnp.arange(rows * top), side="right").astype(jnp.int32)
    table = members.reshape(top, rows).T
    table = table[jax.random.permutation(jax.random.fold_in(own, 1), rows)]
    offset_by = jax.random.randint(jax.random.fold_in(own, 2), (rows, 1), 0, top)
    return jnp.take_along_axis(table, (jnp.arange(top)[None, :] + offset_by) % top, axis=1)


def shares(number_of, total, bound, skew, full):
    weights = [(1 << 20) // math.isqrt(standing ** skew) + 1 for standing in range(1, number_of + 1)]
    largest = bound if full else min(bound, max(-(-total // number_of), total * weights[0] // sum(weights)))
    least = 1 if total - largest >= number_of - 1 else 0
    given, rest = [largest] + [least] * (number_of - 1), total - largest - least * (number_of - 1)
    while rest > 0:
        free = [i for i in range(1, number_of) if given[i] < largest] or [i for i in range(1, number_of) if given[i] < bound]
        whole, left = sum([weights[i] for i in free]), rest
        for i in free:
            more = min(bound - given[i], max(1, left * weights[i] // whole), rest)
            given[i] = given[i] + more
            rest = rest - more
    return np.array(given)


def noise(key, extent, spread, limit, shards=(), kind=jnp.bfloat16):
    values = spread * jax.random.normal(key, extent, jnp.float32)
    if shards:
        values = values * level_of(key, extent, shards, -0.22, 0.18)
    return jnp.clip(values, -limit, limit).astype(kind)


def setup_inputs(seed: int = 0) -> dict:
    keys = jax.random.split(jax.random.key(seed), 10)
    tokens = noise(keys[0], (TOKENS, D), 1.0, 6.0, ((0, 32),))
    cotangent = noise(keys[1], (TOKENS, D), 1.0, 6.0, ((0, 32),))
    w_down = noise(keys[2], (SECTIONS, D, L), D ** -0.5, 0.09375, ((0, 4), (1, 32)))
    w_up = noise(keys[3], (SECTIONS, L, D), L ** -0.5, 0.25, ((0, 4), (1, 32)))
    w_gate_up = noise(keys[4], (SECTIONS, EXPERTS, L, 2 * FFH), L ** -0.5, 0.25, ((0, 4), (1, 32)))
    w_out = noise(keys[5], (SECTIONS, EXPERTS, FFH, L), FFH ** -0.5, 0.1875, ((0, 4), (1, 32)))
    routes_keys = jax.random.split(jax.random.fold_in(keys[6], 1), SECTIONS * TOKENS // TOK_DEV)
    routes_turns = jax.random.permutation(jax.random.fold_in(keys[6], 3), SECTIONS * TOKENS // TOK_DEV)
    routes = jax.vmap(lambda own, number: assign_block(jax.random.fold_in(keys[6], 2), own, number, TOK_DEV, EXPERTS, TOP, CAP, 2))(routes_keys, routes_turns).reshape((SECTIONS, TOKENS, TOP))
    gates = jnp.clip(0.3 + 0.7 * jax.random.uniform(keys[7], (SECTIONS, TOKENS, TOP), jnp.float32) ** level_of(keys[7], (SECTIONS, TOKENS, TOP), ((0, 4), (1, 32)), -0.2, 0.2), 0.3, 1.0)
    token_counts = draw_token_counts(jax.random.fold_in(keys[9], 71), 0)
    return {"tokens": tokens, "cotangent": cotangent, "w_down": w_down, "w_up": w_up, "w_gate_up": w_gate_up, "w_out": w_out, "routes": routes, "gates": gates, "token_counts": token_counts}


EPS = 1e-05

def slots_for(route_ids, counts):
    per_block = route_ids.reshape(N_EXPERT, TOK_DEV * TOP)
    live = jnp.repeat(jnp.arange(TOK_DEV, dtype=jnp.int32)[None, :] < counts[:, None], TOP, axis=1)
    onehot = ((per_block[:, :, None] == jnp.arange(EXPERTS, dtype=jnp.int32)[None, None, :]) & live[:, :, None]).astype(jnp.int32)
    before = jnp.cumsum(onehot, axis=1, dtype=jnp.int32) - onehot
    slot = lax.optimization_barrier(jnp.sum(before * onehot, axis=2, dtype=jnp.int32))
    blocks = jnp.arange(N_EXPERT, dtype=jnp.int32)[:, None]
    dest = jnp.where(live, per_block * (N_EXPERT * CAP) + blocks * CAP + slot, EXPERTS * N_EXPERT * CAP)
    return (dest.reshape(-1).astype(jnp.int32), live.reshape(-1))

def expert_forward(rows, w_gate_up, w_out):
    width = w_out.shape[0]
    both = jnp.dot(rows, w_gate_up, preferred_element_type=jnp.float32)
    hidden = (jax.nn.silu(both[:, :width]) * both[:, width:]).astype(jnp.bfloat16)
    return jnp.dot(hidden, w_out, preferred_element_type=jnp.float32).astype(jnp.bfloat16)

def expert_backward(rows, grads, w_gate_up, w_out):
    width = w_out.shape[0]
    both = jnp.dot(rows, w_gate_up, preferred_element_type=jnp.float32)
    gate_part = both[:, :width]
    up_part = both[:, width:]
    sigma = jax.nn.sigmoid(gate_part)
    hidden_grad = lax.dot_general(grads, w_out, (((1,), (1,)), ((), ())), preferred_element_type=jnp.float32)
    gate_grad = hidden_grad * up_part * sigma * (1.0 + gate_part * (1.0 - sigma))
    up_grad = hidden_grad * gate_part * sigma
    joined = jnp.concatenate([gate_grad, up_grad], axis=1).astype(jnp.bfloat16)
    return lax.dot_general(joined, w_gate_up, (((1,), (1,)), ((), ())), preferred_element_type=jnp.float32).astype(jnp.bfloat16)

def gather_routes(outcome, dest, total):
    picked = jnp.take(outcome, jnp.minimum(dest, total - 1), axis=0)
    return picked.astype(jnp.float32).reshape(TOKENS, TOP, L)

def normalize(inputs):
    values = inputs.astype(jnp.float32)
    inv_rms = lax.rsqrt(lax.optimization_barrier(jnp.mean(values * values, axis=1, keepdims=True)) + EPS)
    return (values, inv_rms)

def layer_forward(inputs, proj_down, proj_up, expert_in, expert_back, dest, live, gate_vals):
    total = EXPERTS * N_EXPERT * CAP
    values, inv_rms = normalize(inputs)
    normed = (values * inv_rms).astype(jnp.bfloat16)
    latent = jnp.dot(normed, proj_down, preferred_element_type=jnp.float32).astype(jnp.bfloat16)
    rows = jnp.zeros((total, L), jnp.bfloat16).at[dest].set(jnp.repeat(latent, TOP, axis=0), mode='drop')
    outcome = lax.map(lambda group: expert_forward(group[0], group[1], group[2]), (rows.reshape(EXPERTS, -1, L), expert_in, expert_back))
    picked = gather_routes(outcome.reshape(total, L), dest, total)
    weights = gate_vals * live.reshape(TOKENS, TOP).astype(jnp.float32)
    mixed = lax.optimization_barrier(jnp.sum(weights[:, :, None] * picked, axis=1)).astype(jnp.bfloat16)
    result = (values + jnp.dot(mixed, proj_up, preferred_element_type=jnp.float32)).astype(jnp.bfloat16)
    return (result, rows)

def layer_backward(inputs, grad, rows, proj_down, proj_up, expert_in, expert_back, dest, live, gate_vals):
    total = EXPERTS * N_EXPERT * CAP
    values, inv_rms = normalize(inputs)
    weights = gate_vals * live.reshape(TOKENS, TOP).astype(jnp.float32)
    mix_grad = lax.dot_general(grad, proj_up, (((1,), (1,)), ((), ())), preferred_element_type=jnp.float32).astype(jnp.bfloat16)
    route_grad = (weights[:, :, None] * mix_grad[:, None, :].astype(jnp.float32)).astype(jnp.bfloat16).reshape(-1, L)
    grad_rows = jnp.zeros((total, L), jnp.bfloat16).at[dest].set(route_grad, mode='drop')
    lat_rows = lax.map(lambda group: expert_backward(group[0], group[1], group[2], group[3]), (rows.reshape(EXPERTS, -1, L), grad_rows.reshape(EXPERTS, -1, L), expert_in, expert_back))
    picked = gather_routes(lat_rows.reshape(total, L), dest, total)
    live_f = live.reshape(TOKENS, TOP).astype(jnp.float32)
    latent_grad = lax.optimization_barrier(jnp.sum(live_f[:, :, None] * picked, axis=1)).astype(jnp.bfloat16)
    normed_grad = lax.dot_general(latent_grad, proj_down, (((1,), (1,)), ((), ())), preferred_element_type=jnp.float32)
    unit = values * inv_rms
    dotted = lax.optimization_barrier(jnp.mean(normed_grad * unit, axis=1, keepdims=True))
    return (grad.astype(jnp.float32) + inv_rms * (normed_grad - unit * dotted)).astype(jnp.bfloat16)

def reference(tokens, cotangent, w_down, w_up, w_gate_up, w_out, routes, gates, token_counts):
    current = tokens
    inputs_kept = []
    rows_kept = []
    slot_kept = []
    outputs = []
    for layer in range(SECTIONS):
        dest, live = slots_for(routes[layer], token_counts[layer])
        result, rows = layer_forward(current, w_down[layer], w_up[layer], w_gate_up[layer], w_out[layer], dest, live, gates[layer])
        inputs_kept.append(current)
        rows_kept.append(rows)
        slot_kept.append((dest, live))
        outputs.append(result)
        current = result
    grad = cotangent
    grads = [None] * SECTIONS
    for layer in reversed(range(SECTIONS)):
        dest, live = slot_kept[layer]
        grad = layer_backward(inputs_kept[layer], grad, rows_kept[layer], w_down[layer], w_up[layer], w_gate_up[layer], w_out[layer], dest, live, gates[layer])
        grads[layer] = grad
    return (jnp.stack(outputs), jnp.stack(grads))
```

```python
import functools

import jax
import jax.numpy as jnp
from jax import lax
from jax.experimental import pallas as pl
from jax.experimental.pallas import tpu as pltpu
from jax.sharding import PartitionSpec as P

EPS = 1e-05
MESH = pl.DeviceIdType.MESH
BF = jnp.bfloat16
F32 = jnp.float32
SLOT = 16


def dot(a, b):
    return jnp.dot(a, b, preferred_element_type=F32)


def dot_t(a, b):
    return lax.dot_general(a, b, (((1,), (1,)), ((), ())), preferred_element_type=F32)


def kernel(
    sections, experts,
    tokens, cot, w_down, w_up, w_gu, w_o, routes, gates, counts,
    out, gin,
    up_full, down_full, down_first,
    x_in, g_in, g_new, g_fin,
    gate_f, up_f, hidden, joined,
    send_a, recv_a, send_b, recv_b, send_c, recv_c, send_d, recv_d,
    put, take0, take1,
    lat_in, lat_out, lg_in, lg_out, lat_f, inv_f,
    zs, zr, us, ur, ds, dr, fs, fr, as_, ar, hs, hr, loc,
):
    t = lax.axis_index("section")
    e = lax.axis_index("expert")
    x = e // 8
    y = (e // 2) % 4
    c = e % 2
    above = (t + 1) % sections
    below = (t + sections - 1) % sections
    toks, width = tokens.shape
    lat_w = lat_in.shape[1]
    ffh = w_o.shape[2]
    last = sections - 1

    def at(xx, yy, cc):
        return (t, (xx * 4 + yy) * 2 + cc)

    def send(src, dst, ssem, rsem, dev):
        pltpu.make_async_remote_copy(
            src_ref=src, dst_ref=dst, send_sem=ssem, recv_sem=rsem, device_id=dev, device_id_type=MESH
        ).start()

    def wait(ref, sem):
        pltpu.make_async_copy(ref, ref, sem).wait()

    barrier = pltpu.get_barrier_semaphore()

    def greet(k, carry):
        pl.semaphore_signal(barrier, inc=1, device_id=(t, (e + k) % experts), device_id_type=MESH)
        return carry

    lax.fori_loop(1, experts, greet, 0)
    pl.semaphore_signal(barrier, inc=1, device_id=(above, e), device_id_type=MESH)
    pl.semaphore_signal(barrier, inc=1, device_id=(below, e), device_id_type=MESH)
    pl.semaphore_wait(barrier, experts + 1)

    def first(buf, ha, hb, ss, rs):
        for d in range(1, 4):
            blk = buf.at[(x, y, c) + ha]
            send(blk, blk, ss.at[0], rs.at[0], at((x + d) % 4, y, c))
            blk = buf.at[(x, y, c) + hb]
            send(blk, blk, ss.at[1], rs.at[1], at(x, (y + d) % 4, c))

    def second(buf, ha, hb, ss, rs):
        wait(buf.at[(pl.ds(0, 3), 0, 0) + ha], rs.at[0])
        wait(buf.at[(pl.ds(0, 3), 0, 0) + hb], rs.at[1])
        for d in range(1, 4):
            blk = buf.at[(slice(None), y, c) + ha]
            send(blk, blk, ss.at[2], rs.at[2], at(x, (y + d) % 4, c))
            blk = buf.at[(x, slice(None), c) + hb]
            send(blk, blk, ss.at[3], rs.at[3], at((x + d) % 4, y, c))

    def third(buf, ha, hb, ss, rs):
        wait(buf.at[(pl.ds(0, 3), slice(None), 0) + ha], rs.at[2])
        wait(buf.at[(pl.ds(0, 3), slice(None), 0) + hb], rs.at[3])
        blk = buf.at[:, :, c]
        send(blk, blk, ss.at[4], rs.at[4], at(x, y, 1 - c))

    def fourth(buf, ss, rs):
        wait(buf.at[:, :, 0], rs.at[4])

    def gather_done(buf, ha, hb, ss):
        wait(buf.at[(pl.ds(0, 3), 0, 0) + ha], ss.at[0])
        wait(buf.at[(pl.ds(0, 3), 0, 0) + hb], ss.at[1])
        wait(buf.at[(pl.ds(0, 3), slice(None), 0) + ha], ss.at[2])
        wait(buf.at[(pl.ds(0, 3), slice(None), 0) + hb], ss.at[3])
        wait(buf.at[:, :, 0], ss.at[4])

    half_cols = width // 2
    u_a = (slice(None), pl.ds(0, half_cols))
    u_b = (slice(None), pl.ds(half_cols, half_cols))
    half_rows = w_down.shape[1] // 2
    d_a = (pl.ds(0, half_rows), slice(None))
    d_b = (pl.ds(half_rows, half_rows), slice(None))

    send(w_down.at[0], down_full.at[x, y, c], zs.at[0], zr.at[0], (below, e))
    up_full[x, y, c] = w_up[0]
    first(up_full, u_a, u_b, us, ur)
    wait(w_down.at[0], zr.at[0])
    first(down_full, d_a, d_b, ds, dr)

    @pl.when(t == 0)
    def _():
        x_in[...] = tokens[...]

    @pl.when(t == last - 1)
    def _():
        g_in[...] = cot[...]

    count = counts[...]
    expert_lane = lax.broadcasted_iota(jnp.int32, (toks, experts), 1)
    live = lax.broadcasted_iota(jnp.int32, (toks, experts), 0) < count
    one0 = jnp.where((routes[0, :, 0:1] == expert_lane) & live, 1.0, 0.0).astype(F32)
    one1 = jnp.where((routes[0, :, 1:2] == expert_lane) & live, 1.0, 0.0).astype(F32)
    below_diag = jnp.where(
        lax.broadcasted_iota(jnp.int32, (toks, toks), 0) > lax.broadcasted_iota(jnp.int32, (toks, toks), 1), 1.0, 0.0
    ).astype(BF)
    before = dot(below_diag, (one0 + one1).astype(BF))
    slots = experts * SLOT
    spread = jnp.where(
        lax.broadcasted_iota(jnp.int32, (experts, slots), 1) // SLOT
        == lax.broadcasted_iota(jnp.int32, (experts, slots), 0),
        1.0,
        0.0,
    ).astype(BF)
    slot_no = (lax.broadcasted_iota(jnp.int32, (toks, slots), 1) % SLOT).astype(F32)
    here = dot(before.astype(BF), spread) == slot_no
    pick0 = jnp.where(here, dot(one0.astype(BF), spread), 0.0)
    pick1 = jnp.where(here, dot(one1.astype(BF), spread), 0.0)
    take0[...] = pick0.astype(BF)
    take1[...] = pick1.astype(BF)
    put[:, 0:toks] = pick0.T.astype(BF)
    put[:, toks : 2 * toks] = pick1.T.astype(BF)
    gate0 = gates[0, :, 0:1]
    gate1 = gates[0, :, 1:2]

    second(down_full, d_a, d_b, ds, dr)
    second(up_full, u_a, u_b, us, ur)
    third(down_full, d_a, d_b, ds, dr)
    fourth(down_full, ds, dr)

    chunk = 512
    n_chunks = width // chunk

    def up_chunk(j):
        return up_full[:, :, :, :, j * chunk : (j + 1) * chunk].reshape(lat_w, chunk)

    def down_chunk(buf, j):
        return buf[j // 2, 2 * (j % 2) : 2 * (j % 2) + 2].reshape(chunk, lat_w)

    @pl.when(t == last)
    def _():
        total = jnp.zeros((toks, lat_w), F32)
        square = jnp.zeros((toks, 1), F32)
        for j in range(n_chunks):
            part = tokens[:, j * chunk : (j + 1) * chunk]
            total += dot(part, down_chunk(down_full, j))
            wide = part.astype(F32)
            square += jnp.sum(wide * wide, axis=1, keepdims=True)
        inv = lax.rsqrt(square / width + EPS)
        lat_out[...] = (total * inv).astype(BF)
        send(lat_out, lat_in, hs.at[0], hr.at[0], (above, e))

    third(up_full, u_a, u_b, us, ur)
    fourth(up_full, us, ur)

    def exchange(src, dst, k):
        mine = pl.ds(pl.multiple_of(e * SLOT, SLOT), SLOT)
        dst[mine] = src[mine]

        def go(i, carry):
            p = (e + i) % experts
            theirs = pl.ds(pl.multiple_of(p * SLOT, SLOT), SLOT)
            send(src.at[theirs], dst.at[mine], as_.at[k], ar.at[k], (t, p))
            return carry

        lax.fori_loop(1, experts, go, 0)

    def arrived(buf, k):
        wait(buf.at[pl.ds(0, (experts - 1) * SLOT)], ar.at[k])

    def route_grads(mix_grad):
        mg = mix_grad.astype(BF).astype(F32)
        both = jnp.concatenate([(gate0 * mg).astype(BF), (gate1 * mg).astype(BF)], axis=0)
        send_c[...] = dot(put[...], both).astype(BF)
        exchange(send_c, recv_c, 2)

    @pl.when(t == last)
    def _():
        mix_grad = jnp.zeros((toks, lat_w), F32)
        for j in range(n_chunks):
            mix_grad += dot_t(cot[:, j * chunk : (j + 1) * chunk], up_chunk(j))
        route_grads(mix_grad)

    wait(lat_in, hr.at[0])
    lat = lat_in[...]
    send_a[...] = dot(put[...], jnp.concatenate([lat, lat], axis=0)).astype(BF)
    exchange(send_a, recv_a, 0)
    arrived(recv_a, 0)
    rows = recv_a[...]
    part = 256
    for j in range(ffh // part):
        lo = j * part
        a = dot(rows, w_gu[0, 0, :, lo : lo + part])
        u = dot(rows, w_gu[0, 0, :, ffh + lo : ffh + lo + part])
        sig = 1.0 / (1.0 + jnp.exp(-a))
        silu = a * sig
        hidden[:, lo : lo + part] = (silu * u).astype(BF)
        up_f[:, lo : lo + part] = silu
        gate_f[:, lo : lo + part] = u * sig * (1.0 + a * (1.0 - sig))
    send_b[...] = dot(hidden[...], w_o[0, 0]).astype(BF)
    exchange(send_b, recv_b, 1)

    def boundary_grad(lg, dn, x_ref, inv, lat_prod, g_ref, out_ref, mix):
        dotted = jnp.sum(lg.astype(F32) * lat_prod, axis=1, keepdims=True) / width
        scale = inv * inv * dotted
        mix_grad = jnp.zeros((toks, lat_w), F32)
        for j in range(n_chunks):
            cols = slice(j * chunk, (j + 1) * chunk)
            ng = dot_t(lg, down_chunk(dn, j))
            new = (g_ref[:, cols].astype(F32) + inv * ng - scale * x_ref[:, cols].astype(F32)).astype(BF)
            out_ref[:, cols] = new
            if mix:
                mix_grad += dot_t(new, up_chunk(j))
        return mix_grad

    def forward_finish():
        arrived(recv_b, 1)
        back = recv_b[...]
        mixed = (gate0 * dot(take0[...], back) + gate1 * dot(take1[...], back)).astype(BF)

        @pl.when(t > 0)
        def _():
            wait(x_in, hr.at[1])

        total = jnp.zeros((toks, lat_w), F32)
        square = jnp.zeros((toks, 1), F32)
        for j in range(n_chunks):
            cols = slice(j * chunk, (j + 1) * chunk)
            new = (x_in[:, cols].astype(F32) + dot(mixed, up_chunk(j))).astype(BF)
            out[0, :, cols] = new
            wide = new.astype(F32)
            square += jnp.sum(wide * wide, axis=1, keepdims=True)
            total += dot(new, down_chunk(down_full, j))
        inv = lax.rsqrt(square / width + EPS)
        lat_next = total * inv
        lat_f[...] = lat_next
        inv_f[...] = jnp.broadcast_to(inv, inv_f.shape)

        @pl.when(t < last)
        def _():
            lat_out[...] = lat_next.astype(BF)
            send(lat_out, lat_in, hs.at[0], hr.at[0], (above, e))
            send(out.at[0], x_in, hs.at[1], hr.at[1], (above, e))

        @pl.when(t == 0)
        def _():
            down_first[x, y, c] = w_down[0]
            first(down_first, d_a, d_b, fs, fr)
            second(down_first, d_a, d_b, fs, fr)
            third(down_first, d_a, d_b, fs, fr)
            fourth(down_first, fs, fr)
            gather_done(down_first, d_a, d_b, fs)

    def backward():
        @pl.when(t < last)
        def _():
            wait(lg_in, hr.at[2])

            @pl.when(t < last - 1)
            def _():
                wait(g_in, hr.at[3])

            mix_grad = boundary_grad(
                lg_in[...], down_full, out.at[0], inv_f[:, 0:1], lat_f[...], g_in, g_new, True
            )
            route_grads(mix_grad)
            send(g_new, g_fin, hs.at[4], hr.at[4], (above, e))

            @pl.when(t > 0)
            def _():
                send(g_new, g_in, hs.at[3], hr.at[3], (below, e))

        arrived(recv_c, 2)
        grads = recv_c[...]
        for j in range(ffh // part):
            lo = j * part
            hg = dot_t(grads, w_o[0, 0, lo : lo + part, :])
            joined[:, lo : lo + part] = (hg * gate_f[:, lo : lo + part]).astype(BF)
            joined[:, ffh + lo : ffh + lo + part] = (hg * up_f[:, lo : lo + part]).astype(BF)
        send_d[...] = dot_t(joined[...], w_gu[0, 0]).astype(BF)
        exchange(send_d, recv_d, 3)
        arrived(recv_d, 3)
        back = recv_d[...]
        lg_out[...] = (dot(take0[...], back) + dot(take1[...], back)).astype(BF)

        @pl.when(t > 0)
        def _():
            send(lg_out, lg_in, hs.at[2], hr.at[2], (below, e))

    def stage(i, carry):
        @pl.when((i == 0) == (t == last))
        def _():
            backward()

        @pl.when(i == 0)
        def _():
            forward_finish()

        return carry

    lax.fori_loop(0, 2, stage, 0)

    @pl.when(t == 0)
    def _():
        square = jnp.zeros((toks, 1), F32)
        for j in range(n_chunks):
            wide = tokens[:, j * chunk : (j + 1) * chunk].astype(F32)
            square += jnp.sum(wide * wide, axis=1, keepdims=True)
        inv = lax.rsqrt(square / width + EPS)
        boundary_grad(
            lg_out[...], down_first, tokens, inv, lat_in[...].astype(F32), g_new, gin.at[0], False
        )

    @pl.when(t > 0)
    def _():
        wait(g_fin, hr.at[4])
        gin[0] = g_fin[...]

    wait(w_down.at[0], zs.at[0])
    gather_done(up_full, u_a, u_b, us)
    gather_done(down_full, d_a, d_b, ds)
    for k in range(4):
        wait(recv_a.at[pl.ds(0, (experts - 1) * SLOT)], as_.at[k])
    wait(lat_out, hs.at[0])

    @pl.when(t < last)
    def _():
        wait(x_in, hs.at[1])
        wait(g_new, hs.at[4])

    @pl.when(t > 0)
    def _():
        wait(lg_out, hs.at[2])

        @pl.when(t < last)
        def _():
            wait(g_new, hs.at[3])


def body(sections, experts, tokens, cot, w_down, w_up, w_gu, w_o, routes, gates, counts):
    toks, width = tokens.shape
    lat_w = w_down.shape[2]
    ffh = w_o.shape[2]
    slots = experts * SLOT
    vm = pltpu.VMEM
    dma = pltpu.SemaphoreType.DMA
    rows = [vm((slots, lat_w), BF) for _ in range(8)]
    spec = pl.BlockSpec(memory_space=pltpu.VMEM)
    shape = jax.ShapeDtypeStruct((1, toks, width), BF)
    return pl.pallas_call(
        functools.partial(kernel, sections, experts),
        out_shape=(shape, shape),
        in_specs=[spec] * 9,
        out_specs=(spec, spec),
        scratch_shapes=[
            vm((4, 4, 2, lat_w // experts, width), BF),
            vm((4, 4, 2, width // experts, lat_w), BF),
            vm((4, 4, 2, width // experts, lat_w), BF),
            vm((toks, width), BF),
            vm((toks, width), BF),
            vm((toks, width), BF),
            vm((toks, width), BF),
            vm((slots, ffh), F32),
            vm((slots, ffh), F32),
            vm((slots, ffh), BF),
            vm((slots, 2 * ffh), BF),
            *rows,
            vm((slots, 2 * toks), BF),
            vm((toks, slots), BF),
            vm((toks, slots), BF),
            vm((toks, lat_w), BF),
            vm((toks, lat_w), BF),
            vm((toks, lat_w), BF),
            vm((toks, lat_w), BF),
            vm((toks, lat_w), F32),
            vm((toks, 128), F32),
            dma((1,)), dma((1,)),
            dma((5,)), dma((5,)),
            dma((5,)), dma((5,)),
            dma((5,)), dma((5,)),
            dma((4,)), dma((4,)),
            dma((5,)), dma((5,)),
            dma((1,)),
        ],
        compiler_params=pltpu.CompilerParams(
            collective_id=0, has_side_effects=True, vmem_limit_bytes=56 * 1024 * 1024
        ),
    )(tokens, cot, w_down, w_up, w_gu, w_o, routes, gates, counts)


def solution(mesh):
    in_specs = (
        P("expert", None),
        P("expert", None),
        P("section", "expert", None),
        P("section", "expert", None),
        P("section", "expert", None, None),
        P("section", "expert", None, None),
        P("section", "expert", None),
        P("section", "expert", None),
        P("section", "expert"),
    )
    out_specs = (P("section", "expert", None), P("section", "expert", None))
    step = functools.partial(body, mesh.shape["section"], mesh.shape["expert"])
    return jax.shard_map(step, mesh=mesh, in_specs=in_specs, out_specs=out_specs, check_vma=False)
```

```python
import functools

import jax
import jax.numpy as jnp
from jax import lax
from jax.experimental import pallas as pl
from jax.experimental.pallas import tpu as pltpu
from jax.sharding import PartitionSpec as P

EPS = 1e-05
MESH = pl.DeviceIdType.MESH
BF = jnp.bfloat16
F32 = jnp.float32
SLOT = 16
GROUPS = 2
PER = 32 // GROUPS
ORDER = sorted(
    [(dx, dy, dc) for dx in range(4) for dy in range(4) for dc in range(2) if (dx, dy, dc) != (0, 0, 0)],
    key=lambda k: -(min(k[0], 4 - k[0]) + min(k[1], 4 - k[1])),
)


def dot(a, b):
    return jnp.dot(a, b, preferred_element_type=F32)


def dot_t(a, b):
    return lax.dot_general(a, b, (((1,), (1,)), ((), ())), preferred_element_type=F32)


def kernel(
    sections, experts,
    tokens, cot, w_down, w_up, w_gu, w_o, routes, gates, counts,
    out, gin,
    up_full, down_full, down_first,
    x_in, g_in, g_new, g_fin,
    gate_f, up_f, hidden, joined,
    send_a, recv_a, send_b, recv_b, send_c, recv_c, send_d, recv_d,
    put, take0, take1,
    lat_in, lat_out, lg_in, lg_out, lat_f, inv_f,
    zs, zr, us, ur, ds, dr, fs, fr, as_, ar, hs, hr, loc,
):
    t = lax.axis_index("section")
    e = lax.axis_index("expert")
    x = e // 8
    y = (e // 2) % 4
    c = e % 2
    above = (t + 1) % sections
    below = (t + sections - 1) % sections
    toks, width = tokens.shape
    lat_w = lat_in.shape[1]
    ffh = w_o.shape[2]
    last = sections - 1

    def at(xx, yy, cc):
        return (t, (xx * 4 + yy) * 2 + cc)

    def send(src, dst, ssem, rsem, dev):
        pltpu.make_async_remote_copy(
            src_ref=src, dst_ref=dst, send_sem=ssem, recv_sem=rsem, device_id=dev, device_id_type=MESH
        ).start()

    def wait(ref, sem):
        pltpu.make_async_copy(ref, ref, sem).wait()

    barrier = pltpu.get_barrier_semaphore()

    def greet(k, carry):
        pl.semaphore_signal(barrier, inc=1, device_id=(t, (e + k) % experts), device_id_type=MESH)
        return carry

    lax.fori_loop(1, experts, greet, 0)
    pl.semaphore_signal(barrier, inc=1, device_id=(above, e), device_id_type=MESH)
    pl.semaphore_signal(barrier, inc=1, device_id=(below, e), device_id_type=MESH)
    pl.semaphore_wait(barrier, experts + 1)

    def first(buf, ha, hb, ss, rs):
        for d in range(1, 4):
            blk = buf.at[(x, y, c) + ha]
            send(blk, blk, ss.at[0], rs.at[0], at((x + d) % 4, y, c))
            blk = buf.at[(x, y, c) + hb]
            send(blk, blk, ss.at[1], rs.at[1], at(x, (y + d) % 4, c))

    def second(buf, ha, hb, ss, rs):
        wait(buf.at[(pl.ds(0, 3), 0, 0) + ha], rs.at[0])
        wait(buf.at[(pl.ds(0, 3), 0, 0) + hb], rs.at[1])
        for d in range(1, 4):
            blk = buf.at[(slice(None), y, c) + ha]
            send(blk, blk, ss.at[2], rs.at[2], at(x, (y + d) % 4, c))
            blk = buf.at[(x, slice(None), c) + hb]
            send(blk, blk, ss.at[3], rs.at[3], at((x + d) % 4, y, c))

    def third(buf, ha, hb, ss, rs):
        wait(buf.at[(pl.ds(0, 3), slice(None), 0) + ha], rs.at[2])
        wait(buf.at[(pl.ds(0, 3), slice(None), 0) + hb], rs.at[3])
        blk = buf.at[:, :, c]
        send(blk, blk, ss.at[4], rs.at[4], at(x, y, 1 - c))

    def fourth(buf, ss, rs):
        wait(buf.at[:, :, 0], rs.at[4])

    def gather_done(buf, ha, hb, ss):
        wait(buf.at[(pl.ds(0, 3), 0, 0) + ha], ss.at[0])
        wait(buf.at[(pl.ds(0, 3), 0, 0) + hb], ss.at[1])
        wait(buf.at[(pl.ds(0, 3), slice(None), 0) + ha], ss.at[2])
        wait(buf.at[(pl.ds(0, 3), slice(None), 0) + hb], ss.at[3])
        wait(buf.at[:, :, 0], ss.at[4])

    half_cols = width // 2
    u_a = (slice(None), pl.ds(0, half_cols))
    u_b = (slice(None), pl.ds(half_cols, half_cols))
    half_rows = w_down.shape[1] // 2
    d_a = (pl.ds(0, half_rows), slice(None))
    d_b = (pl.ds(half_rows, half_rows), slice(None))

    send(w_down.at[0], down_full.at[x, y, c], zs.at[0], zr.at[0], (below, e))
    up_full[x, y, c] = w_up[0]
    first(up_full, u_a, u_b, us, ur)
    wait(w_down.at[0], zr.at[0])
    first(down_full, d_a, d_b, ds, dr)

    @pl.when(t == 0)
    def _():
        x_in[...] = tokens[...]

    @pl.when(t == last - 1)
    def _():
        g_in[...] = cot[...]

    count = counts[...]
    expert_lane = lax.broadcasted_iota(jnp.int32, (toks, experts), 1)
    live = lax.broadcasted_iota(jnp.int32, (toks, experts), 0) < count
    def column(row):
        return jnp.broadcast_to(row, (toks, toks)).T

    one0 = jnp.where((column(routes[0, 0:1])[:, 0:experts] == expert_lane) & live, 1.0, 0.0).astype(F32)
    one1 = jnp.where((column(routes[0, 1:2])[:, 0:experts] == expert_lane) & live, 1.0, 0.0).astype(F32)
    below_diag = jnp.where(
        lax.broadcasted_iota(jnp.int32, (toks, toks), 0) > lax.broadcasted_iota(jnp.int32, (toks, toks), 1), 1.0, 0.0
    ).astype(BF)
    before = dot(below_diag, (one0 + one1).astype(BF))
    slots = experts * SLOT
    spread = jnp.where(
        lax.broadcasted_iota(jnp.int32, (experts, slots), 1) // SLOT
        == lax.broadcasted_iota(jnp.int32, (experts, slots), 0),
        1.0,
        0.0,
    ).astype(BF)
    slot_no = (lax.broadcasted_iota(jnp.int32, (toks, slots), 1) % SLOT).astype(F32)
    here = dot(before.astype(BF), spread) == slot_no
    pick0 = jnp.where(here, dot(one0.astype(BF), spread), 0.0)
    pick1 = jnp.where(here, dot(one1.astype(BF), spread), 0.0)
    take0[...] = pick0.astype(BF)
    take1[...] = pick1.astype(BF)
    put[:, 0:toks] = pick0.T.astype(BF)
    put[:, toks : 2 * toks] = pick1.T.astype(BF)
    gate0 = column(gates[0, 0:1])[:, 0:1]
    gate1 = column(gates[0, 1:2])[:, 0:1]

    second(down_full, d_a, d_b, ds, dr)
    second(up_full, u_a, u_b, us, ur)
    third(down_full, d_a, d_b, ds, dr)
    fourth(down_full, ds, dr)

    chunk = 512
    n_chunks = width // chunk

    def up_chunk(j):
        return up_full[:, :, :, :, j * chunk : (j + 1) * chunk].reshape(lat_w, chunk)

    def down_chunk(buf, j):
        return buf[j // 2, 2 * (j % 2) : 2 * (j % 2) + 2].reshape(chunk, lat_w)

    @pl.when(t == last)
    def _():
        total = jnp.zeros((toks, lat_w), F32)
        square = jnp.zeros((toks, 1), F32)
        for j in range(n_chunks):
            part = tokens[:, j * chunk : (j + 1) * chunk]
            total += dot(part, down_chunk(down_full, j))
            wide = part.astype(F32)
            square += jnp.sum(wide * wide, axis=1, keepdims=True)
        inv = lax.rsqrt(square / width + EPS)
        lat_out[...] = (total * inv).astype(BF)
        send(lat_out, lat_in, hs.at[0], hr.at[0], (above, e))

    third(up_full, u_a, u_b, us, ur)
    fourth(up_full, us, ur)

    def block(i):
        return pl.ds(pl.multiple_of(i * SLOT, SLOT), SLOT)

    def dispatch(src, dst, k):
        for pos, (dx, dy, dc) in enumerate(ORDER):
            p = (((x + dx) % 4) * 4 + (y + dy) % 4) * 2 + (c + dc) % 2
            send(src.at[block(p)], dst.at[block(pos)], as_.at[k], ar.at[k, pos // PER], (t, p))
        dst[block(experts - 1)] = src[block(e)]

    def give_back(src, dst, k, g):
        for pos, (dx, dy, dc) in enumerate(ORDER):
            if pos // PER == g:
                p = (((x + 4 - dx) % 4) * 4 + (y + 4 - dy) % 4) * 2 + (c + dc) % 2
                send(src.at[block(pos)], dst.at[block(e)], as_.at[k], ar.at[k, 0], (t, p))
        if g == GROUPS - 1:
            dst[block(e)] = src[block(experts - 1)]

    def group_arrived(buf, k, g):
        size = PER if g < GROUPS - 1 else PER - 1
        wait(buf.at[pl.ds(0, size * SLOT)], ar.at[k, g])

    def arrived(buf, k):
        wait(buf.at[pl.ds(0, (experts - 1) * SLOT)], ar.at[k, 0])

    def route_grads(mix_grad):
        mg = mix_grad.astype(BF).astype(F32)
        both = jnp.concatenate([(gate0 * mg).astype(BF), (gate1 * mg).astype(BF)], axis=0)
        send_c[...] = dot(put[...], both).astype(BF)
        dispatch(send_c, recv_c, 2)

    @pl.when(t == last)
    def _():
        mix_grad = jnp.zeros((toks, lat_w), F32)
        for j in range(n_chunks):
            mix_grad += dot_t(cot[:, j * chunk : (j + 1) * chunk], up_chunk(j))
        route_grads(mix_grad)

    wait(lat_in, hr.at[0])
    lat = lat_in[...]
    send_a[...] = dot(put[...], jnp.concatenate([lat, lat], axis=0)).astype(BF)
    dispatch(send_a, recv_a, 0)
    part = 256
    height = PER * SLOT
    for g in range(GROUPS):
        group_arrived(recv_a, 0, g)
        span = slice(g * height, (g + 1) * height)
        rows = recv_a[span]
        for j in range(ffh // part):
            lo = j * part
            a = dot(rows, w_gu[0, 0, :, lo : lo + part])
            u = dot(rows, w_gu[0, 0, :, ffh + lo : ffh + lo + part])
            sig = 1.0 / (1.0 + jnp.exp(-a))
            silu = a * sig
            hidden[span, lo : lo + part] = (silu * u).astype(BF)
            up_f[span, lo : lo + part] = silu
            gate_f[span, lo : lo + part] = u * sig * (1.0 + a * (1.0 - sig))
        send_b[span] = dot(hidden[span], w_o[0, 0]).astype(BF)

        @pl.when(t < last)
        def _():
            give_back(send_b, recv_b, 1, g)

    def boundary_grad(lg, dn, x_ref, inv, lat_prod, g_ref, out_ref, mix):
        dotted = jnp.sum(lg.astype(F32) * lat_prod, axis=1, keepdims=True) / width
        scale = inv * inv * dotted
        mix_grad = jnp.zeros((toks, lat_w), F32)
        for j in range(n_chunks):
            cols = slice(j * chunk, (j + 1) * chunk)
            ng = dot_t(lg, down_chunk(dn, j))
            new = (g_ref[:, cols].astype(F32) + inv * ng - scale * x_ref[:, cols].astype(F32)).astype(BF)
            out_ref[:, cols] = new
            if mix:
                mix_grad += dot_t(new, up_chunk(j))
        return mix_grad

    def forward_finish():
        @pl.when(t == last)
        def _():
            for g in range(GROUPS):
                give_back(send_b, recv_b, 1, g)

        arrived(recv_b, 1)
        back = recv_b[...]
        mixed = (gate0 * dot(take0[...], back) + gate1 * dot(take1[...], back)).astype(BF)

        @pl.when(t > 0)
        def _():
            wait(x_in, hr.at[1])

        total = jnp.zeros((toks, lat_w), F32)
        square = jnp.zeros((toks, 1), F32)
        for j in range(n_chunks):
            cols = slice(j * chunk, (j + 1) * chunk)
            new = (x_in[:, cols].astype(F32) + dot(mixed, up_chunk(j))).astype(BF)
            out[0, :, cols] = new
            wide = new.astype(F32)
            square += jnp.sum(wide * wide, axis=1, keepdims=True)
            total += dot(new, down_chunk(down_full, j))
        inv = lax.rsqrt(square / width + EPS)
        lat_next = total * inv
        lat_f[...] = lat_next
        inv_f[...] = jnp.broadcast_to(inv, inv_f.shape)

        @pl.when(t < last)
        def _():
            lat_out[...] = lat_next.astype(BF)
            send(lat_out, lat_in, hs.at[0], hr.at[0], (above, e))
            send(out.at[0], x_in, hs.at[1], hr.at[1], (above, e))

        @pl.when(t == 0)
        def _():
            down_first[x, y, c] = w_down[0]
            first(down_first, d_a, d_b, fs, fr)
            second(down_first, d_a, d_b, fs, fr)
            third(down_first, d_a, d_b, fs, fr)
            fourth(down_first, fs, fr)
            gather_done(down_first, d_a, d_b, fs)

    def backward():
        @pl.when(t < last)
        def _():
            wait(lg_in, hr.at[2])

            @pl.when(t < last - 1)
            def _():
                wait(g_in, hr.at[3])

            mix_grad = boundary_grad(
                lg_in[...], down_full, out.at[0], inv_f[:, 0:1], lat_f[...], g_in, g_new, True
            )
            route_grads(mix_grad)
            send(g_new, g_fin, hs.at[4], hr.at[4], (above, e))

            @pl.when(t > 0)
            def _():
                send(g_new, g_in, hs.at[3], hr.at[3], (below, e))

        for g in range(GROUPS):
            group_arrived(recv_c, 2, g)
            span = slice(g * height, (g + 1) * height)
            grads = recv_c[span]
            for j in range(ffh // part):
                lo = j * part
                hg = dot_t(grads, w_o[0, 0, lo : lo + part, :])
                joined[span, lo : lo + part] = (hg * gate_f[span, lo : lo + part]).astype(BF)
                joined[span, ffh + lo : ffh + lo + part] = (hg * up_f[span, lo : lo + part]).astype(BF)
            send_d[span] = dot_t(joined[span], w_gu[0, 0]).astype(BF)
            give_back(send_d, recv_d, 3, g)
        arrived(recv_d, 3)
        back = recv_d[...]
        lg_out[...] = (dot(take0[...], back) + dot(take1[...], back)).astype(BF)

        @pl.when(t > 0)
        def _():
            send(lg_out, lg_in, hs.at[2], hr.at[2], (below, e))

    def stage(i, carry):
        @pl.when((i == 0) == (t == last))
        def _():
            backward()

        @pl.when(i == 0)
        def _():
            forward_finish()

        return carry

    lax.fori_loop(0, 2, stage, 0)

    @pl.when(t == 0)
    def _():
        square = jnp.zeros((toks, 1), F32)
        for j in range(n_chunks):
            wide = tokens[:, j * chunk : (j + 1) * chunk].astype(F32)
            square += jnp.sum(wide * wide, axis=1, keepdims=True)
        inv = lax.rsqrt(square / width + EPS)
        boundary_grad(
            lg_out[...], down_first, tokens, inv, lat_in[...].astype(F32), g_new, gin.at[0], False
        )

    @pl.when(t > 0)
    def _():
        wait(g_fin, hr.at[4])
        gin[0] = g_fin[...]

    wait(w_down.at[0], zs.at[0])
    gather_done(up_full, u_a, u_b, us)
    gather_done(down_full, d_a, d_b, ds)
    for k in range(4):
        wait(recv_a.at[pl.ds(0, (experts - 1) * SLOT)], as_.at[k])
    wait(lat_out, hs.at[0])

    @pl.when(t < last)
    def _():
        wait(x_in, hs.at[1])
        wait(g_new, hs.at[4])

    @pl.when(t > 0)
    def _():
        wait(lg_out, hs.at[2])

        @pl.when(t < last)
        def _():
            wait(g_new, hs.at[3])


def body(sections, experts, tokens, cot, w_down, w_up, w_gu, w_o, routes, gates, counts):
    toks, width = tokens.shape
    lat_w = w_down.shape[2]
    ffh = w_o.shape[2]
    slots = experts * SLOT
    vm = pltpu.VMEM
    dma = pltpu.SemaphoreType.DMA
    rows = [vm((slots, lat_w), BF) for _ in range(8)]
    spec = pl.BlockSpec(memory_space=pltpu.VMEM)
    shape = jax.ShapeDtypeStruct((1, toks, width), BF)
    return pl.pallas_call(
        functools.partial(kernel, sections, experts),
        out_shape=(shape, shape),
        in_specs=[spec] * 9,
        out_specs=(spec, spec),
        scratch_shapes=[
            vm((4, 4, 2, lat_w // experts, width), BF),
            vm((4, 4, 2, width // experts, lat_w), BF),
            vm((4, 4, 2, width // experts, lat_w), BF),
            vm((toks, width), BF),
            vm((toks, width), BF),
            vm((toks, width), BF),
            vm((toks, width), BF),
            vm((slots, ffh), F32),
            vm((slots, ffh), F32),
            vm((slots, ffh), BF),
            vm((slots, 2 * ffh), BF),
            *rows,
            vm((slots, 2 * toks), BF),
            vm((toks, slots), BF),
            vm((toks, slots), BF),
            vm((toks, lat_w), BF),
            vm((toks, lat_w), BF),
            vm((toks, lat_w), BF),
            vm((toks, lat_w), BF),
            vm((toks, lat_w), F32),
            vm((toks, 128), F32),
            dma((1,)), dma((1,)),
            dma((5,)), dma((5,)),
            dma((5,)), dma((5,)),
            dma((5,)), dma((5,)),
            dma((4,)), dma((4, GROUPS)),
            dma((5,)), dma((5,)),
            dma((1,)),
        ],
        compiler_params=pltpu.CompilerParams(
            collective_id=0, has_side_effects=True, vmem_limit_bytes=56 * 1024 * 1024
        ),
    )(tokens, cot, w_down, w_up, w_gu, w_o, jnp.swapaxes(routes, 1, 2), jnp.swapaxes(gates, 1, 2), counts)


def solution(mesh):
    in_specs = (
        P("expert", None),
        P("expert", None),
        P("section", "expert", None),
        P("section", "expert", None),
        P("section", "expert", None, None),
        P("section", "expert", None, None),
        P("section", "expert", None),
        P("section", "expert", None),
        P("section", "expert"),
    )
    out_specs = (P("section", "expert", None), P("section", "expert", None))
    step = functools.partial(body, mesh.shape["section"], mesh.shape["expert"])
    return jax.shard_map(step, mesh=mesh, in_specs=in_specs, out_specs=out_specs, check_vma=False)
```

```python
import functools

import jax
import jax.numpy as jnp
from jax import lax
from jax.experimental import pallas as pl
from jax.experimental.pallas import tpu as pltpu
from jax.sharding import PartitionSpec as P

EPS = 1e-05
MESH = pl.DeviceIdType.MESH
BF = jnp.bfloat16
F32 = jnp.float32
SLOT = 16
GROUPS = 2
PER = 32 // GROUPS
ORDER = sorted(
    [(dx, dy, dc) for dx in range(4) for dy in range(4) for dc in range(2) if (dx, dy, dc) != (0, 0, 0)],
    key=lambda k: -(min(k[0], 4 - k[0]) + min(k[1], 4 - k[1])),
)


def dot(a, b):
    return jnp.dot(a, b, preferred_element_type=F32)


def dot_t(a, b):
    return lax.dot_general(a, b, (((1,), (1,)), ((), ())), preferred_element_type=F32)


def kernel(
    sections, experts,
    tokens, cot, w_down, w_up, w_gu, w_o, routes, gates, counts,
    out, gin,
    up_all, down_full, quarter, lat_q,
    x_in, g_in,
    gate_f, up_f, hidden, joined,
    send_a, recv_a, send_b, recv_b, send_c, recv_c, send_d, recv_d,
    put, take0, take1,
    m_all, mixed_in, mixed_out, q_in, q_out, inv_in, inv_out,
    y_f, lat_f, xw_f, inv_f,
    zs, zr, us, ur, ds, dr, fs, fr, as_, ar, ms, mr, qs, qr, gs, gr,
):
    t = lax.axis_index("section")
    e = lax.axis_index("expert")
    x = e // 8
    y = (e // 2) % 4
    c = e % 2
    above = (t + 1) % sections
    below = (t + sections - 1) % sections
    toks, width = tokens.shape
    lat_w = w_down.shape[2]
    ffh = w_o.shape[2]
    last = sections - 1

    def at(xx, yy, cc):
        return (t, (xx * 4 + yy) * 2 + cc)

    def send(src, dst, ssem, rsem, dev):
        pltpu.make_async_remote_copy(
            src_ref=src, dst_ref=dst, send_sem=ssem, recv_sem=rsem, device_id=dev, device_id_type=MESH
        ).start()

    def wait(ref, sem):
        pltpu.make_async_copy(ref, ref, sem).wait()

    def loop(n, fn):
        def step(i, carry):
            fn(i)
            return carry

        lax.fori_loop(0, n, step, 0)

    barrier = pltpu.get_barrier_semaphore()

    @functools.partial(loop, experts - 1)
    def _(k):
        pl.semaphore_signal(barrier, inc=1, device_id=(t, (e + k + 1) % experts), device_id_type=MESH)

    for k in range(1, sections):
        pl.semaphore_signal(barrier, inc=1, device_id=((t + k) % sections, e), device_id_type=MESH)
    pl.semaphore_wait(barrier, experts - 1 + sections - 1)

    def first(buf, ha, hb, ss, rs):
        for d in range(1, 4):
            blk = buf.at[(x, y, c) + ha]
            send(blk, blk, ss.at[0], rs.at[0], at((x + d) % 4, y, c))
            blk = buf.at[(x, y, c) + hb]
            send(blk, blk, ss.at[1], rs.at[1], at(x, (y + d) % 4, c))

    def second(buf, ha, hb, ss, rs):
        wait(buf.at[(pl.ds(0, 3), 0, 0) + ha], rs.at[0])
        wait(buf.at[(pl.ds(0, 3), 0, 0) + hb], rs.at[1])
        for d in range(1, 4):
            blk = buf.at[(slice(None), y, c) + ha]
            send(blk, blk, ss.at[2], rs.at[2], at(x, (y + d) % 4, c))
            blk = buf.at[(x, slice(None), c) + hb]
            send(blk, blk, ss.at[3], rs.at[3], at((x + d) % 4, y, c))

    def third(buf, ha, hb, ss, rs):
        wait(buf.at[(pl.ds(0, 3), slice(None), 0) + ha], rs.at[2])
        wait(buf.at[(pl.ds(0, 3), slice(None), 0) + hb], rs.at[3])
        blk = buf.at[:, :, c]
        send(blk, blk, ss.at[4], rs.at[4], at(x, y, 1 - c))

    def fourth(buf, ha, hb, ss, rs):
        wait(buf.at[:, :, 0], rs.at[4])

    def gather_done(buf, ha, hb, ss, rs):
        wait(buf.at[(pl.ds(0, 3), 0, 0) + ha], ss.at[0])
        wait(buf.at[(pl.ds(0, 3), 0, 0) + hb], ss.at[1])
        wait(buf.at[(pl.ds(0, 3), slice(None), 0) + ha], ss.at[2])
        wait(buf.at[(pl.ds(0, 3), slice(None), 0) + hb], ss.at[3])
        wait(buf.at[:, :, 0], ss.at[4])

    half_cols = width // 2
    half_rows = w_down.shape[1] // 2
    d_a = (pl.ds(0, half_rows), slice(None))
    d_b = (pl.ds(half_rows, half_rows), slice(None))

    def up(i):
        return (
            up_all.at[i],
            (slice(None), pl.ds(0, half_cols)),
            (slice(None), pl.ds(half_cols, half_cols)),
            us.at[i],
            ur.at[i],
        )

    down = (down_full, d_a, d_b, ds, dr)
    piece = (quarter, d_a, d_b, fs, fr)

    lanes = lat_w // sections

    @pl.when(t == 0)
    def _():
        for k in range(1, sections):
            send(w_down.at[0, :, pl.ds(k * lanes, lanes)], quarter.at[x, y, c], zs.at[0], zr.at[0], (k, e))
        quarter[x, y, c] = w_down[0, :, 0:lanes]

    up_all[t, x, y, c] = w_up[0]
    for k in range(1, sections):

        @pl.when(t < k)
        def _():
            send(w_up.at[0], up_all.at[t, x, y, c], zs.at[1], zr.at[1 + t], (k, e))

    @pl.when(t > 0)
    def _():
        wait(quarter.at[0, 0, 0], zr.at[0])

    first(*piece)
    x_in[...] = tokens[...]

    @pl.when(t == last)
    def _():
        g_in[...] = cot[...]

    count = counts[...]
    expert_lane = lax.broadcasted_iota(jnp.int32, (toks, experts), 1)
    live = lax.broadcasted_iota(jnp.int32, (toks, experts), 0) < count

    def column(row):
        return jnp.broadcast_to(row, (toks, toks)).T

    one0 = jnp.where((column(routes[0, 0:1])[:, 0:experts] == expert_lane) & live, 1.0, 0.0).astype(F32)
    one1 = jnp.where((column(routes[0, 1:2])[:, 0:experts] == expert_lane) & live, 1.0, 0.0).astype(F32)
    below_diag = jnp.where(
        lax.broadcasted_iota(jnp.int32, (toks, toks), 0) > lax.broadcasted_iota(jnp.int32, (toks, toks), 1), 1.0, 0.0
    ).astype(BF)
    before = dot(below_diag, (one0 + one1).astype(BF))
    slots = experts * SLOT
    spread = jnp.where(
        lax.broadcasted_iota(jnp.int32, (experts, slots), 1) // SLOT
        == lax.broadcasted_iota(jnp.int32, (experts, slots), 0),
        1.0,
        0.0,
    ).astype(BF)
    slot_no = (lax.broadcasted_iota(jnp.int32, (toks, slots), 1) % SLOT).astype(F32)
    here = dot(before.astype(BF), spread) == slot_no
    pick0 = jnp.where(here, dot(one0.astype(BF), spread), 0.0)
    pick1 = jnp.where(here, dot(one1.astype(BF), spread), 0.0)
    take0[...] = pick0.astype(BF)
    take1[...] = pick1.astype(BF)
    put[:, 0:toks] = pick0.T.astype(BF)
    put[:, toks : 2 * toks] = pick1.T.astype(BF)
    gate0 = column(gates[0, 0:1])[:, 0:1]
    gate1 = column(gates[0, 1:2])[:, 0:1]

    second(*piece)
    chunk = 512
    n_chunks = width // chunk

    def cols_of(j):
        return slice(j * chunk, (j + 1) * chunk)

    def up_chunk(i, j):
        return up_all[i, :, :, :, :, j * chunk : (j + 1) * chunk].reshape(lat_w, chunk)

    def down_chunk(buf, j):
        return buf[j // 2, 2 * (j % 2) : 2 * (j % 2) + 2].reshape(chunk, buf.shape[-1])

    def inv_rms(square):
        return lax.rsqrt(square / width + EPS)

    square = jnp.zeros((toks, 1), F32)
    for j in range(n_chunks):
        wide = tokens[:, cols_of(j)].astype(F32)
        square += jnp.sum(wide * wide, axis=1, keepdims=True)
    inv_f[...] = jnp.broadcast_to(inv_rms(square), inv_f.shape)
    third(*piece)
    fourth(*piece)
    total = jnp.zeros((toks, lanes), F32)
    for j in range(n_chunks):
        total += dot(tokens[:, cols_of(j)], down_chunk(quarter, j))
    lat_q[t] = (total * inv_f[...]).astype(BF)

    @pl.when(t > 0)
    def _():
        send(lat_q.at[t], lat_q.at[t], zs.at[2], zr.at[5], (0, e))

    first(*up(t))

    def product(i):
        m_all[i] = dot(up_all[i].reshape(lat_w, width), down_full[...].reshape(width, lat_w)).astype(BF)

    @pl.when(t > 0)
    def _():
        down_full[x, y, c] = w_down[0]
        first(*down)

        @functools.partial(loop, t)
        def _(i):
            wait(w_up.at[0], zr.at[1 + i])
            first(*up(i))

        second(*down)
        loop(t, lambda i: second(*up(i)))
        third(*down)
        loop(t, lambda i: third(*up(i)))
        second(*up(t))
        fourth(*down)
        loop(t, lambda i: fourth(*up(i)))
        loop(t, product)

    def block(i):
        return pl.ds(pl.multiple_of(i * SLOT, SLOT), SLOT)

    def dispatch(src, dst, k):
        for pos, (dx, dy, dc) in enumerate(ORDER):
            p = (((x + dx) % 4) * 4 + (y + dy) % 4) * 2 + (c + dc) % 2
            send(src.at[block(p)], dst.at[block(pos)], as_.at[k], ar.at[k, pos // PER], (t, p))
        dst[block(experts - 1)] = src[block(e)]

    def give_back(src, dst, k, g):
        for pos, (dx, dy, dc) in enumerate(ORDER):
            if pos // PER == g:
                p = (((x + 4 - dx) % 4) * 4 + (y + 4 - dy) % 4) * 2 + (c + dc) % 2
                send(src.at[block(pos)], dst.at[block(e)], as_.at[k], ar.at[k, 0], (t, p))
        if g == GROUPS - 1:
            dst[block(e)] = src[block(experts - 1)]

    def group_arrived(buf, k, g):
        size = PER if g < GROUPS - 1 else PER - 1
        wait(buf.at[pl.ds(0, size * SLOT)], ar.at[k, g])

    def arrived(buf, k):
        wait(buf.at[pl.ds(0, (experts - 1) * SLOT)], ar.at[k, 0])

    def route_grads():
        mg = q_in[t].astype(F32)
        both = jnp.concatenate([(gate0 * mg).astype(BF), (gate1 * mg).astype(BF)], axis=0)
        send_c[...] = dot(put[...], both).astype(BF)
        dispatch(send_c, recv_c, 2)

    def back_through(ref, i):
        total = jnp.zeros((toks, lat_w), F32)
        for j in range(n_chunks):
            total += dot_t(ref[:, cols_of(j)], up_chunk(i, j))
        return total

    @pl.when(t == last)
    def _():
        third(*up(t))
        fourth(*up(t))

        @functools.partial(loop, sections)
        def _(i):
            q_in[i] = back_through(cot, i).astype(BF)

        route_grads()

    def add_mixed(i):
        for j in range(n_chunks):
            new = x_in[:, cols_of(j)].astype(F32) + dot(mixed_in[i], up_chunk(i, j))
            x_in[:, cols_of(j)] = new.astype(BF)

    def pass_on(i):
        @pl.when(t < last)
        def _():
            send(mixed_in.at[i], mixed_in.at[i], ms.at[i], mr.at[i], (above, e))

    @functools.partial(loop, t - 1)
    def _(i):
        wait(mixed_in.at[i], mr.at[i])
        pass_on(i)
        add_mixed(i)

    @pl.when(t > 0)
    def _():
        total = jnp.zeros((toks, lat_w), F32)
        for j in range(n_chunks):
            total += dot(x_in[:, cols_of(j)], down_chunk(down_full, j))
        y_f[...] = total

    @pl.when(t == 0)
    def _():
        wait(lat_q.at[pl.ds(0, sections - 1)], zr.at[5])
        lat_f[...] = jnp.concatenate([lat_q[k] for k in range(sections)], axis=1).astype(F32)

    @pl.when(t > 0)
    def _():
        wait(mixed_in.at[t - 1], mr.at[t - 1])
        raw = y_f[...] + dot(mixed_in[t - 1], m_all[t - 1])
        wait(inv_in, zr.at[6])
        inv = column(inv_in[0:1])
        inv_f[...] = inv
        lat_f[...] = raw * inv[:, 0:1]

    lat = lat_f[...].astype(BF)
    send_a[...] = dot(put[...], jnp.concatenate([lat, lat], axis=0)).astype(BF)
    dispatch(send_a, recv_a, 0)

    @pl.when(t == 0)
    def _():
        second(*up(t))

    @pl.when(t > 0)
    def _():
        pass_on(t - 1)
        add_mixed(t - 1)
        xw_f[...] = back_through(x_in, t - 1)

    part = 256
    height = PER * SLOT
    for g in range(GROUPS):
        group_arrived(recv_a, 0, g)
        span = slice(g * height, (g + 1) * height)
        rows = recv_a[span]
        for j in range(ffh // part):
            lo = j * part
            a = dot(rows, w_gu[0, 0, :, lo : lo + part])
            u = dot(rows, w_gu[0, 0, :, ffh + lo : ffh + lo + part])
            sig = 1.0 / (1.0 + jnp.exp(-a))
            silu = a * sig
            hidden[span, lo : lo + part] = (silu * u).astype(BF)
            up_f[span, lo : lo + part] = silu
            gate_f[span, lo : lo + part] = u * sig * (1.0 + a * (1.0 - sig))
        send_b[span] = dot(hidden[span], w_o[0, 0]).astype(BF)

        @pl.when(t < last)
        def _():
            give_back(send_b, recv_b, 1, g)

    def forward_finish():
        @pl.when(t == last)
        def _():
            for g in range(GROUPS):
                give_back(send_b, recv_b, 1, g)

        @pl.when(t < last)
        def _():
            third(*up(t))
            fourth(*up(t))

        arrived(recv_b, 1)
        back = recv_b[...]
        mixed = (gate0 * dot(take0[...], back) + gate1 * dot(take1[...], back)).astype(BF)
        mixed_out[...] = mixed

        @pl.when(t < last)
        def _():
            send(mixed_out, mixed_in.at[t], ms.at[t], mr.at[t], (above, e))

        square = jnp.zeros((toks, 1), F32)
        for j in range(n_chunks):
            new = (x_in[:, cols_of(j)].astype(F32) + dot(mixed, up_chunk(t, j))).astype(BF)
            out[0, :, cols_of(j)] = new
            wide = new.astype(F32)
            square += jnp.sum(wide * wide, axis=1, keepdims=True)

        @pl.when(t < last)
        def _():
            inv_out[...] = jnp.broadcast_to(inv_rms(square), (toks, toks)).T[0 : inv_out.shape[0]]
            send(inv_out, inv_in, zs.at[3], zr.at[6], (above, e))

        @pl.when(t == 0)
        def _():
            down_full[x, y, c] = w_down[0]
            for phase in (first, second, third, fourth):
                phase(*down)

    wide_chunk = width // 4

    def backward():
        @pl.when(t < last)
        def _():
            wait(q_in.at[t], qr.at[t])
            route_grads()

        for g in range(GROUPS):
            group_arrived(recv_c, 2, g)
            span = slice(g * height, (g + 1) * height)
            grads = recv_c[span]
            for j in range(ffh // part):
                lo = j * part
                hg = dot_t(grads, w_o[0, 0, lo : lo + part, :])
                joined[span, lo : lo + part] = (hg * gate_f[span, lo : lo + part]).astype(BF)
                joined[span, ffh + lo : ffh + lo + part] = (hg * up_f[span, lo : lo + part]).astype(BF)
            send_d[span] = dot_t(joined[span], w_gu[0, 0]).astype(BF)
            give_back(send_d, recv_d, 3, g)

        arrived(recv_d, 3)
        back = recv_d[...]
        lg = (dot(take0[...], back) + dot(take1[...], back)).astype(BF)
        inv = inv_f[:, 0:1]
        dotted = jnp.sum(lg.astype(F32) * lat_f[...], axis=1, keepdims=True) / width
        scale = inv * inv * dotted

        def mix_grad(i, xw):
            q_out[i] = (q_in[i].astype(F32) + inv * dot_t(lg, m_all[i]) - scale * xw).astype(BF)
            send(q_out.at[i], q_in.at[i], qs.at[i], qr.at[i], (below, e))

        @pl.when(t > 0)
        def _():
            @pl.when(t < last)
            def _():
                loop(t, lambda i: wait(q_in.at[i], qr.at[i]))

            mix_grad(t - 1, xw_f[...])

        for j in range(4):
            here = pl.ds(j * wide_chunk, wide_chunk)

            @pl.when(t < last)
            def _():
                wait(g_in.at[:, here], gr.at[j])

            for h in range(2 * j, 2 * j + 2):
                ng = dot_t(lg, down_chunk(down_full, h))
                new = g_in[:, cols_of(h)].astype(F32) + inv * ng - scale * x_in[:, cols_of(h)].astype(F32)
                gin[0, :, cols_of(h)] = new.astype(BF)

            @pl.when(t > 0)
            def _():
                send(gin.at[0, :, here], g_in.at[:, here], gs.at[j], gr.at[j], (below, e))

        loop(t - 1, lambda i: mix_grad(i, back_through(x_in, i)))

    def stage(i):
        @pl.when((i == 0) == (t == last))
        def _():
            backward()

        @pl.when(i == 0)
        def _():
            forward_finish()

    loop(2, stage)

    @pl.when(t == 0)
    def _():
        wait(lat_q.at[pl.ds(0, sections - 1)], zs.at[0])

    @pl.when(t > 0)
    def _():
        wait(lat_q.at[0], zs.at[2])

    loop(last - t, lambda i: wait(w_up.at[0], zs.at[1]))
    gather_done(*piece)
    gather_done(*down)
    loop(t + 1, lambda i: gather_done(*up(i)))
    for k in range(4):
        wait(recv_a.at[pl.ds(0, (experts - 1) * SLOT)], as_.at[k])

    @pl.when(t < last)
    def _():
        loop(t + 1, lambda i: wait(mixed_out, ms.at[i]))
        wait(inv_out, zs.at[3])

    @pl.when(t > 0)
    def _():
        loop(t, lambda i: wait(mixed_out, qs.at[i]))
        for j in range(4):
            wait(g_in.at[:, pl.ds(0, wide_chunk)], gs.at[j])


def body(sections, experts, tokens, cot, w_down, w_up, w_gu, w_o, routes, gates, counts):
    toks, width = tokens.shape
    lat_w = w_down.shape[2]
    ffh = w_o.shape[2]
    slots = experts * SLOT
    vm = pltpu.VMEM
    dma = pltpu.SemaphoreType.DMA
    rows = [vm((slots, lat_w), BF) for _ in range(8)]
    spec = pl.BlockSpec(memory_space=pltpu.VMEM)
    shape = jax.ShapeDtypeStruct((1, toks, width), BF)
    return pl.pallas_call(
        functools.partial(kernel, sections, experts),
        out_shape=(shape, shape),
        in_specs=[spec] * 9,
        out_specs=(spec, spec),
        scratch_shapes=[
            vm((sections, 4, 4, 2, lat_w // experts, width), BF),
            vm((4, 4, 2, width // experts, lat_w), BF),
            vm((4, 4, 2, width // experts, lat_w // sections), BF),
            vm((sections, toks, lat_w // sections), BF),
            vm((toks, width), BF),
            vm((toks, width), BF),
            vm((slots, ffh), F32),
            vm((slots, ffh), F32),
            vm((slots, ffh), BF),
            vm((slots, 2 * ffh), BF),
            *rows,
            vm((slots, 2 * toks), BF),
            vm((toks, slots), BF),
            vm((toks, slots), BF),
            vm((sections - 1, lat_w, lat_w), BF),
            vm((sections - 1, toks, lat_w), BF),
            vm((toks, lat_w), BF),
            vm((sections, toks, lat_w), BF),
            vm((sections - 1, toks, lat_w), BF),
            vm((8, toks), F32),
            vm((8, toks), F32),
            vm((toks, lat_w), F32),
            vm((toks, lat_w), F32),
            vm((toks, lat_w), F32),
            vm((toks, 128), F32),
            dma((4,)), dma((7,)),
            dma((sections, 5)), dma((sections, 5)),
            dma((5,)), dma((5,)),
            dma((5,)), dma((5,)),
            dma((4,)), dma((4, GROUPS)),
            dma((sections,)), dma((sections,)),
            dma((sections,)), dma((sections,)),
            dma((4,)), dma((4,)),
        ],
        compiler_params=pltpu.CompilerParams(
            collective_id=0, has_side_effects=True, vmem_limit_bytes=60 * 1024 * 1024
        ),
    )(
        tokens, cot, w_down, w_up, w_gu, w_o, jnp.swapaxes(routes, 1, 2), jnp.swapaxes(gates, 1, 2), counts
    )


def solution(mesh):
    in_specs = (
        P("expert", None),
        P("expert", None),
        P("section", "expert", None),
        P("section", "expert", None),
        P("section", "expert", None, None),
        P("section", "expert", None, None),
        P("section", "expert", None),
        P("section", "expert", None),
        P("section", "expert"),
    )
    out_specs = (P("section", "expert", None), P("section", "expert", None))
    step = functools.partial(body, mesh.shape["section"], mesh.shape["expert"])
    return jax.shard_map(step, mesh=mesh, in_specs=in_specs, out_specs=out_specs, check_vma=False)
```

```python
import functools

import jax
import jax.numpy as jnp
from jax import lax
from jax.experimental import pallas as pl
from jax.experimental.pallas import tpu as pltpu
from jax.sharding import PartitionSpec as P

EPS = 1e-05
MESH = pl.DeviceIdType.MESH
BF = jnp.bfloat16
F32 = jnp.float32
SLOT = 16
GROUPS = 2
PER = 32 // GROUPS
ORDER = sorted(
    [(dx, dy, dc) for dx in range(4) for dy in range(4) for dc in range(2) if (dx, dy, dc) != (0, 0, 0)],
    key=lambda k: -(min(k[0], 4 - k[0]) + min(k[1], 4 - k[1])),
)


def dot(a, b):
    return jnp.dot(a, b, preferred_element_type=F32)


def dot_t(a, b):
    return lax.dot_general(a, b, (((1,), (1,)), ((), ())), preferred_element_type=F32)


def kernel(
    sections, experts,
    tokens, cot, w_down, w_up, w_gu, w_o, routes, gates, counts,
    out, gin,
    up_all, down_full, quarter, lat_q,
    x_in, g_in,
    gate_f, up_f, hidden, joined,
    send_a, recv_a, send_b, recv_b, send_c, recv_c, send_d, recv_d,
    put, take0, take1,
    m_all, mixed_in, mixed_out, q_in, q_out,
    y_f, lat_f, xw_f, inv_f,
    zs, zr, us, ur, ds, dr, fs, fr, as_, ar, ms, mr, qs, qr, gs, gr,
):
    t = lax.axis_index("section")
    e = lax.axis_index("expert")
    x = e // 8
    y = (e // 2) % 4
    c = e % 2
    above = (t + 1) % sections
    below = (t + sections - 1) % sections
    toks, width = tokens.shape
    lat_w = w_down.shape[2]
    ffh = w_o.shape[2]
    last = sections - 1

    def at(xx, yy, cc):
        return (t, (xx * 4 + yy) * 2 + cc)

    def send(src, dst, ssem, rsem, dev):
        pltpu.make_async_remote_copy(
            src_ref=src, dst_ref=dst, send_sem=ssem, recv_sem=rsem, device_id=dev, device_id_type=MESH
        ).start()

    def wait(ref, sem):
        pltpu.make_async_copy(ref, ref, sem).wait()

    def loop(n, fn):
        def step(i, carry):
            fn(i)
            return carry

        lax.fori_loop(0, n, step, 0)

    barrier = pltpu.get_barrier_semaphore()

    @functools.partial(loop, experts - 1)
    def _(k):
        pl.semaphore_signal(barrier, inc=1, device_id=(t, (e + k + 1) % experts), device_id_type=MESH)

    for k in range(1, sections):
        pl.semaphore_signal(barrier, inc=1, device_id=((t + k) % sections, e), device_id_type=MESH)
    pl.semaphore_wait(barrier, experts - 1 + sections - 1)

    def first(buf, ha, hb, ss, rs):
        for d in range(1, 4):
            blk = buf.at[(x, y, c) + ha]
            send(blk, blk, ss.at[0], rs.at[0], at((x + d) % 4, y, c))
            blk = buf.at[(x, y, c) + hb]
            send(blk, blk, ss.at[1], rs.at[1], at(x, (y + d) % 4, c))

    def second(buf, ha, hb, ss, rs):
        wait(buf.at[(pl.ds(0, 3), 0, 0) + ha], rs.at[0])
        wait(buf.at[(pl.ds(0, 3), 0, 0) + hb], rs.at[1])
        for d in range(1, 4):
            blk = buf.at[(slice(None), y, c) + ha]
            send(blk, blk, ss.at[2], rs.at[2], at(x, (y + d) % 4, c))
            blk = buf.at[(x, slice(None), c) + hb]
            send(blk, blk, ss.at[3], rs.at[3], at((x + d) % 4, y, c))

    def third(buf, ha, hb, ss, rs):
        wait(buf.at[(pl.ds(0, 3), slice(None), 0) + ha], rs.at[2])
        wait(buf.at[(pl.ds(0, 3), slice(None), 0) + hb], rs.at[3])
        blk = buf.at[:, :, c]
        send(blk, blk, ss.at[4], rs.at[4], at(x, y, 1 - c))

    def fourth(buf, ha, hb, ss, rs):
        wait(buf.at[:, :, 0], rs.at[4])

    def gather_done(buf, ha, hb, ss, rs):
        wait(buf.at[(pl.ds(0, 3), 0, 0) + ha], ss.at[0])
        wait(buf.at[(pl.ds(0, 3), 0, 0) + hb], ss.at[1])
        wait(buf.at[(pl.ds(0, 3), slice(None), 0) + ha], ss.at[2])
        wait(buf.at[(pl.ds(0, 3), slice(None), 0) + hb], ss.at[3])
        wait(buf.at[:, :, 0], ss.at[4])

    half_cols = width // 2
    half_rows = w_down.shape[1] // 2
    d_a = (pl.ds(0, half_rows), slice(None))
    d_b = (pl.ds(half_rows, half_rows), slice(None))

    def up(i):
        return (
            up_all.at[i],
            (slice(None), pl.ds(0, half_cols)),
            (slice(None), pl.ds(half_cols, half_cols)),
            us.at[i],
            ur.at[i],
        )

    down = (down_full, d_a, d_b, ds, dr)
    piece = (quarter.at[0], d_a, d_b, fs.at[0], fr.at[0])
    piece2 = (quarter.at[1], d_a, d_b, fs.at[1], fr.at[1])

    lanes = lat_w // sections

    @pl.when(t == 0)
    def _():
        for k in range(2, sections):
            send(w_down.at[0, :, pl.ds(k * lanes, lanes)], quarter.at[0, x, y, c], zs.at[0], zr.at[0], (k, e))
        quarter[0, x, y, c] = w_down[0, :, 0:lanes]
        quarter[1, x, y, c] = w_down[0, :, lanes : 2 * lanes]
        first(*piece)
        first(*piece2)

    up_all[t, x, y, c] = w_up[0]
    for k in range(1, sections):

        @pl.when(t < k)
        def _():
            send(w_up.at[0], up_all.at[t, x, y, c], zs.at[1], zr.at[1 + t], (k, e))

    @pl.when(t == last)
    def _():
        send(w_up.at[0], up_all.at[t, x, y, c], zs.at[1], zr.at[1 + t], (0, e))

    @pl.when(t > 1)
    def _():
        wait(quarter.at[0, 0, 0, 0], zr.at[0])
        first(*piece)

    def product(i):
        m_all[i] = dot(up_all[i].reshape(lat_w, width), down_full[...].reshape(width, lat_w)).astype(BF)

    def gather_first():
        down_full[x, y, c] = w_down[0]
        first(*down)

        @functools.partial(loop, t)
        def _(i):
            wait(w_up.at[0], zr.at[1 + i])
            first(*up(i))

    @pl.when(t == 1)
    def _():
        gather_first()

    x_in[...] = tokens[...]

    @pl.when(t == last)
    def _():
        g_in[...] = cot[...]

    count = counts[...]
    expert_lane = lax.broadcasted_iota(jnp.int32, (toks, experts), 1)
    live = lax.broadcasted_iota(jnp.int32, (toks, experts), 0) < count

    def column(row):
        return jnp.broadcast_to(row, (toks, toks)).T

    one0 = jnp.where((column(routes[0, 0:1])[:, 0:experts] == expert_lane) & live, 1.0, 0.0).astype(F32)
    one1 = jnp.where((column(routes[0, 1:2])[:, 0:experts] == expert_lane) & live, 1.0, 0.0).astype(F32)
    below_diag = jnp.where(
        lax.broadcasted_iota(jnp.int32, (toks, toks), 0) > lax.broadcasted_iota(jnp.int32, (toks, toks), 1), 1.0, 0.0
    ).astype(BF)
    before = dot(below_diag, (one0 + one1).astype(BF))
    slots = experts * SLOT
    spread = jnp.where(
        lax.broadcasted_iota(jnp.int32, (experts, slots), 1) // SLOT
        == lax.broadcasted_iota(jnp.int32, (experts, slots), 0),
        1.0,
        0.0,
    ).astype(BF)
    slot_no = (lax.broadcasted_iota(jnp.int32, (toks, slots), 1) % SLOT).astype(F32)
    here = dot(before.astype(BF), spread) == slot_no
    pick0 = jnp.where(here, dot(one0.astype(BF), spread), 0.0)
    pick1 = jnp.where(here, dot(one1.astype(BF), spread), 0.0)
    take0[...] = pick0.astype(BF)
    take1[...] = pick1.astype(BF)
    put[:, 0:toks] = pick0.T.astype(BF)
    put[:, toks : 2 * toks] = pick1.T.astype(BF)
    gate0 = column(gates[0, 0:1])[:, 0:1]
    gate1 = column(gates[0, 1:2])[:, 0:1]

    @pl.when(t != 1)
    def _():
        second(*piece)

    @pl.when(t == 0)
    def _():
        second(*piece2)

    chunk = 512
    n_chunks = width // chunk

    def cols_of(j):
        return slice(j * chunk, (j + 1) * chunk)

    def up_chunk(i, j):
        return up_all[i, :, :, :, :, j * chunk : (j + 1) * chunk].reshape(lat_w, chunk)

    def down_chunk(buf, j):
        return buf[j // 2, 2 * (j % 2) : 2 * (j % 2) + 2].reshape(chunk, buf.shape[-1])

    def inv_rms(square):
        return lax.rsqrt(square / width + EPS)

    square = jnp.zeros((toks, 1), F32)
    for j in range(n_chunks):
        wide = tokens[:, cols_of(j)].astype(F32)
        square += jnp.sum(wide * wide, axis=1, keepdims=True)
    inv_f[...] = jnp.broadcast_to(inv_rms(square), inv_f.shape)
    def raw_piece(k):
        total = jnp.zeros((toks, lanes), F32)
        for j in range(n_chunks):
            total += dot(tokens[:, cols_of(j)], down_chunk(quarter.at[k], j))
        return (total * inv_f[...]).astype(BF)

    @pl.when(t != 1)
    def _():
        third(*piece)

    @pl.when(t == 0)
    def _():
        third(*piece2)
        fourth(*piece2)
        lat_q[1] = raw_piece(1)

    @pl.when(t != 1)
    def _():
        fourth(*piece)
        lat_q[t] = raw_piece(0)

    @pl.when(t > 1)
    def _():
        send(lat_q.at[t], lat_q.at[t], zs.at[2], zr.at[5], (0, e))
        gather_first()

    @pl.when(t > 0)
    def _():
        second(*down)
        loop(t, lambda i: second(*up(i)))
        third(*down)
        loop(t, lambda i: third(*up(i)))
        fourth(*down)
        loop(t, lambda i: fourth(*up(i)))
        product(t - 1)

    def block(i):
        return pl.ds(pl.multiple_of(i * SLOT, SLOT), SLOT)

    def dispatch(src, dst, k):
        for pos, (dx, dy, dc) in enumerate(ORDER):
            p = (((x + dx) % 4) * 4 + (y + dy) % 4) * 2 + (c + dc) % 2
            send(src.at[block(p)], dst.at[block(pos)], as_.at[k], ar.at[k, pos // PER], (t, p))
        dst[block(experts - 1)] = src[block(e)]

    def give_back(src, dst, k, g):
        for pos, (dx, dy, dc) in enumerate(ORDER):
            if pos // PER == g:
                p = (((x + 4 - dx) % 4) * 4 + (y + 4 - dy) % 4) * 2 + (c + dc) % 2
                send(src.at[block(pos)], dst.at[block(e)], as_.at[k], ar.at[k, 0], (t, p))
        if g == GROUPS - 1:
            dst[block(e)] = src[block(experts - 1)]

    def group_arrived(buf, k, g):
        size = PER if g < GROUPS - 1 else PER - 1
        wait(buf.at[pl.ds(0, size * SLOT)], ar.at[k, g])

    def arrived(buf, k):
        wait(buf.at[pl.ds(0, (experts - 1) * SLOT)], ar.at[k, 0])

    def route_grads():
        mg = q_in[t].astype(F32)
        both = jnp.concatenate([(gate0 * mg).astype(BF), (gate1 * mg).astype(BF)], axis=0)
        send_c[...] = dot(put[...], both).astype(BF)
        dispatch(send_c, recv_c, 2)

    def back_through(ref, i):
        total = jnp.zeros((toks, lat_w), F32)
        for j in range(n_chunks):
            total += dot_t(ref[:, cols_of(j)], up_chunk(i, j))
        return total

    @pl.when(t == last)
    def _():
        wait(q_in.at[t], qr.at[t])
        route_grads()

    def add_mixed(i):
        square = jnp.zeros((toks, 1), F32)
        for j in range(n_chunks):
            new = (x_in[:, cols_of(j)].astype(F32) + dot(mixed_in[i], up_chunk(i, j))).astype(BF)
            x_in[:, cols_of(j)] = new
            wide = new.astype(F32)
            square += jnp.sum(wide * wide, axis=1, keepdims=True)
        return square

    def pass_on(i):
        @pl.when(t < last)
        def _():
            send(mixed_in.at[i], mixed_in.at[i], ms.at[i], mr.at[i], (above, e))

    @functools.partial(loop, t - 1)
    def _(i):
        wait(mixed_in.at[i], mr.at[i])
        pass_on(i)
        add_mixed(i)

    @pl.when(t > 0)
    def _():
        total = jnp.zeros((toks, lat_w), F32)
        for j in range(n_chunks):
            total += dot(x_in[:, cols_of(j)], down_chunk(down_full, j))
        y_f[...] = total

    @pl.when(t == 0)
    def _():
        wait(lat_q.at[pl.ds(0, sections - 2)], zr.at[5])
        lat_f[...] = jnp.concatenate([lat_q[k] for k in range(sections)], axis=1).astype(F32)

    @pl.when(t > 0)
    def _():
        wait(mixed_in.at[t - 1], mr.at[t - 1])
        pass_on(t - 1)
        inv = inv_rms(add_mixed(t - 1))
        inv_f[...] = jnp.broadcast_to(inv, inv_f.shape)
        lat_f[...] = (y_f[...] + dot(mixed_in[t - 1], m_all[t - 1])) * inv

    lat = lat_f[...].astype(BF)
    send_a[...] = dot(put[...], jnp.concatenate([lat, lat], axis=0)).astype(BF)
    dispatch(send_a, recv_a, 0)

    @pl.when(t > 0)
    def _():
        xw_f[...] = back_through(x_in, t - 1)

    @pl.when(t == last)
    def _():
        q_in[t - 1] = back_through(cot, t - 1).astype(BF)

    part = 256
    height = PER * SLOT
    for g in range(GROUPS):
        group_arrived(recv_a, 0, g)
        span = slice(g * height, (g + 1) * height)
        rows = recv_a[span]
        for j in range(ffh // part):
            lo = j * part
            a = dot(rows, w_gu[0, 0, :, lo : lo + part])
            u = dot(rows, w_gu[0, 0, :, ffh + lo : ffh + lo + part])
            sig = 1.0 / (1.0 + jnp.exp(-a))
            silu = a * sig
            hidden[span, lo : lo + part] = (silu * u).astype(BF)
            up_f[span, lo : lo + part] = silu
            gate_f[span, lo : lo + part] = u * sig * (1.0 + a * (1.0 - sig))
        send_b[span] = dot(hidden[span], w_o[0, 0]).astype(BF)

        @pl.when(t < last)
        def _():
            give_back(send_b, recv_b, 1, g)

    def forward_finish():
        @pl.when(t == last)
        def _():
            for g in range(GROUPS):
                give_back(send_b, recv_b, 1, g)

        arrived(recv_b, 1)
        back = recv_b[...]
        mixed = (gate0 * dot(take0[...], back) + gate1 * dot(take1[...], back)).astype(BF)
        mixed_out[...] = mixed

        @pl.when(t < last)
        def _():
            send(mixed_out, mixed_in.at[t], ms.at[t], mr.at[t], (above, e))

        @pl.when(t == 0)
        def _():
            wait(w_up.at[0], zr.at[1 + last])
            for phase in (first, second, third, fourth):
                phase(*up(last))
            q_out[0] = back_through(cot, last).astype(BF)
            send(q_out.at[0], q_in.at[last], qs.at[0], qr.at[last], (last, e))

        for phase in (first, second, third, fourth):
            phase(*up(t))

        for j in range(n_chunks):
            new = x_in[:, cols_of(j)].astype(F32) + dot(mixed_out[...], up_chunk(t, j))
            out[0, :, cols_of(j)] = new.astype(BF)

        @pl.when(t == 0)
        def _():
            down_full[x, y, c] = w_down[0]
            for phase in (first, second, third, fourth):
                phase(*down)

    wide_chunk = width // 4

    def backward():
        @pl.when(t < last)
        def _():
            wait(q_in.at[t], qr.at[t])
            route_grads()

        for g in range(GROUPS):
            group_arrived(recv_c, 2, g)
            span = slice(g * height, (g + 1) * height)
            grads = recv_c[span]
            for j in range(ffh // part):
                lo = j * part
                hg = dot_t(grads, w_o[0, 0, lo : lo + part, :])
                joined[span, lo : lo + part] = (hg * gate_f[span, lo : lo + part]).astype(BF)
                joined[span, ffh + lo : ffh + lo + part] = (hg * up_f[span, lo : lo + part]).astype(BF)
            send_d[span] = dot_t(joined[span], w_gu[0, 0]).astype(BF)
            give_back(send_d, recv_d, 3, g)

        arrived(recv_d, 3)
        back = recv_d[...]
        lg = (dot(take0[...], back) + dot(take1[...], back)).astype(BF)
        inv = inv_f[:, 0:1]
        dotted = jnp.sum(lg.astype(F32) * lat_f[...], axis=1, keepdims=True) / width
        scale = inv * inv * dotted

        def mix_grad(i, xw):
            @pl.when(t < last)
            def _():
                wait(q_in.at[i], qr.at[i])

            q_out[i] = (q_in[i].astype(F32) + inv * dot_t(lg, m_all[i]) - scale * xw).astype(BF)
            send(q_out.at[i], q_in.at[i], qs.at[i], qr.at[i], (below, e))

        @pl.when(t > 0)
        def _():
            mix_grad(t - 1, xw_f[...])

            @functools.partial(loop, t - 1)
            def _(i):
                product(i)

                @pl.when(t == last)
                def _():
                    q_in[i] = back_through(cot, i).astype(BF)

                mix_grad(i, back_through(x_in, i))

        for j in range(4):
            here = pl.ds(j * wide_chunk, wide_chunk)

            @pl.when(t < last)
            def _():
                wait(g_in.at[:, here], gr.at[j])

            for h in range(2 * j, 2 * j + 2):
                ng = dot_t(lg, down_chunk(down_full, h))
                new = g_in[:, cols_of(h)].astype(F32) + inv * ng - scale * x_in[:, cols_of(h)].astype(F32)
                gin[0, :, cols_of(h)] = new.astype(BF)

            @pl.when(t > 0)
            def _():
                send(gin.at[0, :, here], g_in.at[:, here], gs.at[j], gr.at[j], (below, e))

    def stage(i):
        @pl.when((i == 0) == (t == last))
        def _():
            backward()

        @pl.when(i == 0)
        def _():
            forward_finish()

    loop(2, stage)

    @pl.when(t == 0)
    def _():
        wait(lat_q.at[pl.ds(0, sections - 2)], zs.at[0])
        gather_done(*piece2)
        gather_done(*up(last))
        wait(q_out.at[0], qs.at[0])

    @pl.when(t > 1)
    def _():
        wait(lat_q.at[0], zs.at[2])

    @pl.when(t != 1)
    def _():
        gather_done(*piece)

    loop(jnp.where(t == last, 1, last - t), lambda i: wait(w_up.at[0], zs.at[1]))
    gather_done(*down)
    loop(t + 1, lambda i: gather_done(*up(i)))
    for k in range(4):
        wait(recv_a.at[pl.ds(0, (experts - 1) * SLOT)], as_.at[k])

    @pl.when(t < last)
    def _():
        loop(t + 1, lambda i: wait(mixed_out, ms.at[i]))

    @pl.when(t > 0)
    def _():
        loop(t, lambda i: wait(mixed_out, qs.at[i]))
        for j in range(4):
            wait(g_in.at[:, pl.ds(0, wide_chunk)], gs.at[j])


def body(sections, experts, tokens, cot, w_down, w_up, w_gu, w_o, routes, gates, counts):
    toks, width = tokens.shape
    lat_w = w_down.shape[2]
    ffh = w_o.shape[2]
    slots = experts * SLOT
    vm = pltpu.VMEM
    dma = pltpu.SemaphoreType.DMA
    rows = [vm((slots, lat_w), BF) for _ in range(8)]
    spec = pl.BlockSpec(memory_space=pltpu.VMEM)
    shape = jax.ShapeDtypeStruct((1, toks, width), BF)
    return pl.pallas_call(
        functools.partial(kernel, sections, experts),
        out_shape=(shape, shape),
        in_specs=[spec] * 9,
        out_specs=(spec, spec),
        scratch_shapes=[
            vm((sections, 4, 4, 2, lat_w // experts, width), BF),
            vm((4, 4, 2, width // experts, lat_w), BF),
            vm((2, 4, 4, 2, width // experts, lat_w // sections), BF),
            vm((sections, toks, lat_w // sections), BF),
            vm((toks, width), BF),
            vm((toks, width), BF),
            vm((slots, ffh), F32),
            vm((slots, ffh), F32),
            vm((slots, ffh), BF),
            vm((slots, 2 * ffh), BF),
            *rows,
            vm((slots, 2 * toks), BF),
            vm((toks, slots), BF),
            vm((toks, slots), BF),
            vm((sections - 1, lat_w, lat_w), BF),
            vm((sections - 1, toks, lat_w), BF),
            vm((toks, lat_w), BF),
            vm((sections, toks, lat_w), BF),
            vm((sections - 1, toks, lat_w), BF),
            vm((toks, lat_w), F32),
            vm((toks, lat_w), F32),
            vm((toks, lat_w), F32),
            vm((toks, 128), F32),
            dma((4,)), dma((7,)),
            dma((sections, 5)), dma((sections, 5)),
            dma((5,)), dma((5,)),
            dma((2, 5)), dma((2, 5)),
            dma((4,)), dma((4, GROUPS)),
            dma((sections,)), dma((sections,)),
            dma((sections,)), dma((sections,)),
            dma((4,)), dma((4,)),
        ],
        compiler_params=pltpu.CompilerParams(
            collective_id=0, has_side_effects=True, vmem_limit_bytes=60 * 1024 * 1024
        ),
    )(
        tokens, cot, w_down, w_up, w_gu, w_o, jnp.swapaxes(routes, 1, 2), jnp.swapaxes(gates, 1, 2), counts
    )


def solution(mesh):
    in_specs = (
        P("expert", None),
        P("expert", None),
        P("section", "expert", None),
        P("section", "expert", None),
        P("section", "expert", None, None),
        P("section", "expert", None, None),
        P("section", "expert", None),
        P("section", "expert", None),
        P("section", "expert"),
    )
    out_specs = (P("section", "expert", None), P("section", "expert", None))
    step = functools.partial(body, mesh.shape["section"], mesh.shape["expert"])
    return jax.shard_map(step, mesh=mesh, in_specs=in_specs, out_specs=out_specs, check_vma=False)
```

```python
import functools

import jax
import jax.numpy as jnp
from jax import lax
from jax.experimental import pallas as pl
from jax.experimental.pallas import tpu as pltpu
from jax.sharding import PartitionSpec as P

EPS = 1e-05
MESH = pl.DeviceIdType.MESH
BF = jnp.bfloat16
F32 = jnp.float32
SLOT = 16
GROUPS = 2
PER = 32 // GROUPS
ORDER = sorted(
    [(dx, dy, dc) for dx in range(4) for dy in range(4) for dc in range(2) if (dx, dy, dc) != (0, 0, 0)],
    key=lambda k: -(min(k[0], 4 - k[0]) + min(k[1], 4 - k[1])),
)


def dot(a, b):
    return jnp.dot(a, b, preferred_element_type=F32)


def dot_t(a, b):
    return lax.dot_general(a, b, (((1,), (1,)), ((), ())), preferred_element_type=F32)


def swap(v):
    return jnp.concatenate([v[:, 4:8], v[:, 0:4]], axis=1)


def pack(rows):
    n, w = rows.shape[0] // SLOT, rows.shape[1] // 4
    full = rows.reshape(n, SLOT, 4 * w)
    lo, hi = full[:, 0:8], full[:, 8:16]
    used = lax.broadcasted_iota(jnp.int32, (n, 8, w), 1) < 4
    tail_lo, tail_hi = lo[:, :, 3 * w :], hi[:, :, 3 * w :]
    spare = [swap(tail_lo), tail_lo, swap(tail_hi)]
    hi = jnp.concatenate([jnp.where(used, hi[:, :, k * w : (k + 1) * w], spare[k]) for k in range(3)], axis=2)
    return jnp.concatenate([lo[:, :, 0 : 3 * w], hi], axis=1).reshape(n * SLOT, 3 * w).astype(BF)


def unpack(slabs):
    n, w = slabs.shape[0] // SLOT, slabs.shape[1] // 3
    hi = slabs.astype(F32).reshape(n, SLOT, 3 * w)[:, 8:16]
    used = lax.broadcasted_iota(jnp.int32, (n, 8, w), 1) < 4
    tail_lo = jnp.where(used, swap(hi[:, :, 0:w]), hi[:, :, w : 2 * w])
    tail = jnp.concatenate([tail_lo, swap(hi[:, :, 2 * w :])], axis=1).reshape(n * SLOT, w)
    return jnp.concatenate([slabs, tail.astype(BF)], axis=1)


def kernel(
    sections, experts,
    tokens, cot, w_down, w_up, w_gu, w_o, routes, gates, counts,
    out, gin,
    up_all, down_full, quarter, lat_q,
    x_in, g_in,
    gate_f, up_f, hidden, joined,
    send_a, recv_a, send_b, recv_b, send_c, recv_c, send_d, recv_d,
    put, take0, take1,
    m_all, mixed_in, mixed_out, q_in, q_out,
    y_f, lat_f, xw_f, inv_f,
    zs, zr, us, ur, ds, dr, fs, fr, as_, ar, ms, mr, qs, qr, gs, gr,
):
    t = lax.axis_index("section")
    e = lax.axis_index("expert")
    x = e // 8
    y = (e // 2) % 4
    c = e % 2
    above = (t + 1) % sections
    below = (t + sections - 1) % sections
    toks, width = tokens.shape
    lat_w = w_down.shape[2]
    ffh = w_o.shape[2]
    last = sections - 1

    def at(xx, yy, cc):
        return (t, (xx * 4 + yy) * 2 + cc)

    def send(src, dst, ssem, rsem, dev):
        pltpu.make_async_remote_copy(
            src_ref=src, dst_ref=dst, send_sem=ssem, recv_sem=rsem, device_id=dev, device_id_type=MESH
        ).start()

    def wait(ref, sem):
        pltpu.make_async_copy(ref, ref, sem).wait()

    def loop(n, fn):
        def step(i, carry):
            fn(i)
            return carry

        lax.fori_loop(0, n, step, 0)

    barrier = pltpu.get_barrier_semaphore()

    @functools.partial(loop, experts - 1)
    def _(k):
        pl.semaphore_signal(barrier, inc=1, device_id=(t, (e + k + 1) % experts), device_id_type=MESH)

    for k in range(1, sections):
        pl.semaphore_signal(barrier, inc=1, device_id=((t + k) % sections, e), device_id_type=MESH)
    pl.semaphore_wait(barrier, experts - 1 + sections - 1)

    def first(buf, ha, hb, ss, rs):
        for d in range(1, 4):
            blk = buf.at[(x, y, c) + ha]
            send(blk, blk, ss.at[0], rs.at[0], at((x + d) % 4, y, c))
            blk = buf.at[(x, y, c) + hb]
            send(blk, blk, ss.at[1], rs.at[1], at(x, (y + d) % 4, c))

    def second(buf, ha, hb, ss, rs):
        wait(buf.at[(pl.ds(0, 3), 0, 0) + ha], rs.at[0])
        wait(buf.at[(pl.ds(0, 3), 0, 0) + hb], rs.at[1])
        for d in range(1, 4):
            blk = buf.at[(slice(None), y, c) + ha]
            send(blk, blk, ss.at[2], rs.at[2], at(x, (y + d) % 4, c))
            blk = buf.at[(x, slice(None), c) + hb]
            send(blk, blk, ss.at[3], rs.at[3], at((x + d) % 4, y, c))

    def third(buf, ha, hb, ss, rs):
        wait(buf.at[(pl.ds(0, 3), slice(None), 0) + ha], rs.at[2])
        wait(buf.at[(pl.ds(0, 3), slice(None), 0) + hb], rs.at[3])
        blk = buf.at[:, :, c]
        send(blk, blk, ss.at[4], rs.at[4], at(x, y, 1 - c))

    def fourth(buf, ha, hb, ss, rs):
        wait(buf.at[:, :, 0], rs.at[4])

    def gather_done(buf, ha, hb, ss, rs):
        wait(buf.at[(pl.ds(0, 3), 0, 0) + ha], ss.at[0])
        wait(buf.at[(pl.ds(0, 3), 0, 0) + hb], ss.at[1])
        wait(buf.at[(pl.ds(0, 3), slice(None), 0) + ha], ss.at[2])
        wait(buf.at[(pl.ds(0, 3), slice(None), 0) + hb], ss.at[3])
        wait(buf.at[:, :, 0], ss.at[4])

    half_cols = width // 2
    half_rows = w_down.shape[1] // 2
    d_a = (pl.ds(0, half_rows), slice(None))
    d_b = (pl.ds(half_rows, half_rows), slice(None))

    def up(i):
        return (
            up_all.at[i],
            (slice(None), pl.ds(0, half_cols)),
            (slice(None), pl.ds(half_cols, half_cols)),
            us.at[i],
            ur.at[i],
        )

    down = (down_full, d_a, d_b, ds, dr)
    piece = (quarter.at[0], d_a, d_b, fs.at[0], fr.at[0])
    piece2 = (quarter.at[1], d_a, d_b, fs.at[1], fr.at[1])

    lanes = lat_w // sections

    @pl.when(t == 0)
    def _():
        for k in range(2, sections):
            send(w_down.at[0, :, pl.ds(k * lanes, lanes)], quarter.at[0, x, y, c], zs.at[0], zr.at[0], (k, e))
        quarter[0, x, y, c] = w_down[0, :, 0:lanes]
        quarter[1, x, y, c] = w_down[0, :, lanes : 2 * lanes]
        first(*piece)
        first(*piece2)

    up_all[t, x, y, c] = w_up[0]
    for k in range(1, sections):

        @pl.when(t < k)
        def _():
            send(w_up.at[0], up_all.at[t, x, y, c], zs.at[1], zr.at[1 + t], (k, e))

    @pl.when(t == last)
    def _():
        send(w_up.at[0], up_all.at[t, x, y, c], zs.at[1], zr.at[1 + t], (0, e))

    @pl.when(t > 1)
    def _():
        wait(quarter.at[0, 0, 0, 0], zr.at[0])
        first(*piece)

    def product(i):
        m_all[i] = dot(up_all[i].reshape(lat_w, width), down_full[...].reshape(width, lat_w)).astype(BF)

    def gather_first():
        down_full[x, y, c] = w_down[0]
        first(*down)

        @functools.partial(loop, t)
        def _(i):
            wait(w_up.at[0], zr.at[1 + i])
            first(*up(i))

    @pl.when(t == 1)
    def _():
        gather_first()

    x_in[...] = tokens[...]

    @pl.when(t == last)
    def _():
        g_in[...] = cot[...]

    count = counts[...]
    expert_lane = lax.broadcasted_iota(jnp.int32, (toks, experts), 1)
    live = lax.broadcasted_iota(jnp.int32, (toks, experts), 0) < count

    def column(row):
        return jnp.broadcast_to(row, (toks, toks)).T

    one0 = jnp.where((column(routes[0, 0:1])[:, 0:experts] == expert_lane) & live, 1.0, 0.0).astype(F32)
    one1 = jnp.where((column(routes[0, 1:2])[:, 0:experts] == expert_lane) & live, 1.0, 0.0).astype(F32)
    below_diag = jnp.where(
        lax.broadcasted_iota(jnp.int32, (toks, toks), 0) > lax.broadcasted_iota(jnp.int32, (toks, toks), 1), 1.0, 0.0
    ).astype(BF)
    before = dot(below_diag, (one0 + one1).astype(BF))
    slots = experts * SLOT
    spread = jnp.where(
        lax.broadcasted_iota(jnp.int32, (experts, slots), 1) // SLOT
        == lax.broadcasted_iota(jnp.int32, (experts, slots), 0),
        1.0,
        0.0,
    ).astype(BF)
    slot_no = (lax.broadcasted_iota(jnp.int32, (toks, slots), 1) % SLOT).astype(F32)
    here = dot(before.astype(BF), spread) == slot_no
    pick0 = jnp.where(here, dot(one0.astype(BF), spread), 0.0)
    pick1 = jnp.where(here, dot(one1.astype(BF), spread), 0.0)
    take0[...] = pick0.astype(BF)
    take1[...] = pick1.astype(BF)
    put[:, 0:toks] = pick0.T.astype(BF)
    put[:, toks : 2 * toks] = pick1.T.astype(BF)
    gate0 = column(gates[0, 0:1])[:, 0:1]
    gate1 = column(gates[0, 1:2])[:, 0:1]

    @pl.when(t != 1)
    def _():
        second(*piece)

    @pl.when(t == 0)
    def _():
        second(*piece2)

    chunk = 512
    n_chunks = width // chunk

    def cols_of(j):
        return slice(j * chunk, (j + 1) * chunk)

    def up_chunk(i, j):
        return up_all[i, :, :, :, :, j * chunk : (j + 1) * chunk].reshape(lat_w, chunk)

    def down_chunk(buf, j):
        return buf[j // 2, 2 * (j % 2) : 2 * (j % 2) + 2].reshape(chunk, buf.shape[-1])

    def inv_rms(square):
        return lax.rsqrt(square / width + EPS)

    square = jnp.zeros((toks, 1), F32)
    for j in range(n_chunks):
        wide = tokens[:, cols_of(j)].astype(F32)
        square += jnp.sum(wide * wide, axis=1, keepdims=True)
    inv_f[...] = jnp.broadcast_to(inv_rms(square), inv_f.shape)
    def raw_piece(k):
        total = jnp.zeros((toks, lanes), F32)
        for j in range(n_chunks):
            total += dot(tokens[:, cols_of(j)], down_chunk(quarter.at[k], j))
        return (total * inv_f[...]).astype(BF)

    @pl.when(t != 1)
    def _():
        third(*piece)

    @pl.when(t == 0)
    def _():
        third(*piece2)
        fourth(*piece2)
        lat_q[1] = raw_piece(1)

    @pl.when(t != 1)
    def _():
        fourth(*piece)
        lat_q[t] = raw_piece(0)

    @pl.when(t > 1)
    def _():
        send(lat_q.at[t], lat_q.at[t], zs.at[2], zr.at[5], (0, e))
        gather_first()

    @pl.when(t > 0)
    def _():
        second(*down)
        loop(t, lambda i: second(*up(i)))
        third(*down)
        loop(t, lambda i: third(*up(i)))
        fourth(*down)
        loop(t, lambda i: fourth(*up(i)))
        product(t - 1)

    def block(i):
        return pl.ds(pl.multiple_of(i * SLOT, SLOT), SLOT)

    def dispatch(src, dst, k):
        for pos, (dx, dy, dc) in enumerate(ORDER):
            p = (((x + dx) % 4) * 4 + (y + dy) % 4) * 2 + (c + dc) % 2
            send(src.at[block(p)], dst.at[block(pos)], as_.at[k], ar.at[k, pos // PER], (t, p))
        dst[block(experts - 1)] = src[block(e)]

    def give_back(src, dst, k, g):
        for pos, (dx, dy, dc) in enumerate(ORDER):
            if pos // PER == g:
                p = (((x + 4 - dx) % 4) * 4 + (y + 4 - dy) % 4) * 2 + (c + dc) % 2
                send(src.at[block(pos)], dst.at[block(e)], as_.at[k], ar.at[k, 0], (t, p))
        if g == GROUPS - 1:
            dst[block(e)] = src[block(experts - 1)]

    def group_arrived(buf, k, g):
        size = PER if g < GROUPS - 1 else PER - 1
        wait(buf.at[pl.ds(0, size * SLOT)], ar.at[k, g])

    def arrived(buf, k):
        wait(buf.at[pl.ds(0, (experts - 1) * SLOT)], ar.at[k, 0])

    def route_grads():
        mg = q_in[t].astype(F32)
        both = jnp.concatenate([(gate0 * mg).astype(BF), (gate1 * mg).astype(BF)], axis=0)
        send_c[...] = pack(dot(put[...], both))
        dispatch(send_c, recv_c, 2)

    def back_through(ref, i):
        total = jnp.zeros((toks, lat_w), F32)
        for j in range(n_chunks):
            total += dot_t(ref[:, cols_of(j)], up_chunk(i, j))
        return total

    @pl.when(t == last)
    def _():
        wait(q_in.at[t], qr.at[t])
        route_grads()

    def add_mixed(i):
        square = jnp.zeros((toks, 1), F32)
        for j in range(n_chunks):
            new = (x_in[:, cols_of(j)].astype(F32) + dot(mixed_in[i], up_chunk(i, j))).astype(BF)
            x_in[:, cols_of(j)] = new
            wide = new.astype(F32)
            square += jnp.sum(wide * wide, axis=1, keepdims=True)
        return square

    def pass_on(i):
        @pl.when(t < last)
        def _():
            send(mixed_in.at[i], mixed_in.at[i], ms.at[i], mr.at[i], (above, e))

    @functools.partial(loop, t - 1)
    def _(i):
        wait(mixed_in.at[i], mr.at[i])
        pass_on(i)
        add_mixed(i)

    @pl.when(t > 0)
    def _():
        total = jnp.zeros((toks, lat_w), F32)
        for j in range(n_chunks):
            total += dot(x_in[:, cols_of(j)], down_chunk(down_full, j))
        y_f[...] = total

    @pl.when(t == 0)
    def _():
        wait(lat_q.at[pl.ds(0, sections - 2)], zr.at[5])
        lat_f[...] = jnp.concatenate([lat_q[k] for k in range(sections)], axis=1).astype(F32)

    @pl.when(t > 0)
    def _():
        wait(mixed_in.at[t - 1], mr.at[t - 1])
        pass_on(t - 1)
        inv = inv_rms(add_mixed(t - 1))
        inv_f[...] = jnp.broadcast_to(inv, inv_f.shape)
        lat_f[...] = (y_f[...] + dot(mixed_in[t - 1], m_all[t - 1])) * inv

    lat = lat_f[...].astype(BF)
    send_a[...] = pack(dot(put[...], jnp.concatenate([lat, lat], axis=0)))
    dispatch(send_a, recv_a, 0)

    @pl.when(t > 0)
    def _():
        xw_f[...] = back_through(x_in, t - 1)

    @pl.when(t == last)
    def _():
        q_in[t - 1] = back_through(cot, t - 1).astype(BF)

    part = 256
    height = PER * SLOT
    for g in range(GROUPS):
        group_arrived(recv_a, 0, g)
        span = slice(g * height, (g + 1) * height)
        rows = unpack(recv_a[span])
        for j in range(ffh // part):
            lo = j * part
            a = dot(rows, w_gu[0, 0, :, lo : lo + part])
            u = dot(rows, w_gu[0, 0, :, ffh + lo : ffh + lo + part])
            sig = 1.0 / (1.0 + jnp.exp(-a))
            silu = a * sig
            hidden[span, lo : lo + part] = (silu * u).astype(BF)
            up_f[span, lo : lo + part] = silu
            gate_f[span, lo : lo + part] = u * sig * (1.0 + a * (1.0 - sig))
        send_b[span] = pack(dot(hidden[span], w_o[0, 0]))

        @pl.when(t < last)
        def _():
            give_back(send_b, recv_b, 1, g)

    def forward_finish():
        @pl.when(t == last)
        def _():
            for g in range(GROUPS):
                give_back(send_b, recv_b, 1, g)

        arrived(recv_b, 1)
        back = unpack(recv_b[...])
        mixed = (gate0 * dot(take0[...], back) + gate1 * dot(take1[...], back)).astype(BF)
        mixed_out[...] = mixed

        @pl.when(t < last)
        def _():
            send(mixed_out, mixed_in.at[t], ms.at[t], mr.at[t], (above, e))

        @pl.when(t == 0)
        def _():
            wait(w_up.at[0], zr.at[1 + last])
            for phase in (first, second, third, fourth):
                phase(*up(last))
            q_out[0] = back_through(cot, last).astype(BF)
            send(q_out.at[0], q_in.at[last], qs.at[0], qr.at[last], (last, e))

        for phase in (first, second, third, fourth):
            phase(*up(t))

        for j in range(n_chunks):
            new = x_in[:, cols_of(j)].astype(F32) + dot(mixed_out[...], up_chunk(t, j))
            out[0, :, cols_of(j)] = new.astype(BF)

        @pl.when(t == 0)
        def _():
            down_full[x, y, c] = w_down[0]
            for phase in (first, second, third, fourth):
                phase(*down)

    wide_chunk = width // 4

    def backward():
        @pl.when(t < last)
        def _():
            wait(q_in.at[t], qr.at[t])
            route_grads()

        for g in range(GROUPS):
            group_arrived(recv_c, 2, g)
            span = slice(g * height, (g + 1) * height)
            grads = unpack(recv_c[span])
            for j in range(ffh // part):
                lo = j * part
                hg = dot_t(grads, w_o[0, 0, lo : lo + part, :])
                joined[span, lo : lo + part] = (hg * gate_f[span, lo : lo + part]).astype(BF)
                joined[span, ffh + lo : ffh + lo + part] = (hg * up_f[span, lo : lo + part]).astype(BF)
            send_d[span] = pack(dot_t(joined[span], w_gu[0, 0]))
            give_back(send_d, recv_d, 3, g)

        arrived(recv_d, 3)
        back = unpack(recv_d[...])
        lg = (dot(take0[...], back) + dot(take1[...], back)).astype(BF)
        inv = inv_f[:, 0:1]
        dotted = jnp.sum(lg.astype(F32) * lat_f[...], axis=1, keepdims=True) / width
        scale = inv * inv * dotted

        def mix_grad(i, xw):
            @pl.when(t < last)
            def _():
                wait(q_in.at[i], qr.at[i])

            q_out[i] = (q_in[i].astype(F32) + inv * dot_t(lg, m_all[i]) - scale * xw).astype(BF)
            send(q_out.at[i], q_in.at[i], qs.at[i], qr.at[i], (below, e))

        @pl.when(t > 0)
        def _():
            mix_grad(t - 1, xw_f[...])

            @functools.partial(loop, t - 1)
            def _(i):
                product(i)

                @pl.when(t == last)
                def _():
                    q_in[i] = back_through(cot, i).astype(BF)

                mix_grad(i, back_through(x_in, i))

        for j in range(4):
            here = pl.ds(j * wide_chunk, wide_chunk)

            @pl.when(t < last)
            def _():
                wait(g_in.at[:, here], gr.at[j])

            for h in range(2 * j, 2 * j + 2):
                ng = dot_t(lg, down_chunk(down_full, h))
                new = g_in[:, cols_of(h)].astype(F32) + inv * ng - scale * x_in[:, cols_of(h)].astype(F32)
                gin[0, :, cols_of(h)] = new.astype(BF)

            @pl.when(t > 0)
            def _():
                send(gin.at[0, :, here], g_in.at[:, here], gs.at[j], gr.at[j], (below, e))

    def stage(i):
        @pl.when((i == 0) == (t == last))
        def _():
            backward()

        @pl.when(i == 0)
        def _():
            forward_finish()

    loop(2, stage)

    @pl.when(t == 0)
    def _():
        wait(lat_q.at[pl.ds(0, sections - 2)], zs.at[0])
        gather_done(*piece2)
        gather_done(*up(last))
        wait(q_out.at[0], qs.at[0])

    @pl.when(t > 1)
    def _():
        wait(lat_q.at[0], zs.at[2])

    @pl.when(t != 1)
    def _():
        gather_done(*piece)

    loop(jnp.where(t == last, 1, last - t), lambda i: wait(w_up.at[0], zs.at[1]))
    gather_done(*down)
    loop(t + 1, lambda i: gather_done(*up(i)))
    for k in range(4):
        wait(recv_a.at[pl.ds(0, (experts - 1) * SLOT)], as_.at[k])

    @pl.when(t < last)
    def _():
        loop(t + 1, lambda i: wait(mixed_out, ms.at[i]))

    @pl.when(t > 0)
    def _():
        loop(t, lambda i: wait(mixed_out, qs.at[i]))
        for j in range(4):
            wait(g_in.at[:, pl.ds(0, wide_chunk)], gs.at[j])


def body(sections, experts, tokens, cot, w_down, w_up, w_gu, w_o, routes, gates, counts):
    toks, width = tokens.shape
    lat_w = w_down.shape[2]
    ffh = w_o.shape[2]
    slots = experts * SLOT
    vm = pltpu.VMEM
    dma = pltpu.SemaphoreType.DMA
    rows = [vm((slots, 3 * lat_w // 4), BF) for _ in range(8)]
    spec = pl.BlockSpec(memory_space=pltpu.VMEM)
    shape = jax.ShapeDtypeStruct((1, toks, width), BF)
    return pl.pallas_call(
        functools.partial(kernel, sections, experts),
        out_shape=(shape, shape),
        in_specs=[spec] * 9,
        out_specs=(spec, spec),
        scratch_shapes=[
            vm((sections, 4, 4, 2, lat_w // experts, width), BF),
            vm((4, 4, 2, width // experts, lat_w), BF),
            vm((2, 4, 4, 2, width // experts, lat_w // sections), BF),
            vm((sections, toks, lat_w // sections), BF),
            vm((toks, width), BF),
            vm((toks, width), BF),
            vm((slots, ffh), F32),
            vm((slots, ffh), F32),
            vm((slots, ffh), BF),
            vm((slots, 2 * ffh), BF),
            *rows,
            vm((slots, 2 * toks), BF),
            vm((toks, slots), BF),
            vm((toks, slots), BF),
            vm((sections - 1, lat_w, lat_w), BF),
            vm((sections - 1, toks, lat_w), BF),
            vm((toks, lat_w), BF),
            vm((sections, toks, lat_w), BF),
            vm((sections - 1, toks, lat_w), BF),
            vm((toks, lat_w), F32),
            vm((toks, lat_w), F32),
            vm((toks, lat_w), F32),
            vm((toks, 128), F32),
            dma((4,)), dma((7,)),
            dma((sections, 5)), dma((sections, 5)),
            dma((5,)), dma((5,)),
            dma((2, 5)), dma((2, 5)),
            dma((4,)), dma((4, GROUPS)),
            dma((sections,)), dma((sections,)),
            dma((sections,)), dma((sections,)),
            dma((4,)), dma((4,)),
        ],
        compiler_params=pltpu.CompilerParams(
            collective_id=0, has_side_effects=True, vmem_limit_bytes=60 * 1024 * 1024
        ),
    )(
        tokens, cot, w_down, w_up, w_gu, w_o, jnp.swapaxes(routes, 1, 2), jnp.swapaxes(gates, 1, 2), counts
    )


def solution(mesh):
    in_specs = (
        P("expert", None),
        P("expert", None),
        P("section", "expert", None),
        P("section", "expert", None),
        P("section", "expert", None, None),
        P("section", "expert", None, None),
        P("section", "expert", None),
        P("section", "expert", None),
        P("section", "expert"),
    )
    out_specs = (P("section", "expert", None), P("section", "expert", None))
    step = functools.partial(body, mesh.shape["section"], mesh.shape["expert"])
    return jax.shard_map(step, mesh=mesh, in_specs=in_specs, out_specs=out_specs, check_vma=False)
```

```python
import functools

import jax
import jax.numpy as jnp
from jax import lax
from jax.experimental import pallas as pl
from jax.experimental.pallas import tpu as pltpu
from jax.sharding import PartitionSpec as P

EPS = 1e-05
MESH = pl.DeviceIdType.MESH
BF = jnp.bfloat16
F32 = jnp.float32
SLOT = 16
CUTS = (0, 11, 22, 32)
GROUPS = len(CUTS) - 1
ORDER = sorted(
    [(dx, dy, dc) for dx in range(4) for dy in range(4) for dc in range(2) if (dx, dy, dc) != (0, 0, 0)],
    key=lambda k: -(min(k[0], 4 - k[0]) + min(k[1], 4 - k[1])),
)


def dot(a, b):
    return jnp.dot(a, b, preferred_element_type=F32)


def dot_t(a, b):
    return lax.dot_general(a, b, (((1,), (1,)), ((), ())), preferred_element_type=F32)


def swap(v):
    return jnp.concatenate([v[:, 4:8], v[:, 0:4]], axis=1)


def pack(rows):
    n, w = rows.shape[0] // SLOT, rows.shape[1] // 4
    full = rows.reshape(n, SLOT, 4 * w)
    lo, hi = full[:, 0:8], full[:, 8:16]
    used = lax.broadcasted_iota(jnp.int32, (n, 8, w), 1) < 4
    tail_lo, tail_hi = lo[:, :, 3 * w :], hi[:, :, 3 * w :]
    spare = [swap(tail_lo), tail_lo, swap(tail_hi)]
    hi = jnp.concatenate([jnp.where(used, hi[:, :, k * w : (k + 1) * w], spare[k]) for k in range(3)], axis=2)
    return jnp.concatenate([lo[:, :, 0 : 3 * w], hi], axis=1).reshape(n * SLOT, 3 * w).astype(BF)


def unpack(slabs):
    n, w = slabs.shape[0] // SLOT, slabs.shape[1] // 3
    hi = slabs.astype(F32).reshape(n, SLOT, 3 * w)[:, 8:16]
    used = lax.broadcasted_iota(jnp.int32, (n, 8, w), 1) < 4
    tail_lo = jnp.where(used, swap(hi[:, :, 0:w]), hi[:, :, w : 2 * w])
    tail = jnp.concatenate([tail_lo, swap(hi[:, :, 2 * w :])], axis=1).reshape(n * SLOT, w)
    return jnp.concatenate([slabs, tail.astype(BF)], axis=1)


def kernel(
    sections, experts,
    tokens_hbm, cot_hbm, w_down, w_up, w_gu_hbm, w_o_hbm, routes, gates, counts,
    out_hbm, gin_hbm,
    cot, w_gu, w_o, out, gin, ins, outs,
    up_all, down_full, quarter, lat_q,
    x_in, g_in,
    gate_f, up_f, hidden, joined,
    send_a, recv_a, send_b, recv_b, send_c, recv_c, send_d, recv_d,
    put, take0, take1,
    m_all, mixed_in, mixed_out, q_in, q_out,
    y_f, lat_f, xw_f, inv_f,
    zs, zr, us, ur, ds, dr, fs, fr, as_, ar, ms, mr, qs, qr, gs, gr,
):
    t = lax.axis_index("section")
    e = lax.axis_index("expert")
    x = e // 8
    y = (e // 2) % 4
    c = e % 2
    above = (t + 1) % sections
    below = (t + sections - 1) % sections
    toks, width = tokens_hbm.shape
    lat_w = w_down.shape[2]
    ffh = w_o_hbm.shape[2]
    last = sections - 1

    def at(xx, yy, cc):
        return (t, (xx * 4 + yy) * 2 + cc)

    def send(src, dst, ssem, rsem, dev):
        pltpu.make_async_remote_copy(
            src_ref=src, dst_ref=dst, send_sem=ssem, recv_sem=rsem, device_id=dev, device_id_type=MESH
        ).start()

    def wait(ref, sem):
        pltpu.make_async_copy(ref, ref, sem).wait()

    def loop(n, fn):
        def step(i, carry):
            fn(i)
            return carry

        lax.fori_loop(0, n, step, 0)

    loads = [
        pltpu.make_async_copy(src, dst, ins.at[k])
        for k, (src, dst) in enumerate(((tokens_hbm, x_in), (w_gu_hbm, w_gu), (w_o_hbm, w_o), (cot_hbm, cot)))
    ]
    for load in loads:
        load.start()

    barrier = pltpu.get_barrier_semaphore()

    @functools.partial(loop, experts - 1)
    def _(k):
        pl.semaphore_signal(barrier, inc=1, device_id=(t, (e + k + 1) % experts), device_id_type=MESH)

    for k in range(1, sections):
        pl.semaphore_signal(barrier, inc=1, device_id=((t + k) % sections, e), device_id_type=MESH)
    pl.semaphore_wait(barrier, experts - 1 + sections - 1)

    def first(buf, ha, hb, ss, rs):
        for d in range(1, 4):
            blk = buf.at[(x, y, c) + ha]
            send(blk, blk, ss.at[0], rs.at[0], at((x + d) % 4, y, c))
            blk = buf.at[(x, y, c) + hb]
            send(blk, blk, ss.at[1], rs.at[1], at(x, (y + d) % 4, c))

    def second(buf, ha, hb, ss, rs):
        wait(buf.at[(pl.ds(0, 3), 0, 0) + ha], rs.at[0])
        wait(buf.at[(pl.ds(0, 3), 0, 0) + hb], rs.at[1])
        for d in range(1, 4):
            blk = buf.at[(slice(None), y, c) + ha]
            send(blk, blk, ss.at[2], rs.at[2], at(x, (y + d) % 4, c))
            blk = buf.at[(x, slice(None), c) + hb]
            send(blk, blk, ss.at[3], rs.at[3], at((x + d) % 4, y, c))

    def third(buf, ha, hb, ss, rs):
        wait(buf.at[(pl.ds(0, 3), slice(None), 0) + ha], rs.at[2])
        wait(buf.at[(pl.ds(0, 3), slice(None), 0) + hb], rs.at[3])
        blk = buf.at[:, :, c]
        send(blk, blk, ss.at[4], rs.at[4], at(x, y, 1 - c))

    def fourth(buf, ha, hb, ss, rs):
        wait(buf.at[:, :, 0], rs.at[4])

    def gather_done(buf, ha, hb, ss, rs):
        wait(buf.at[(pl.ds(0, 3), 0, 0) + ha], ss.at[0])
        wait(buf.at[(pl.ds(0, 3), 0, 0) + hb], ss.at[1])
        wait(buf.at[(pl.ds(0, 3), slice(None), 0) + ha], ss.at[2])
        wait(buf.at[(pl.ds(0, 3), slice(None), 0) + hb], ss.at[3])
        wait(buf.at[:, :, 0], ss.at[4])

    half_cols = width // 2
    half_rows = w_down.shape[1] // 2
    d_a = (pl.ds(0, half_rows), slice(None))
    d_b = (pl.ds(half_rows, half_rows), slice(None))

    def up(i):
        return (
            up_all.at[i],
            (slice(None), pl.ds(0, half_cols)),
            (slice(None), pl.ds(half_cols, half_cols)),
            us.at[i],
            ur.at[i],
        )

    down = (down_full, d_a, d_b, ds, dr)
    piece = (quarter.at[0], d_a, d_b, fs.at[0], fr.at[0])
    piece2 = (quarter.at[1], d_a, d_b, fs.at[1], fr.at[1])

    lanes = lat_w // sections

    @pl.when(t == 0)
    def _():
        for k in range(2, sections):
            send(w_down.at[0, :, pl.ds(k * lanes, lanes)], quarter.at[0, x, y, c], zs.at[0], zr.at[0], (k, e))
        quarter[0, x, y, c] = w_down[0, :, 0:lanes]
        quarter[1, x, y, c] = w_down[0, :, lanes : 2 * lanes]
        first(*piece)
        first(*piece2)

    up_all[t, x, y, c] = w_up[0]
    for k in range(1, sections):

        @pl.when(t < k)
        def _():
            send(w_up.at[0], up_all.at[t, x, y, c], zs.at[1], zr.at[1 + t], (k, e))

    @pl.when(t == last)
    def _():
        send(w_up.at[0], up_all.at[t, x, y, c], zs.at[1], zr.at[1 + t], (0, e))

    @pl.when(t > 1)
    def _():
        wait(quarter.at[0, 0, 0, 0], zr.at[0])
        first(*piece)

    def product(i):
        m_all[i] = dot(up_all[i].reshape(lat_w, width), down_full[...].reshape(width, lat_w)).astype(BF)

    def gather_first():
        down_full[x, y, c] = w_down[0]
        first(*down)

        @functools.partial(loop, t)
        def _(i):
            wait(w_up.at[0], zr.at[1 + i])
            first(*up(i))

    @pl.when(t == 1)
    def _():
        gather_first()

    count = counts[...]
    expert_lane = lax.broadcasted_iota(jnp.int32, (toks, experts), 1)
    live = lax.broadcasted_iota(jnp.int32, (toks, experts), 0) < count

    def column(row):
        return jnp.broadcast_to(row, (toks, toks)).T

    one0 = jnp.where((column(routes[0, 0:1])[:, 0:experts] == expert_lane) & live, 1.0, 0.0).astype(F32)
    one1 = jnp.where((column(routes[0, 1:2])[:, 0:experts] == expert_lane) & live, 1.0, 0.0).astype(F32)
    below_diag = jnp.where(
        lax.broadcasted_iota(jnp.int32, (toks, toks), 0) > lax.broadcasted_iota(jnp.int32, (toks, toks), 1), 1.0, 0.0
    ).astype(BF)
    before = dot(below_diag, (one0 + one1).astype(BF))
    slots = experts * SLOT
    spread = jnp.where(
        lax.broadcasted_iota(jnp.int32, (experts, slots), 1) // SLOT
        == lax.broadcasted_iota(jnp.int32, (experts, slots), 0),
        1.0,
        0.0,
    ).astype(BF)
    slot_no = (lax.broadcasted_iota(jnp.int32, (toks, slots), 1) % SLOT).astype(F32)
    here = dot(before.astype(BF), spread) == slot_no
    pick0 = jnp.where(here, dot(one0.astype(BF), spread), 0.0)
    pick1 = jnp.where(here, dot(one1.astype(BF), spread), 0.0)
    take0[...] = pick0.astype(BF)
    take1[...] = pick1.astype(BF)
    put[:, 0:toks] = pick0.T.astype(BF)
    put[:, toks : 2 * toks] = pick1.T.astype(BF)
    gate0 = column(gates[0, 0:1])[:, 0:1]
    gate1 = column(gates[0, 1:2])[:, 0:1]

    @pl.when(t != 1)
    def _():
        second(*piece)

    @pl.when(t == 0)
    def _():
        second(*piece2)

    chunk = 512
    n_chunks = width // chunk

    def cols_of(j):
        return slice(j * chunk, (j + 1) * chunk)

    def up_chunk(i, j):
        return up_all[i, :, :, :, :, j * chunk : (j + 1) * chunk].reshape(lat_w, chunk)

    def down_chunk(buf, j):
        return buf[j // 2, 2 * (j % 2) : 2 * (j % 2) + 2].reshape(chunk, buf.shape[-1])

    def inv_rms(square):
        return lax.rsqrt(square / width + EPS)

    loads[0].wait()
    square = jnp.zeros((toks, 1), F32)
    for j in range(n_chunks):
        wide = x_in[:, cols_of(j)].astype(F32)
        square += jnp.sum(wide * wide, axis=1, keepdims=True)
    inv_f[...] = jnp.broadcast_to(inv_rms(square), inv_f.shape)
    def raw_piece(k):
        total = jnp.zeros((toks, lanes), F32)
        for j in range(n_chunks):
            total += dot(x_in[:, cols_of(j)], down_chunk(quarter.at[k], j))
        return (total * inv_f[...]).astype(BF)

    @pl.when(t != 1)
    def _():
        third(*piece)

    @pl.when(t == 0)
    def _():
        third(*piece2)
        fourth(*piece2)
        lat_q[1] = raw_piece(1)

    @pl.when(t != 1)
    def _():
        fourth(*piece)
        lat_q[t] = raw_piece(0)

    @pl.when(t > 1)
    def _():
        send(lat_q.at[t], lat_q.at[t], zs.at[2], zr.at[5], (0, e))
        gather_first()

    @pl.when(t > 0)
    def _():
        second(*down)
        loop(t, lambda i: second(*up(i)))
        third(*down)
        loop(t, lambda i: third(*up(i)))
        fourth(*down)
        loop(t, lambda i: fourth(*up(i)))
        product(t - 1)

    for load in loads[1:]:
        load.wait()

    def block(i):
        return pl.ds(pl.multiple_of(i * SLOT, SLOT), SLOT)

    def dispatch(src, dst, k):
        for pos, (dx, dy, dc) in enumerate(ORDER):
            p = (((x + dx) % 4) * 4 + (y + dy) % 4) * 2 + (c + dc) % 2
            g = sum(pos >= cut for cut in CUTS[1:])
            send(src.at[block(p)], dst.at[block(pos)], as_.at[k], ar.at[k, g], (t, p))
        dst[block(experts - 1)] = src[block(e)]

    def give_back(src, dst, k, g):
        for pos, (dx, dy, dc) in enumerate(ORDER):
            if CUTS[g] <= pos < CUTS[g + 1]:
                p = (((x + 4 - dx) % 4) * 4 + (y + 4 - dy) % 4) * 2 + (c + dc) % 2
                send(src.at[block(pos)], dst.at[block(e)], as_.at[k], ar.at[k, 0], (t, p))
        if g == GROUPS - 1:
            dst[block(e)] = src[block(experts - 1)]

    def group_arrived(buf, k, g):
        size = CUTS[g + 1] - CUTS[g] - (g == GROUPS - 1)
        wait(buf.at[pl.ds(0, size * SLOT)], ar.at[k, g])

    def arrived(buf, k):
        wait(buf.at[pl.ds(0, (experts - 1) * SLOT)], ar.at[k, 0])

    def route_grads():
        mg = q_in[t].astype(F32)
        both = jnp.concatenate([(gate0 * mg).astype(BF), (gate1 * mg).astype(BF)], axis=0)
        send_c[...] = pack(dot(put[...], both))
        dispatch(send_c, recv_c, 2)

    def back_through(ref, i):
        total = jnp.zeros((toks, lat_w), F32)
        for j in range(n_chunks):
            total += dot_t(ref[:, cols_of(j)], up_chunk(i, j))
        return total

    @pl.when(t == last)
    def _():
        g_in[...] = cot[...]
        wait(q_in.at[t], qr.at[t])
        route_grads()

    def add_mixed(i):
        square = jnp.zeros((toks, 1), F32)
        for j in range(n_chunks):
            new = (x_in[:, cols_of(j)].astype(F32) + dot(mixed_in[i], up_chunk(i, j))).astype(BF)
            x_in[:, cols_of(j)] = new
            wide = new.astype(F32)
            square += jnp.sum(wide * wide, axis=1, keepdims=True)
        return square

    def pass_on(i):
        @pl.when(t < last)
        def _():
            send(mixed_in.at[i], mixed_in.at[i], ms.at[i], mr.at[i], (above, e))

    @functools.partial(loop, t - 1)
    def _(i):
        wait(mixed_in.at[i], mr.at[i])
        pass_on(i)
        add_mixed(i)

    @pl.when(t > 0)
    def _():
        total = jnp.zeros((toks, lat_w), F32)
        for j in range(n_chunks):
            total += dot(x_in[:, cols_of(j)], down_chunk(down_full, j))
        y_f[...] = total

    @pl.when(t == 0)
    def _():
        wait(lat_q.at[pl.ds(0, sections - 2)], zr.at[5])
        lat_f[...] = jnp.concatenate([lat_q[k] for k in range(sections)], axis=1).astype(F32)

    @pl.when(t > 0)
    def _():
        wait(mixed_in.at[t - 1], mr.at[t - 1])
        pass_on(t - 1)
        inv = inv_rms(add_mixed(t - 1))
        inv_f[...] = jnp.broadcast_to(inv, inv_f.shape)
        lat_f[...] = (y_f[...] + dot(mixed_in[t - 1], m_all[t - 1])) * inv

    lat = lat_f[...].astype(BF)
    send_a[...] = pack(dot(put[...], jnp.concatenate([lat, lat], axis=0)))
    dispatch(send_a, recv_a, 0)

    @pl.when(t > 0)
    def _():
        xw_f[...] = back_through(x_in, t - 1)

    @pl.when(t == last)
    def _():
        q_in[t - 1] = back_through(cot, t - 1).astype(BF)

    part = 256
    for g in range(GROUPS):
        group_arrived(recv_a, 0, g)
        span = slice(CUTS[g] * SLOT, CUTS[g + 1] * SLOT)
        rows = unpack(recv_a[span])
        for j in range(ffh // part):
            lo = j * part
            a = dot(rows, w_gu[0, 0, :, lo : lo + part])
            u = dot(rows, w_gu[0, 0, :, ffh + lo : ffh + lo + part])
            sig = 1.0 / (1.0 + jnp.exp(-a))
            silu = a * sig
            hidden[span, lo : lo + part] = (silu * u).astype(BF)
            up_f[span, lo : lo + part] = silu
            gate_f[span, lo : lo + part] = u * sig * (1.0 + a * (1.0 - sig))
        send_b[span] = pack(dot(hidden[span], w_o[0, 0]))

        @pl.when(t < last)
        def _():
            give_back(send_b, recv_b, 1, g)

    store_out = pltpu.make_async_copy(out, out_hbm, outs.at[0])

    def forward_finish():
        @pl.when(t == last)
        def _():
            for g in range(GROUPS):
                give_back(send_b, recv_b, 1, g)

        arrived(recv_b, 1)
        back = unpack(recv_b[...])
        mixed = (gate0 * dot(take0[...], back) + gate1 * dot(take1[...], back)).astype(BF)
        mixed_out[...] = mixed

        @pl.when(t < last)
        def _():
            send(mixed_out, mixed_in.at[t], ms.at[t], mr.at[t], (above, e))

        @pl.when(t == 0)
        def _():
            wait(w_up.at[0], zr.at[1 + last])
            for phase in (first, second, third, fourth):
                phase(*up(last))
            q_out[0] = back_through(cot, last).astype(BF)
            send(q_out.at[0], q_in.at[last], qs.at[0], qr.at[last], (last, e))

        for phase in (first, second, third, fourth):
            phase(*up(t))

        for j in range(n_chunks):
            new = x_in[:, cols_of(j)].astype(F32) + dot(mixed_out[...], up_chunk(t, j))
            out[0, :, cols_of(j)] = new.astype(BF)
        store_out.start()

        @pl.when(t == 0)
        def _():
            down_full[x, y, c] = w_down[0]
            for phase in (first, second, third, fourth):
                phase(*down)

    wide_chunk = width // 4

    def backward():
        @pl.when(t < last)
        def _():
            wait(q_in.at[t], qr.at[t])
            route_grads()

        for g in range(GROUPS):
            group_arrived(recv_c, 2, g)
            span = slice(CUTS[g] * SLOT, CUTS[g + 1] * SLOT)
            grads = unpack(recv_c[span])
            for j in range(ffh // part):
                lo = j * part
                hg = dot_t(grads, w_o[0, 0, lo : lo + part, :])
                joined[span, lo : lo + part] = (hg * gate_f[span, lo : lo + part]).astype(BF)
                joined[span, ffh + lo : ffh + lo + part] = (hg * up_f[span, lo : lo + part]).astype(BF)
            send_d[span] = pack(dot_t(joined[span], w_gu[0, 0]))
            give_back(send_d, recv_d, 3, g)

        arrived(recv_d, 3)
        back = unpack(recv_d[...])
        lg = (dot(take0[...], back) + dot(take1[...], back)).astype(BF)
        inv = inv_f[:, 0:1]
        dotted = jnp.sum(lg.astype(F32) * lat_f[...], axis=1, keepdims=True) / width
        scale = inv * inv * dotted

        def mix_grad(i, xw):
            @pl.when(t < last)
            def _():
                wait(q_in.at[i], qr.at[i])

            q_out[i] = (q_in[i].astype(F32) + inv * dot_t(lg, m_all[i]) - scale * xw).astype(BF)
            send(q_out.at[i], q_in.at[i], qs.at[i], qr.at[i], (below, e))

        @pl.when(t > 0)
        def _():
            mix_grad(t - 1, xw_f[...])

            @functools.partial(loop, t - 1)
            def _(i):
                product(i)

                @pl.when(t == last)
                def _():
                    q_in[i] = back_through(cot, i).astype(BF)

                mix_grad(i, back_through(x_in, i))

        for j in range(4):
            here = pl.ds(j * wide_chunk, wide_chunk)

            @pl.when(t < last)
            def _():
                wait(g_in.at[:, here], gr.at[j])

            for h in range(2 * j, 2 * j + 2):
                ng = dot_t(lg, down_chunk(down_full, h))
                new = g_in[:, cols_of(h)].astype(F32) + inv * ng - scale * x_in[:, cols_of(h)].astype(F32)
                gin[0, :, cols_of(h)] = new.astype(BF)

            @pl.when(t > 0)
            def _():
                send(gin.at[0, :, here], g_in.at[:, here], gs.at[j], gr.at[j], (below, e))

            pltpu.make_async_copy(gin.at[:, :, here], gin_hbm.at[:, :, here], outs.at[1 + j]).start()

    def stage(i):
        @pl.when((i == 0) == (t == last))
        def _():
            backward()

        @pl.when(i == 0)
        def _():
            forward_finish()

    loop(2, stage)

    store_out.wait()
    for j in range(4):
        here = pl.ds(j * wide_chunk, wide_chunk)
        pltpu.make_async_copy(gin.at[:, :, here], gin_hbm.at[:, :, here], outs.at[1 + j]).wait()

    @pl.when(t == 0)
    def _():
        wait(lat_q.at[pl.ds(0, sections - 2)], zs.at[0])
        gather_done(*piece2)
        gather_done(*up(last))
        wait(q_out.at[0], qs.at[0])

    @pl.when(t > 1)
    def _():
        wait(lat_q.at[0], zs.at[2])

    @pl.when(t != 1)
    def _():
        gather_done(*piece)

    loop(jnp.where(t == last, 1, last - t), lambda i: wait(w_up.at[0], zs.at[1]))
    gather_done(*down)
    loop(t + 1, lambda i: gather_done(*up(i)))
    for k in range(4):
        wait(recv_a.at[pl.ds(0, (experts - 1) * SLOT)], as_.at[k])

    @pl.when(t < last)
    def _():
        loop(t + 1, lambda i: wait(mixed_out, ms.at[i]))

    @pl.when(t > 0)
    def _():
        loop(t, lambda i: wait(mixed_out, qs.at[i]))
        for j in range(4):
            wait(g_in.at[:, pl.ds(0, wide_chunk)], gs.at[j])


def hand_over(out, gin, out_to, gin_to, held, loads, stores):
    rows = out.shape[1] // 4
    ways = []
    for k in range(8):
        src, dst = ((out, out_to), (gin, gin_to))[k // 4]
        part = pl.ds((k % 4) * rows, rows)
        slot = held.at[k // 4, :, part]
        ways.append(
            (
                pltpu.make_async_copy(src.at[:, part], slot, loads.at[k]),
                pltpu.make_async_copy(slot, dst.at[:, part], stores.at[k]),
            )
        )
    for load, _ in ways:
        load.start()
    for load, store in ways:
        load.wait()
        store.start()
    for _, store in ways:
        store.wait()


def body(sections, experts, tokens, cot, w_down, w_up, w_gu, w_o, routes, gates, counts):
    toks, width = tokens.shape
    lat_w = w_down.shape[2]
    ffh = w_o.shape[2]
    slots = experts * SLOT
    vm = pltpu.VMEM
    dma = pltpu.SemaphoreType.DMA
    rows = [vm((slots, 3 * lat_w // 4), BF) for _ in range(8)]
    spec = pl.BlockSpec(memory_space=pltpu.VMEM)
    shape = jax.ShapeDtypeStruct((1, toks, width), BF)
    hbm = pl.BlockSpec(memory_space=pl.ANY)
    results = pl.pallas_call(
        functools.partial(kernel, sections, experts),
        out_shape=(shape, shape),
        in_specs=[hbm, hbm, spec, spec, hbm, hbm, spec, spec, spec],
        out_specs=(hbm, hbm),
        scratch_shapes=[
            vm((toks, width), BF),
            vm(w_gu.shape, BF),
            vm(w_o.shape, BF),
            vm((1, toks, width), BF),
            vm((1, toks, width), BF),
            dma((4,)), dma((5,)),
            vm((sections, 4, 4, 2, lat_w // experts, width), BF),
            vm((4, 4, 2, width // experts, lat_w), BF),
            vm((2, 4, 4, 2, width // experts, lat_w // sections), BF),
            vm((sections, toks, lat_w // sections), BF),
            vm((toks, width), BF),
            vm((toks, width), BF),
            vm((slots, ffh), F32),
            vm((slots, ffh), F32),
            vm((slots, ffh), BF),
            vm((slots, 2 * ffh), BF),
            *rows,
            vm((slots, 2 * toks), BF),
            vm((toks, slots), BF),
            vm((toks, slots), BF),
            vm((sections - 1, lat_w, lat_w), BF),
            vm((sections - 1, toks, lat_w), BF),
            vm((toks, lat_w), BF),
            vm((sections, toks, lat_w), BF),
            vm((sections - 1, toks, lat_w), BF),
            vm((toks, lat_w), F32),
            vm((toks, lat_w), F32),
            vm((toks, lat_w), F32),
            vm((toks, 128), F32),
            dma((4,)), dma((7,)),
            dma((sections, 5)), dma((sections, 5)),
            dma((5,)), dma((5,)),
            dma((2, 5)), dma((2, 5)),
            dma((4,)), dma((4, GROUPS)),
            dma((sections,)), dma((sections,)),
            dma((sections,)), dma((sections,)),
            dma((4,)), dma((4,)),
        ],
        compiler_params=pltpu.CompilerParams(
            collective_id=0, has_side_effects=True, vmem_limit_bytes=60 * 1024 * 1024
        ),
    )(
        tokens, cot, w_down, w_up, w_gu, w_o, jnp.swapaxes(routes, 1, 2), jnp.swapaxes(gates, 1, 2), counts
    )
    return pl.pallas_call(
        hand_over,
        out_shape=(shape, shape),
        in_specs=[hbm, hbm],
        out_specs=(hbm, hbm),
        scratch_shapes=[vm((2, 1, toks, width), BF), dma((8,)), dma((8,))],
        compiler_params=pltpu.CompilerParams(vmem_limit_bytes=60 * 1024 * 1024),
    )(*results)


def solution(mesh):
    in_specs = (
        P("expert", None),
        P("expert", None),
        P("section", "expert", None),
        P("section", "expert", None),
        P("section", "expert", None, None),
        P("section", "expert", None, None),
        P("section", "expert", None),
        P("section", "expert", None),
        P("section", "expert"),
    )
    out_specs = (P("section", "expert", None), P("section", "expert", None))
    step = functools.partial(body, mesh.shape["section"], mesh.shape["expert"])
    return jax.shard_map(step, mesh=mesh, in_specs=in_specs, out_specs=out_specs, check_vma=False)
```

```python
import functools

import jax
import jax.numpy as jnp
from jax import lax
from jax.experimental import pallas as pl
from jax.experimental.pallas import tpu as pltpu
from jax.sharding import PartitionSpec as P

EPS = 1e-05
MESH = pl.DeviceIdType.MESH
BF = jnp.bfloat16
F32 = jnp.float32
SLOT = 16
CUTS = (0, 11, 22, 32)
GROUPS = len(CUTS) - 1
ORDER = sorted(
    [(dx, dy, dc) for dx in range(4) for dy in range(4) for dc in range(2) if (dx, dy, dc) != (0, 0, 0)],
    key=lambda k: -(min(k[0], 4 - k[0]) + min(k[1], 4 - k[1])),
)


def dot(a, b):
    return jnp.dot(a, b, preferred_element_type=F32)


def dot_t(a, b):
    return lax.dot_general(a, b, (((1,), (1,)), ((), ())), preferred_element_type=F32)


def swap(v):
    return jnp.concatenate([v[:, 4:8], v[:, 0:4]], axis=1)


def pack(rows):
    n, w = rows.shape[0] // SLOT, rows.shape[1] // 4
    full = rows.reshape(n, SLOT, 4 * w)
    lo, hi = full[:, 0:8], full[:, 8:16]
    used = lax.broadcasted_iota(jnp.int32, (n, 8, w), 1) < 4
    tail_lo, tail_hi = lo[:, :, 3 * w :], hi[:, :, 3 * w :]
    spare = [swap(tail_lo), tail_lo, swap(tail_hi)]
    hi = jnp.concatenate([jnp.where(used, hi[:, :, k * w : (k + 1) * w], spare[k]) for k in range(3)], axis=2)
    return jnp.concatenate([lo[:, :, 0 : 3 * w], hi], axis=1).reshape(n * SLOT, 3 * w).astype(BF)


def unpack(slabs):
    n, w = slabs.shape[0] // SLOT, slabs.shape[1] // 3
    hi = slabs.astype(F32).reshape(n, SLOT, 3 * w)[:, 8:16]
    used = lax.broadcasted_iota(jnp.int32, (n, 8, w), 1) < 4
    tail_lo = jnp.where(used, swap(hi[:, :, 0:w]), hi[:, :, w : 2 * w])
    tail = jnp.concatenate([tail_lo, swap(hi[:, :, 2 * w :])], axis=1).reshape(n * SLOT, w)
    return jnp.concatenate([slabs, tail.astype(BF)], axis=1)


def kernel(
    sections, experts,
    tokens_hbm, cot_hbm, w_down, w_up, w_gu_hbm, w_o_hbm, routes, gates, counts,
    out_hbm, gin_hbm,
    cot, w_gu, w_o, w_gu_t, w_o_t, out, gin, ins, outs,
    up_all, down_full, quarter, lat_q,
    x_in, g_in,
    gate_f, up_f, hidden, joined,
    send_a, recv_a, send_b, recv_b, send_c, recv_c, send_d, recv_d,
    put, take0, take1,
    m_all, mixed_in, mixed_out, q_in, q_out,
    y_f, lat_f, xw_f, inv_f,
    zs, zr, us, ur, ds, dr, fs, fr, as_, ar, ms, mr, qs, qr, gs, gr,
):
    t = lax.axis_index("section")
    e = lax.axis_index("expert")
    x = e // 8
    y = (e // 2) % 4
    c = e % 2
    above = (t + 1) % sections
    below = (t + sections - 1) % sections
    toks, width = tokens_hbm.shape
    lat_w = w_down.shape[2]
    ffh = w_o_hbm.shape[2]
    last = sections - 1

    def at(xx, yy, cc):
        return (t, (xx * 4 + yy) * 2 + cc)

    def send(src, dst, ssem, rsem, dev):
        pltpu.make_async_remote_copy(
            src_ref=src, dst_ref=dst, send_sem=ssem, recv_sem=rsem, device_id=dev, device_id_type=MESH
        ).start()

    def wait(ref, sem):
        pltpu.make_async_copy(ref, ref, sem).wait()

    def loop(n, fn):
        def step(i, carry):
            fn(i)
            return carry

        lax.fori_loop(0, n, step, 0)

    loads = [
        pltpu.make_async_copy(src, dst, ins.at[k])
        for k, (src, dst) in enumerate(((tokens_hbm, x_in), (w_gu_hbm, w_gu), (w_o_hbm, w_o), (cot_hbm, cot)))
    ]
    for load in loads:
        load.start()

    barrier = pltpu.get_barrier_semaphore()

    @functools.partial(loop, experts - 1)
    def _(k):
        pl.semaphore_signal(barrier, inc=1, device_id=(t, (e + k + 1) % experts), device_id_type=MESH)

    for k in range(1, sections):
        pl.semaphore_signal(barrier, inc=1, device_id=((t + k) % sections, e), device_id_type=MESH)
    pl.semaphore_wait(barrier, experts - 1 + sections - 1)

    def first(buf, ha, hb, ss, rs):
        for d in range(1, 4):
            blk = buf.at[(x, y, c) + ha]
            send(blk, blk, ss.at[0], rs.at[0], at((x + d) % 4, y, c))
            blk = buf.at[(x, y, c) + hb]
            send(blk, blk, ss.at[1], rs.at[1], at(x, (y + d) % 4, c))

    def second(buf, ha, hb, ss, rs):
        wait(buf.at[(pl.ds(0, 3), 0, 0) + ha], rs.at[0])
        wait(buf.at[(pl.ds(0, 3), 0, 0) + hb], rs.at[1])
        for d in range(1, 4):
            blk = buf.at[(slice(None), y, c) + ha]
            send(blk, blk, ss.at[2], rs.at[2], at(x, (y + d) % 4, c))
            blk = buf.at[(x, slice(None), c) + hb]
            send(blk, blk, ss.at[3], rs.at[3], at((x + d) % 4, y, c))

    def third(buf, ha, hb, ss, rs):
        wait(buf.at[(pl.ds(0, 3), slice(None), 0) + ha], rs.at[2])
        wait(buf.at[(pl.ds(0, 3), slice(None), 0) + hb], rs.at[3])
        blk = buf.at[:, :, c]
        send(blk, blk, ss.at[4], rs.at[4], at(x, y, 1 - c))

    def fourth(buf, ha, hb, ss, rs):
        wait(buf.at[:, :, 0], rs.at[4])

    def gather_done(buf, ha, hb, ss, rs):
        wait(buf.at[(pl.ds(0, 3), 0, 0) + ha], ss.at[0])
        wait(buf.at[(pl.ds(0, 3), 0, 0) + hb], ss.at[1])
        wait(buf.at[(pl.ds(0, 3), slice(None), 0) + ha], ss.at[2])
        wait(buf.at[(pl.ds(0, 3), slice(None), 0) + hb], ss.at[3])
        wait(buf.at[:, :, 0], ss.at[4])

    half_cols = width // 2
    half_rows = w_down.shape[1] // 2
    d_a = (pl.ds(0, half_rows), slice(None))
    d_b = (pl.ds(half_rows, half_rows), slice(None))

    def up(i):
        return (
            up_all.at[i],
            (slice(None), pl.ds(0, half_cols)),
            (slice(None), pl.ds(half_cols, half_cols)),
            us.at[i],
            ur.at[i],
        )

    down = (down_full, d_a, d_b, ds, dr)

    def piece(k):
        return (quarter.at[k], d_a, d_b, fs.at[k], fr.at[k])

    own_pieces = sections - 1
    ends = (t == 0) | (t == last)

    lanes = lat_w // sections

    @pl.when(t == 0)
    def _():
        there = w_down.at[0, :, pl.ds(own_pieces * lanes, lanes)]
        send(there, quarter.at[0, x, y, c], zs.at[0], zr.at[0], (last, e))
        for k in range(own_pieces):
            quarter[k, x, y, c] = w_down[0, :, k * lanes : (k + 1) * lanes]
            first(*piece(k))

    up_all[t, x, y, c] = w_up[0]
    for k in range(1, sections):

        @pl.when(t < k)
        def _():
            send(w_up.at[0], up_all.at[t, x, y, c], zs.at[1], zr.at[1 + t], (k, e))

    @pl.when(t == last)
    def _():
        send(w_up.at[0], up_all.at[t, x, y, c], zs.at[1], zr.at[1 + t], (0, e))

    @pl.when(t == last)
    def _():
        wait(quarter.at[0, 0, 0, 0], zr.at[0])
        first(*piece(0))

    def product(i):
        m_all[i] = dot(up_all[i].reshape(lat_w, width), down_full[...].reshape(width, lat_w)).astype(BF)

    def gather_first():
        down_full[x, y, c] = w_down[0]
        first(*down)

        @functools.partial(loop, t)
        def _(i):
            wait(w_up.at[0], zr.at[1 + i])
            first(*up(i))

    @pl.when((t > 0) & (t < last))
    def _():
        gather_first()

    count = counts[...]
    expert_lane = lax.broadcasted_iota(jnp.int32, (toks, experts), 1)
    live = lax.broadcasted_iota(jnp.int32, (toks, experts), 0) < count

    def column(row):
        return jnp.broadcast_to(row, (toks, toks)).T

    one0 = jnp.where((column(routes[0, 0:1])[:, 0:experts] == expert_lane) & live, 1.0, 0.0).astype(F32)
    one1 = jnp.where((column(routes[0, 1:2])[:, 0:experts] == expert_lane) & live, 1.0, 0.0).astype(F32)
    below_diag = jnp.where(
        lax.broadcasted_iota(jnp.int32, (toks, toks), 0) > lax.broadcasted_iota(jnp.int32, (toks, toks), 1), 1.0, 0.0
    ).astype(BF)
    before = dot(below_diag, (one0 + one1).astype(BF))
    slots = experts * SLOT
    spread = jnp.where(
        lax.broadcasted_iota(jnp.int32, (experts, slots), 1) // SLOT
        == lax.broadcasted_iota(jnp.int32, (experts, slots), 0),
        1.0,
        0.0,
    ).astype(BF)
    slot_no = (lax.broadcasted_iota(jnp.int32, (toks, slots), 1) % SLOT).astype(F32)
    here = dot(before.astype(BF), spread) == slot_no
    pick0 = jnp.where(here, dot(one0.astype(BF), spread), 0.0)
    pick1 = jnp.where(here, dot(one1.astype(BF), spread), 0.0)
    take0[...] = pick0.astype(BF)
    take1[...] = pick1.astype(BF)
    put[:, 0:toks] = pick0.T.astype(BF)
    put[:, toks : 2 * toks] = pick1.T.astype(BF)
    gate0 = column(gates[0, 0:1])[:, 0:1]
    gate1 = column(gates[0, 1:2])[:, 0:1]

    def extra(fn):
        @pl.when(t == 0)
        def _():
            for k in range(1, own_pieces):
                fn(k)

    @pl.when(ends)
    def _():
        second(*piece(0))

    extra(lambda k: second(*piece(k)))

    chunk = 512
    n_chunks = width // chunk

    def cols_of(j):
        return slice(j * chunk, (j + 1) * chunk)

    def up_chunk(i, j):
        return up_all[i, :, :, :, :, j * chunk : (j + 1) * chunk].reshape(lat_w, chunk)

    def down_chunk(buf, j):
        return buf[j // 2, 2 * (j % 2) : 2 * (j % 2) + 2].reshape(chunk, buf.shape[-1])

    def inv_rms(square):
        return lax.rsqrt(square / width + EPS)

    loads[0].wait()
    square = jnp.zeros((toks, 1), F32)
    for j in range(n_chunks):
        wide = x_in[:, cols_of(j)].astype(F32)
        square += jnp.sum(wide * wide, axis=1, keepdims=True)
    inv_f[...] = jnp.broadcast_to(inv_rms(square), inv_f.shape)
    def raw_piece(k):
        total = jnp.zeros((toks, lanes), F32)
        for j in range(n_chunks):
            total += dot(x_in[:, cols_of(j)], down_chunk(quarter.at[k], j))
        return (total * inv_f[...]).astype(BF)

    @pl.when(ends)
    def _():
        third(*piece(0))

    extra(lambda k: third(*piece(k)))

    @pl.when(ends)
    def _():
        fourth(*piece(0))
        lat_q[t] = raw_piece(0)

    @pl.when(t == 0)
    def _():
        for k in range(1, own_pieces):
            fourth(*piece(k))
            lat_q[k] = raw_piece(k)

    @pl.when(t == last)
    def _():
        send(lat_q.at[t], lat_q.at[t], zs.at[2], zr.at[5], (0, e))
        gather_first()

    @pl.when(t > 0)
    def _():
        second(*down)
        loop(t, lambda i: second(*up(i)))
        third(*down)
        loop(t, lambda i: third(*up(i)))
        fourth(*down)
        loop(t, lambda i: fourth(*up(i)))
        product(t - 1)

    for load in loads[1:]:
        load.wait()

    def turn_weights():
        for j in range(ffh // 256):
            w_o_t[:, j * 256 : (j + 1) * 256] = w_o[0, 0, j * 256 : (j + 1) * 256, :].T
        for j in range(2 * ffh // 256):
            w_gu_t[j * 256 : (j + 1) * 256, :] = w_gu[0, 0, :, j * 256 : (j + 1) * 256].T

    @pl.when(t == last)
    def _():
        turn_weights()

    def block(i):
        return pl.ds(pl.multiple_of(i * SLOT, SLOT), SLOT)

    def dispatch(src, dst, k):
        for pos, (dx, dy, dc) in enumerate(ORDER):
            p = (((x + dx) % 4) * 4 + (y + dy) % 4) * 2 + (c + dc) % 2
            g = sum(pos >= cut for cut in CUTS[1:])
            send(src.at[block(p)], dst.at[block(pos)], as_.at[k], ar.at[k, g], (t, p))
        dst[block(experts - 1)] = src[block(e)]

    def give_back(src, dst, k, g):
        for pos, (dx, dy, dc) in enumerate(ORDER):
            if CUTS[g] <= pos < CUTS[g + 1]:
                p = (((x + 4 - dx) % 4) * 4 + (y + 4 - dy) % 4) * 2 + (c + dc) % 2
                send(src.at[block(pos)], dst.at[block(e)], as_.at[k], ar.at[k, 0], (t, p))
        if g == GROUPS - 1:
            dst[block(e)] = src[block(experts - 1)]

    def group_arrived(buf, k, g):
        size = CUTS[g + 1] - CUTS[g] - (g == GROUPS - 1)
        wait(buf.at[pl.ds(0, size * SLOT)], ar.at[k, g])

    def arrived(buf, k):
        wait(buf.at[pl.ds(0, (experts - 1) * SLOT)], ar.at[k, 0])

    def route_grads():
        mg = q_in[t].astype(F32)
        both = jnp.concatenate([(gate0 * mg).astype(BF), (gate1 * mg).astype(BF)], axis=0)
        send_c[...] = pack(dot(put[...], both))
        dispatch(send_c, recv_c, 2)

    def back_through(ref, i):
        total = jnp.zeros((toks, lat_w), F32)
        for j in range(n_chunks):
            total += dot_t(ref[:, cols_of(j)], up_chunk(i, j))
        return total

    @pl.when(t == last)
    def _():
        g_in[...] = cot[...]
        wait(q_in.at[t], qr.at[t])
        route_grads()

    def add_mixed(i):
        square = jnp.zeros((toks, 1), F32)
        for j in range(n_chunks):
            new = (x_in[:, cols_of(j)].astype(F32) + dot(mixed_in[i], up_chunk(i, j))).astype(BF)
            x_in[:, cols_of(j)] = new
            wide = new.astype(F32)
            square += jnp.sum(wide * wide, axis=1, keepdims=True)
        return square

    def pass_on(i):
        @pl.when(t < last)
        def _():
            send(mixed_in.at[i], mixed_in.at[i], ms.at[i], mr.at[i], (above, e))

    @functools.partial(loop, t - 1)
    def _(i):
        wait(mixed_in.at[i], mr.at[i])
        pass_on(i)
        add_mixed(i)

    @pl.when(t > 0)
    def _():
        total = jnp.zeros((toks, lat_w), F32)
        for j in range(n_chunks):
            total += dot(x_in[:, cols_of(j)], down_chunk(down_full, j))
        y_f[...] = total

    @pl.when(t == 0)
    def _():
        wait(lat_q.at[last], zr.at[5])
        lat_f[...] = jnp.concatenate([lat_q[k] for k in range(sections)], axis=1).astype(F32)

    @pl.when(t > 0)
    def _():
        wait(mixed_in.at[t - 1], mr.at[t - 1])
        pass_on(t - 1)
        inv = inv_rms(add_mixed(t - 1))
        inv_f[...] = jnp.broadcast_to(inv, inv_f.shape)
        lat_f[...] = (y_f[...] + dot(mixed_in[t - 1], m_all[t - 1])) * inv

    lat = lat_f[...].astype(BF)
    send_a[...] = pack(dot(put[...], jnp.concatenate([lat, lat], axis=0)))
    dispatch(send_a, recv_a, 0)

    @pl.when(t > 0)
    def _():
        xw_f[...] = back_through(x_in, t - 1)

    @pl.when(t == last)
    def _():
        q_in[t - 1] = back_through(cot, t - 1).astype(BF)

    part = 256
    for g in range(GROUPS):
        group_arrived(recv_a, 0, g)
        span = slice(CUTS[g] * SLOT, CUTS[g + 1] * SLOT)
        rows = unpack(recv_a[span])
        for j in range(ffh // part):
            lo = j * part
            a = dot(rows, w_gu[0, 0, :, lo : lo + part])
            u = dot(rows, w_gu[0, 0, :, ffh + lo : ffh + lo + part])
            sig = 1.0 / (1.0 + jnp.exp(-a))
            silu = a * sig
            hidden[span, lo : lo + part] = (silu * u).astype(BF)
            up_f[span, lo : lo + part] = silu
            gate_f[span, lo : lo + part] = u * sig * (1.0 + a * (1.0 - sig))
        send_b[span] = pack(dot(hidden[span], w_o[0, 0]))

        @pl.when(t < last)
        def _():
            give_back(send_b, recv_b, 1, g)

    store_out = pltpu.make_async_copy(out, out_hbm, outs.at[0])

    def forward_finish():
        @pl.when(t == last)
        def _():
            for g in range(GROUPS):
                give_back(send_b, recv_b, 1, g)

        arrived(recv_b, 1)
        back = unpack(recv_b[...])
        mixed = (gate0 * dot(take0[...], back) + gate1 * dot(take1[...], back)).astype(BF)
        mixed_out[...] = mixed

        @pl.when(t < last)
        def _():
            send(mixed_out, mixed_in.at[t], ms.at[t], mr.at[t], (above, e))

        @pl.when(t == 0)
        def _():
            wait(w_up.at[0], zr.at[1 + last])
            for phase in (first, second, third, fourth):
                phase(*up(last))
            q_out[0] = back_through(cot, last).astype(BF)
            send(q_out.at[0], q_in.at[last], qs.at[0], qr.at[last], (last, e))

        for phase in (first, second, third, fourth):
            phase(*up(t))

        for j in range(n_chunks):
            new = x_in[:, cols_of(j)].astype(F32) + dot(mixed_out[...], up_chunk(t, j))
            out[0, :, cols_of(j)] = new.astype(BF)
        store_out.start()

        @pl.when(t < last)
        def _():
            turn_weights()

        @pl.when(t == 0)
        def _():
            down_full[x, y, c] = w_down[0]
            for phase in (first, second, third, fourth):
                phase(*down)

    wide_chunk = width // 4

    def backward():
        @pl.when(t < last)
        def _():
            wait(q_in.at[t], qr.at[t])
            route_grads()

        for g in range(GROUPS):
            group_arrived(recv_c, 2, g)
            span = slice(CUTS[g] * SLOT, CUTS[g + 1] * SLOT)
            grads = unpack(recv_c[span])
            for j in range(ffh // part):
                lo = j * part
                hg = dot(grads, w_o_t[:, lo : lo + part])
                joined[span, lo : lo + part] = (hg * gate_f[span, lo : lo + part]).astype(BF)
                joined[span, ffh + lo : ffh + lo + part] = (hg * up_f[span, lo : lo + part]).astype(BF)
            send_d[span] = pack(dot(joined[span], w_gu_t[...]))
            give_back(send_d, recv_d, 3, g)

        arrived(recv_d, 3)
        back = unpack(recv_d[...])
        lg = (dot(take0[...], back) + dot(take1[...], back)).astype(BF)
        inv = inv_f[:, 0:1]
        dotted = jnp.sum(lg.astype(F32) * lat_f[...], axis=1, keepdims=True) / width
        scale = inv * inv * dotted

        def mix_grad(i, xw):
            @pl.when(t < last)
            def _():
                wait(q_in.at[i], qr.at[i])

            q_out[i] = (q_in[i].astype(F32) + inv * dot_t(lg, m_all[i]) - scale * xw).astype(BF)
            send(q_out.at[i], q_in.at[i], qs.at[i], qr.at[i], (below, e))

        @pl.when(t > 0)
        def _():
            mix_grad(t - 1, xw_f[...])

            @functools.partial(loop, t - 1)
            def _(i):
                product(i)

                @pl.when(t == last)
                def _():
                    q_in[i] = back_through(cot, i).astype(BF)

                mix_grad(i, back_through(x_in, i))

        for j in range(4):
            here = pl.ds(j * wide_chunk, wide_chunk)

            @pl.when(t < last)
            def _():
                wait(g_in.at[:, here], gr.at[j])

            for h in range(2 * j, 2 * j + 2):
                ng = dot_t(lg, down_chunk(down_full, h))
                new = g_in[:, cols_of(h)].astype(F32) + inv * ng - scale * x_in[:, cols_of(h)].astype(F32)
                gin[0, :, cols_of(h)] = new.astype(BF)

            @pl.when(t > 0)
            def _():
                send(gin.at[0, :, here], g_in.at[:, here], gs.at[j], gr.at[j], (below, e))

            pltpu.make_async_copy(gin.at[:, :, here], gin_hbm.at[:, :, here], outs.at[1 + j]).start()

    def stage(i):
        @pl.when((i == 0) == (t == last))
        def _():
            backward()

        @pl.when(i == 0)
        def _():
            forward_finish()

    loop(2, stage)

    store_out.wait()
    for j in range(4):
        here = pl.ds(j * wide_chunk, wide_chunk)
        pltpu.make_async_copy(gin.at[:, :, here], gin_hbm.at[:, :, here], outs.at[1 + j]).wait()

    @pl.when(t == 0)
    def _():
        wait(lat_q.at[0], zs.at[0])
        gather_done(*up(last))
        wait(q_out.at[0], qs.at[0])

    @pl.when(t == last)
    def _():
        wait(lat_q.at[0], zs.at[2])

    @pl.when(ends)
    def _():
        gather_done(*piece(0))

    extra(lambda k: gather_done(*piece(k)))

    loop(jnp.where(t == last, 1, last - t), lambda i: wait(w_up.at[0], zs.at[1]))
    gather_done(*down)
    loop(t + 1, lambda i: gather_done(*up(i)))
    for k in range(4):
        wait(recv_a.at[pl.ds(0, (experts - 1) * SLOT)], as_.at[k])

    @pl.when(t < last)
    def _():
        loop(t + 1, lambda i: wait(mixed_out, ms.at[i]))

    @pl.when(t > 0)
    def _():
        loop(t, lambda i: wait(mixed_out, qs.at[i]))
        for j in range(4):
            wait(g_in.at[:, pl.ds(0, wide_chunk)], gs.at[j])


def hand_over(out, gin, out_to, gin_to, held, loads, stores):
    rows = out.shape[1] // 4
    ways = []
    for k in range(8):
        src, dst = ((out, out_to), (gin, gin_to))[k // 4]
        part = pl.ds((k % 4) * rows, rows)
        slot = held.at[k // 4, :, part]
        ways.append(
            (
                pltpu.make_async_copy(src.at[:, part], slot, loads.at[k]),
                pltpu.make_async_copy(slot, dst.at[:, part], stores.at[k]),
            )
        )
    for load, _ in ways:
        load.start()
    for load, store in ways:
        load.wait()
        store.start()
    for _, store in ways:
        store.wait()


def body(sections, experts, tokens, cot, w_down, w_up, w_gu, w_o, routes, gates, counts):
    toks, width = tokens.shape
    lat_w = w_down.shape[2]
    ffh = w_o.shape[2]
    slots = experts * SLOT
    vm = pltpu.VMEM
    dma = pltpu.SemaphoreType.DMA
    rows = [vm((slots, 3 * lat_w // 4), BF) for _ in range(8)]
    spec = pl.BlockSpec(memory_space=pltpu.VMEM)
    shape = jax.ShapeDtypeStruct((1, toks, width), BF)
    hbm = pl.BlockSpec(memory_space=pl.ANY)
    results = pl.pallas_call(
        functools.partial(kernel, sections, experts),
        out_shape=(shape, shape),
        in_specs=[hbm, hbm, spec, spec, hbm, hbm, spec, spec, spec],
        out_specs=(hbm, hbm),
        scratch_shapes=[
            vm((toks, width), BF),
            vm(w_gu.shape, BF),
            vm(w_o.shape, BF),
            vm((2 * ffh, lat_w), BF),
            vm((lat_w, ffh), BF),
            vm((1, toks, width), BF),
            vm((1, toks, width), BF),
            dma((4,)), dma((5,)),
            vm((sections, 4, 4, 2, lat_w // experts, width), BF),
            vm((4, 4, 2, width // experts, lat_w), BF),
            vm((sections - 1, 4, 4, 2, width // experts, lat_w // sections), BF),
            vm((sections, toks, lat_w // sections), BF),
            vm((toks, width), BF),
            vm((toks, width), BF),
            vm((slots, ffh), F32),
            vm((slots, ffh), F32),
            vm((slots, ffh), BF),
            vm((slots, 2 * ffh), BF),
            *rows,
            vm((slots, 2 * toks), BF),
            vm((toks, slots), BF),
            vm((toks, slots), BF),
            vm((sections - 1, lat_w, lat_w), BF),
            vm((sections - 1, toks, lat_w), BF),
            vm((toks, lat_w), BF),
            vm((sections, toks, lat_w), BF),
            vm((sections - 1, toks, lat_w), BF),
            vm((toks, lat_w), F32),
            vm((toks, lat_w), F32),
            vm((toks, lat_w), F32),
            vm((toks, 128), F32),
            dma((4,)), dma((7,)),
            dma((sections, 5)), dma((sections, 5)),
            dma((5,)), dma((5,)),
            dma((sections - 1, 5)), dma((sections - 1, 5)),
            dma((4,)), dma((4, GROUPS)),
            dma((sections,)), dma((sections,)),
            dma((sections,)), dma((sections,)),
            dma((4,)), dma((4,)),
        ],
        compiler_params=pltpu.CompilerParams(
            collective_id=0, has_side_effects=True, vmem_limit_bytes=60 * 1024 * 1024
        ),
    )(
        tokens, cot, w_down, w_up, w_gu, w_o, jnp.swapaxes(routes, 1, 2), jnp.swapaxes(gates, 1, 2), counts
    )
    return pl.pallas_call(
        hand_over,
        out_shape=(shape, shape),
        in_specs=[hbm, hbm],
        out_specs=(hbm, hbm),
        scratch_shapes=[vm((2, 1, toks, width), BF), dma((8,)), dma((8,))],
        compiler_params=pltpu.CompilerParams(vmem_limit_bytes=60 * 1024 * 1024),
    )(*results)


def solution(mesh):
    in_specs = (
        P("expert", None),
        P("expert", None),
        P("section", "expert", None),
        P("section", "expert", None),
        P("section", "expert", None, None),
        P("section", "expert", None, None),
        P("section", "expert", None),
        P("section", "expert", None),
        P("section", "expert"),
    )
    out_specs = (P("section", "expert", None), P("section", "expert", None))
    step = functools.partial(body, mesh.shape["section"], mesh.shape["expert"])
    return jax.shard_map(step, mesh=mesh, in_specs=in_specs, out_specs=out_specs, check_vma=False)
```

```python
import functools

import jax
import jax.numpy as jnp
from jax import lax
from jax.experimental import pallas as pl
from jax.experimental.pallas import tpu as pltpu
from jax.sharding import PartitionSpec as P

EPS = 1e-05
MESH = pl.DeviceIdType.MESH
BF = jnp.bfloat16
F32 = jnp.float32
SLOT = 16
CUTS = (0, 11, 22, 32)
GROUPS = len(CUTS) - 1
ORDER = sorted(
    [(dx, dy, dc) for dx in range(4) for dy in range(4) for dc in range(2) if (dx, dy, dc) != (0, 0, 0)],
    key=lambda k: -(min(k[0], 4 - k[0]) + min(k[1], 4 - k[1])),
)


def dot(a, b):
    return jnp.dot(a, b, preferred_element_type=F32)


def dot_t(a, b):
    return lax.dot_general(a, b, (((1,), (1,)), ((), ())), preferred_element_type=F32)


def swap(v):
    return jnp.concatenate([v[:, 4:8], v[:, 0:4]], axis=1)


def pack(rows):
    n, w = rows.shape[0] // SLOT, rows.shape[1] // 4
    full = rows.reshape(n, SLOT, 4 * w)
    lo, hi = full[:, 0:8], full[:, 8:16]
    used = lax.broadcasted_iota(jnp.int32, (n, 8, w), 1) < 4
    tail_lo, tail_hi = lo[:, :, 3 * w :], hi[:, :, 3 * w :]
    spare = [swap(tail_lo), tail_lo, swap(tail_hi)]
    hi = jnp.concatenate([jnp.where(used, hi[:, :, k * w : (k + 1) * w], spare[k]) for k in range(3)], axis=2)
    return jnp.concatenate([lo[:, :, 0 : 3 * w], hi], axis=1).reshape(n * SLOT, 3 * w).astype(BF)


def unpack(slabs):
    n, w = slabs.shape[0] // SLOT, slabs.shape[1] // 3
    hi = slabs.astype(F32).reshape(n, SLOT, 3 * w)[:, 8:16]
    used = lax.broadcasted_iota(jnp.int32, (n, 8, w), 1) < 4
    tail_lo = jnp.where(used, swap(hi[:, :, 0:w]), hi[:, :, w : 2 * w])
    tail = jnp.concatenate([tail_lo, swap(hi[:, :, 2 * w :])], axis=1).reshape(n * SLOT, w)
    return jnp.concatenate([slabs, tail.astype(BF)], axis=1)


def kernel(
    sections, experts,
    tokens_hbm, cot_hbm, w_down, w_up, w_gu_hbm, w_o_hbm, routes, gates, counts,
    out_hbm, gin_hbm,
    cot, w_gu, w_o, w_gu_t, w_o_t, out, gin, ins, outs,
    up_all, down_full, quarter, lat_q,
    x_in, g_in,
    gate_f, up_f, hidden, joined,
    send_a, recv_a, send_b, recv_b, send_c, recv_c, send_d, recv_d,
    put, take0, take1,
    m_all, mixed_in, mixed_out, q_in, q_out,
    y_f, lat_f, xw_f, inv_f,
    zs, zr, us, ur, ds, dr, fs, fr, as_, ar, ms, mr, qs, qr, gs, gr,
):
    t = lax.axis_index("section")
    e = lax.axis_index("expert")
    x = e // 8
    y = (e // 2) % 4
    c = e % 2
    above = (t + 1) % sections
    below = (t + sections - 1) % sections
    toks, width = tokens_hbm.shape
    lat_w = w_down.shape[2]
    ffh = w_o_hbm.shape[2]
    last = sections - 1

    def at(xx, yy, cc):
        return (t, (xx * 4 + yy) * 2 + cc)

    def send(src, dst, ssem, rsem, dev):
        pltpu.make_async_remote_copy(
            src_ref=src, dst_ref=dst, send_sem=ssem, recv_sem=rsem, device_id=dev, device_id_type=MESH
        ).start()

    def wait(ref, sem):
        pltpu.make_async_copy(ref, ref, sem).wait()

    def loop(n, fn):
        def step(i, carry):
            fn(i)
            return carry

        lax.fori_loop(0, n, step, 0)

    loads = [
        pltpu.make_async_copy(src, dst, ins.at[k])
        for k, (src, dst) in enumerate(((tokens_hbm, x_in), (w_gu_hbm, w_gu), (w_o_hbm, w_o), (cot_hbm, cot)))
    ]
    for load in loads:
        load.start()

    barrier = pltpu.get_barrier_semaphore()

    @functools.partial(loop, experts - 1)
    def _(k):
        pl.semaphore_signal(barrier, inc=1, device_id=(t, (e + k + 1) % experts), device_id_type=MESH)

    for k in range(1, sections):
        pl.semaphore_signal(barrier, inc=1, device_id=((t + k) % sections, e), device_id_type=MESH)

    count = counts[...]
    expert_lane = lax.broadcasted_iota(jnp.int32, (toks, experts), 1)
    live = lax.broadcasted_iota(jnp.int32, (toks, experts), 0) < count

    def column(row):
        return jnp.broadcast_to(row, (toks, toks)).T

    one0 = jnp.where((column(routes[0, 0:1])[:, 0:experts] == expert_lane) & live, 1.0, 0.0).astype(F32)
    one1 = jnp.where((column(routes[0, 1:2])[:, 0:experts] == expert_lane) & live, 1.0, 0.0).astype(F32)
    below_diag = jnp.where(
        lax.broadcasted_iota(jnp.int32, (toks, toks), 0) > lax.broadcasted_iota(jnp.int32, (toks, toks), 1), 1.0, 0.0
    ).astype(BF)
    before = dot(below_diag, (one0 + one1).astype(BF))
    slots = experts * SLOT
    spread = jnp.where(
        lax.broadcasted_iota(jnp.int32, (experts, slots), 1) // SLOT
        == lax.broadcasted_iota(jnp.int32, (experts, slots), 0),
        1.0,
        0.0,
    ).astype(BF)
    slot_no = (lax.broadcasted_iota(jnp.int32, (toks, slots), 1) % SLOT).astype(F32)
    here = dot(before.astype(BF), spread) == slot_no
    pick0 = jnp.where(here, dot(one0.astype(BF), spread), 0.0)
    pick1 = jnp.where(here, dot(one1.astype(BF), spread), 0.0)
    take0[...] = pick0.astype(BF)
    take1[...] = pick1.astype(BF)
    put[:, 0:toks] = pick0.T.astype(BF)
    put[:, toks : 2 * toks] = pick1.T.astype(BF)
    gate0 = column(gates[0, 0:1])[:, 0:1]
    gate1 = column(gates[0, 1:2])[:, 0:1]

    chunk = 512
    n_chunks = width // chunk

    def cols_of(j):
        return slice(j * chunk, (j + 1) * chunk)

    def inv_rms(square):
        return lax.rsqrt(square / width + EPS)

    loads[0].wait()
    square = jnp.zeros((toks, 1), F32)
    for j in range(n_chunks):
        wide = x_in[:, cols_of(j)].astype(F32)
        square += jnp.sum(wide * wide, axis=1, keepdims=True)
    inv_f[...] = jnp.broadcast_to(inv_rms(square), inv_f.shape)
    pl.semaphore_wait(barrier, experts - 1 + sections - 1)

    def first(buf, ha, hb, ss, rs):
        for d in range(1, 4):
            blk = buf.at[(x, y, c) + ha]
            send(blk, blk, ss.at[0], rs.at[0], at((x + d) % 4, y, c))
            blk = buf.at[(x, y, c) + hb]
            send(blk, blk, ss.at[1], rs.at[1], at(x, (y + d) % 4, c))

    def second(buf, ha, hb, ss, rs):
        wait(buf.at[(pl.ds(0, 3), 0, 0) + ha], rs.at[0])
        wait(buf.at[(pl.ds(0, 3), 0, 0) + hb], rs.at[1])
        for d in range(1, 4):
            blk = buf.at[(slice(None), y, c) + ha]
            send(blk, blk, ss.at[2], rs.at[2], at(x, (y + d) % 4, c))
            blk = buf.at[(x, slice(None), c) + hb]
            send(blk, blk, ss.at[3], rs.at[3], at((x + d) % 4, y, c))

    def third(buf, ha, hb, ss, rs):
        wait(buf.at[(pl.ds(0, 3), slice(None), 0) + ha], rs.at[2])
        wait(buf.at[(pl.ds(0, 3), slice(None), 0) + hb], rs.at[3])
        blk = buf.at[:, :, c]
        send(blk, blk, ss.at[4], rs.at[4], at(x, y, 1 - c))

    def fourth(buf, ha, hb, ss, rs):
        wait(buf.at[:, :, 0], rs.at[4])

    def gather_done(buf, ha, hb, ss, rs):
        wait(buf.at[(pl.ds(0, 3), 0, 0) + ha], ss.at[0])
        wait(buf.at[(pl.ds(0, 3), 0, 0) + hb], ss.at[1])
        wait(buf.at[(pl.ds(0, 3), slice(None), 0) + ha], ss.at[2])
        wait(buf.at[(pl.ds(0, 3), slice(None), 0) + hb], ss.at[3])
        wait(buf.at[:, :, 0], ss.at[4])

    half_cols = width // 2
    half_rows = w_down.shape[1] // 2
    d_a = (pl.ds(0, half_rows), slice(None))
    d_b = (pl.ds(half_rows, half_rows), slice(None))

    def up(i):
        return (
            up_all.at[i],
            (slice(None), pl.ds(0, half_cols)),
            (slice(None), pl.ds(half_cols, half_cols)),
            us.at[i],
            ur.at[i],
        )

    down = (down_full, d_a, d_b, ds, dr)

    def piece(k):
        return (quarter.at[k], d_a, d_b, fs.at[k], fr.at[k])

    own_pieces = sections - 1
    ends = (t == 0) | (t == last)

    lanes = lat_w // sections

    @pl.when(t == 0)
    def _():
        there = w_down.at[0, :, pl.ds(own_pieces * lanes, lanes)]
        send(there, quarter.at[0, x, y, c], zs.at[0], zr.at[0], (last, e))
        for k in range(own_pieces):
            quarter[k, x, y, c] = w_down[0, :, k * lanes : (k + 1) * lanes]
            first(*piece(k))

    up_all[t, x, y, c] = w_up[0]
    for k in range(1, sections):

        @pl.when(t < k)
        def _():
            send(w_up.at[0], up_all.at[t, x, y, c], zs.at[1], zr.at[1 + t], (k, e))

    @pl.when(t == last)
    def _():
        send(w_up.at[0], up_all.at[t, x, y, c], zs.at[1], zr.at[1 + t], (0, e))

    @pl.when(t == last)
    def _():
        wait(quarter.at[0, 0, 0, 0], zr.at[0])
        first(*piece(0))

    def product(i):
        m_all[i] = dot(up_all[i].reshape(lat_w, width), down_full[...].reshape(width, lat_w)).astype(BF)

    def gather_first():
        down_full[x, y, c] = w_down[0]
        first(*down)

        @functools.partial(loop, t)
        def _(i):
            wait(w_up.at[0], zr.at[1 + i])
            first(*up(i))

    @pl.when((t > 0) & (t < last))
    def _():
        gather_first()

    def extra(fn):
        @pl.when(t == 0)
        def _():
            for k in range(1, own_pieces):
                fn(k)

    @pl.when(ends)
    def _():
        second(*piece(0))

    extra(lambda k: second(*piece(k)))

    @pl.when(t == last)
    def _():
        gather_first()

    def up_chunk(i, j):
        return up_all[i, :, :, :, :, j * chunk : (j + 1) * chunk].reshape(lat_w, chunk)

    def down_chunk(buf, j):
        return buf[j // 2, 2 * (j % 2) : 2 * (j % 2) + 2].reshape(chunk, buf.shape[-1])

    def raw_piece(k):
        total = jnp.zeros((toks, lanes), F32)
        for j in range(n_chunks):
            total += dot(x_in[:, cols_of(j)], down_chunk(quarter.at[k], j))
        return (total * inv_f[...]).astype(BF)

    @pl.when(ends)
    def _():
        third(*piece(0))

    extra(lambda k: third(*piece(k)))

    @pl.when(ends)
    def _():
        fourth(*piece(0))
        lat_q[t] = raw_piece(0)

    @pl.when(t == 0)
    def _():
        for k in range(1, own_pieces):
            fourth(*piece(k))
            lat_q[k] = raw_piece(k)

    @pl.when(t == last)
    def _():
        send(lat_q.at[t], lat_q.at[t], zs.at[2], zr.at[5], (0, e))

    @pl.when(t > 0)
    def _():
        second(*down)
        loop(t, lambda i: second(*up(i)))
        third(*down)
        loop(t, lambda i: third(*up(i)))
        fourth(*down)
        loop(t, lambda i: fourth(*up(i)))
        product(t - 1)

    for load in loads[1:]:
        load.wait()

    def turn_weights():
        for j in range(ffh // 256):
            w_o_t[:, j * 256 : (j + 1) * 256] = w_o[0, 0, j * 256 : (j + 1) * 256, :].T
        for j in range(2 * ffh // 256):
            w_gu_t[j * 256 : (j + 1) * 256, :] = w_gu[0, 0, :, j * 256 : (j + 1) * 256].T

    @pl.when(t == last)
    def _():
        turn_weights()

    def block(i):
        return pl.ds(pl.multiple_of(i * SLOT, SLOT), SLOT)

    def dispatch(src, dst, k):
        for pos, (dx, dy, dc) in enumerate(ORDER):
            p = (((x + dx) % 4) * 4 + (y + dy) % 4) * 2 + (c + dc) % 2
            g = sum(pos >= cut for cut in CUTS[1:])
            send(src.at[block(p)], dst.at[block(pos)], as_.at[k], ar.at[k, g], (t, p))
        dst[block(experts - 1)] = src[block(e)]

    def give_back(src, dst, k, g):
        for pos, (dx, dy, dc) in enumerate(ORDER):
            if CUTS[g] <= pos < CUTS[g + 1]:
                p = (((x + 4 - dx) % 4) * 4 + (y + 4 - dy) % 4) * 2 + (c + dc) % 2
                send(src.at[block(pos)], dst.at[block(e)], as_.at[k], ar.at[k, 0], (t, p))
        if g == GROUPS - 1:
            dst[block(e)] = src[block(experts - 1)]

    def group_arrived(buf, k, g):
        size = CUTS[g + 1] - CUTS[g] - (g == GROUPS - 1)
        wait(buf.at[pl.ds(0, size * SLOT)], ar.at[k, g])

    def arrived(buf, k):
        wait(buf.at[pl.ds(0, (experts - 1) * SLOT)], ar.at[k, 0])

    def route_grads():
        mg = q_in[t].astype(F32)
        both = jnp.concatenate([(gate0 * mg).astype(BF), (gate1 * mg).astype(BF)], axis=0)
        send_c[...] = pack(dot(put[...], both))
        dispatch(send_c, recv_c, 2)

    def back_through(ref, i):
        total = jnp.zeros((toks, lat_w), F32)
        for j in range(n_chunks):
            total += dot_t(ref[:, cols_of(j)], up_chunk(i, j))
        return total

    @pl.when(t == last)
    def _():
        g_in[...] = cot[...]
        wait(q_in.at[t], qr.at[t])
        route_grads()

    def add_mixed(i):
        square = jnp.zeros((toks, 1), F32)
        for j in range(n_chunks):
            new = (x_in[:, cols_of(j)].astype(F32) + dot(mixed_in[i], up_chunk(i, j))).astype(BF)
            x_in[:, cols_of(j)] = new
            wide = new.astype(F32)
            square += jnp.sum(wide * wide, axis=1, keepdims=True)
        return square

    def pass_on(i):
        @pl.when(t < last)
        def _():
            send(mixed_in.at[i], mixed_in.at[i], ms.at[i], mr.at[i], (above, e))

    @functools.partial(loop, t - 1)
    def _(i):
        wait(mixed_in.at[i], mr.at[i])
        pass_on(i)
        add_mixed(i)

    @pl.when(t > 0)
    def _():
        total = jnp.zeros((toks, lat_w), F32)
        for j in range(n_chunks):
            total += dot(x_in[:, cols_of(j)], down_chunk(down_full, j))
        y_f[...] = total

    @pl.when(t == 0)
    def _():
        wait(lat_q.at[last], zr.at[5])
        lat_f[...] = jnp.concatenate([lat_q[k] for k in range(sections)], axis=1).astype(F32)

    @pl.when(t > 0)
    def _():
        wait(mixed_in.at[t - 1], mr.at[t - 1])
        pass_on(t - 1)
        inv = inv_rms(add_mixed(t - 1))
        inv_f[...] = jnp.broadcast_to(inv, inv_f.shape)
        lat_f[...] = (y_f[...] + dot(mixed_in[t - 1], m_all[t - 1])) * inv

    lat = lat_f[...].astype(BF)
    send_a[...] = pack(dot(put[...], jnp.concatenate([lat, lat], axis=0)))
    dispatch(send_a, recv_a, 0)

    @pl.when(t > 0)
    def _():
        xw_f[...] = back_through(x_in, t - 1)

    @pl.when(t == last)
    def _():
        q_in[t - 1] = back_through(cot, t - 1).astype(BF)

    part = 256
    for g in range(GROUPS):
        group_arrived(recv_a, 0, g)
        span = slice(CUTS[g] * SLOT, CUTS[g + 1] * SLOT)
        rows = unpack(recv_a[span])
        for j in range(ffh // part):
            lo = j * part
            a = dot(rows, w_gu[0, 0, :, lo : lo + part])
            u = dot(rows, w_gu[0, 0, :, ffh + lo : ffh + lo + part])
            sig = 1.0 / (1.0 + jnp.exp(-a))
            silu = a * sig
            hidden[span, lo : lo + part] = (silu * u).astype(BF)
            up_f[span, lo : lo + part] = silu
            gate_f[span, lo : lo + part] = u * sig * (1.0 + a * (1.0 - sig))
        send_b[span] = pack(dot(hidden[span], w_o[0, 0]))

        @pl.when(t < last)
        def _():
            give_back(send_b, recv_b, 1, g)

    store_out = pltpu.make_async_copy(out, out_hbm, outs.at[0])

    def forward_finish():
        @pl.when(t == last)
        def _():
            for g in range(GROUPS):
                give_back(send_b, recv_b, 1, g)

        arrived(recv_b, 1)
        back = unpack(recv_b[...])
        mixed = (gate0 * dot(take0[...], back) + gate1 * dot(take1[...], back)).astype(BF)
        mixed_out[...] = mixed

        @pl.when(t < last)
        def _():
            send(mixed_out, mixed_in.at[t], ms.at[t], mr.at[t], (above, e))

        @pl.when(t == 0)
        def _():
            wait(w_up.at[0], zr.at[1 + last])
            for phase in (first, second, third, fourth):
                phase(*up(last))
            q_out[0] = back_through(cot, last).astype(BF)
            send(q_out.at[0], q_in.at[last], qs.at[0], qr.at[last], (last, e))

        for phase in (first, second, third, fourth):
            phase(*up(t))

        for j in range(n_chunks):
            new = x_in[:, cols_of(j)].astype(F32) + dot(mixed_out[...], up_chunk(t, j))
            out[0, :, cols_of(j)] = new.astype(BF)
        store_out.start()

        @pl.when(t < last)
        def _():
            turn_weights()

        @pl.when(t == 0)
        def _():
            down_full[x, y, c] = w_down[0]
            for phase in (first, second, third, fourth):
                phase(*down)


    def backward():
        @pl.when(t < last)
        def _():
            wait(q_in.at[t], qr.at[t])
            route_grads()

        for g in range(GROUPS):
            group_arrived(recv_c, 2, g)
            span = slice(CUTS[g] * SLOT, CUTS[g + 1] * SLOT)
            grads = unpack(recv_c[span])
            for j in range(ffh // part):
                lo = j * part
                hg = dot(grads, w_o_t[:, lo : lo + part])
                joined[span, lo : lo + part] = (hg * gate_f[span, lo : lo + part]).astype(BF)
                joined[span, ffh + lo : ffh + lo + part] = (hg * up_f[span, lo : lo + part]).astype(BF)
            send_d[span] = pack(dot(joined[span], w_gu_t[...]))
            give_back(send_d, recv_d, 3, g)

        arrived(recv_d, 3)
        back = unpack(recv_d[...])
        lg = (dot(take0[...], back) + dot(take1[...], back)).astype(BF)
        inv = inv_f[:, 0:1]
        dotted = jnp.sum(lg.astype(F32) * lat_f[...], axis=1, keepdims=True) / width
        scale = inv * inv * dotted

        def mix_grad(i, xw):
            @pl.when(t < last)
            def _():
                wait(q_in.at[i], qr.at[i])

            q_out[i] = (q_in[i].astype(F32) + inv * dot_t(lg, m_all[i]) - scale * xw).astype(BF)
            send(q_out.at[i], q_in.at[i], qs.at[i], qr.at[i], (below, e))

        @pl.when(t > 0)
        def _():
            mix_grad(t - 1, xw_f[...])

            @functools.partial(loop, t - 1)
            def _(i):
                product(i)

                @pl.when(t == last)
                def _():
                    q_in[i] = back_through(cot, i).astype(BF)

                mix_grad(i, back_through(x_in, i))

        for j in range(n_chunks):
            here = pl.ds(j * chunk, chunk)

            @pl.when(t < last)
            def _():
                wait(g_in.at[:, here], gr.at[j])

            ng = dot_t(lg, down_chunk(down_full, j))
            new = g_in[:, cols_of(j)].astype(F32) + inv * ng - scale * x_in[:, cols_of(j)].astype(F32)
            gin[0, :, cols_of(j)] = new.astype(BF)

            @pl.when(t > 0)
            def _():
                send(gin.at[0, :, here], g_in.at[:, here], gs.at[j], gr.at[j], (below, e))

            pltpu.make_async_copy(gin.at[:, :, here], gin_hbm.at[:, :, here], outs.at[1 + j]).start()

    def stage(i):
        @pl.when((i == 0) == (t == last))
        def _():
            backward()

        @pl.when(i == 0)
        def _():
            forward_finish()

    loop(2, stage)

    store_out.wait()
    for j in range(n_chunks):
        here = pl.ds(j * chunk, chunk)
        pltpu.make_async_copy(gin.at[:, :, here], gin_hbm.at[:, :, here], outs.at[1 + j]).wait()

    @pl.when(t == 0)
    def _():
        wait(lat_q.at[0], zs.at[0])
        gather_done(*up(last))
        wait(q_out.at[0], qs.at[0])

    @pl.when(t == last)
    def _():
        wait(lat_q.at[0], zs.at[2])

    @pl.when(ends)
    def _():
        gather_done(*piece(0))

    extra(lambda k: gather_done(*piece(k)))

    loop(jnp.where(t == last, 1, last - t), lambda i: wait(w_up.at[0], zs.at[1]))
    gather_done(*down)
    loop(t + 1, lambda i: gather_done(*up(i)))
    for k in range(4):
        wait(recv_a.at[pl.ds(0, (experts - 1) * SLOT)], as_.at[k])

    @pl.when(t < last)
    def _():
        loop(t + 1, lambda i: wait(mixed_out, ms.at[i]))

    @pl.when(t > 0)
    def _():
        loop(t, lambda i: wait(mixed_out, qs.at[i]))
        for j in range(n_chunks):
            wait(g_in.at[:, pl.ds(0, chunk)], gs.at[j])


def hand_over(out, gin, out_to, gin_to, held, loads, stores):
    rows = out.shape[1] // 4
    ways = []
    for k in range(8):
        src, dst = ((out, out_to), (gin, gin_to))[k // 4]
        part = pl.ds((k % 4) * rows, rows)
        slot = held.at[k // 4, :, part]
        ways.append(
            (
                pltpu.make_async_copy(src.at[:, part], slot, loads.at[k]),
                pltpu.make_async_copy(slot, dst.at[:, part], stores.at[k]),
            )
        )
    for load, _ in ways:
        load.start()
    for load, store in ways:
        load.wait()
        store.start()
    for _, store in ways:
        store.wait()


def body(sections, experts, tokens, cot, w_down, w_up, w_gu, w_o, routes, gates, counts):
    toks, width = tokens.shape
    lat_w = w_down.shape[2]
    ffh = w_o.shape[2]
    slots = experts * SLOT
    vm = pltpu.VMEM
    dma = pltpu.SemaphoreType.DMA
    rows = [vm((slots, 3 * lat_w // 4), BF) for _ in range(8)]
    spec = pl.BlockSpec(memory_space=pltpu.VMEM)
    shape = jax.ShapeDtypeStruct((1, toks, width), BF)
    hbm = pl.BlockSpec(memory_space=pl.ANY)
    results = pl.pallas_call(
        functools.partial(kernel, sections, experts),
        out_shape=(shape, shape),
        in_specs=[hbm, hbm, spec, spec, hbm, hbm, spec, spec, spec],
        out_specs=(hbm, hbm),
        scratch_shapes=[
            vm((toks, width), BF),
            vm(w_gu.shape, BF),
            vm(w_o.shape, BF),
            vm((2 * ffh, lat_w), BF),
            vm((lat_w, ffh), BF),
            vm((1, toks, width), BF),
            vm((1, toks, width), BF),
            dma((4,)), dma((9,)),
            vm((sections, 4, 4, 2, lat_w // experts, width), BF),
            vm((4, 4, 2, width // experts, lat_w), BF),
            vm((sections - 1, 4, 4, 2, width // experts, lat_w // sections), BF),
            vm((sections, toks, lat_w // sections), BF),
            vm((toks, width), BF),
            vm((toks, width), BF),
            vm((slots, ffh), F32),
            vm((slots, ffh), F32),
            vm((slots, ffh), BF),
            vm((slots, 2 * ffh), BF),
            *rows,
            vm((slots, 2 * toks), BF),
            vm((toks, slots), BF),
            vm((toks, slots), BF),
            vm((sections - 1, lat_w, lat_w), BF),
            vm((sections - 1, toks, lat_w), BF),
            vm((toks, lat_w), BF),
            vm((sections, toks, lat_w), BF),
            vm((sections - 1, toks, lat_w), BF),
            vm((toks, lat_w), F32),
            vm((toks, lat_w), F32),
            vm((toks, lat_w), F32),
            vm((toks, 128), F32),
            dma((4,)), dma((7,)),
            dma((sections, 5)), dma((sections, 5)),
            dma((5,)), dma((5,)),
            dma((sections - 1, 5)), dma((sections - 1, 5)),
            dma((4,)), dma((4, GROUPS)),
            dma((sections,)), dma((sections,)),
            dma((sections,)), dma((sections,)),
            dma((8,)), dma((8,)),
        ],
        compiler_params=pltpu.CompilerParams(
            collective_id=0, has_side_effects=True, vmem_limit_bytes=60 * 1024 * 1024
        ),
    )(
        tokens, cot, w_down, w_up, w_gu, w_o, jnp.swapaxes(routes, 1, 2), jnp.swapaxes(gates, 1, 2), counts
    )
    return pl.pallas_call(
        hand_over,
        out_shape=(shape, shape),
        in_specs=[hbm, hbm],
        out_specs=(hbm, hbm),
        scratch_shapes=[vm((2, 1, toks, width), BF), dma((8,)), dma((8,))],
        compiler_params=pltpu.CompilerParams(vmem_limit_bytes=60 * 1024 * 1024),
    )(*results)


def solution(mesh):
    in_specs = (
        P("expert", None),
        P("expert", None),
        P("section", "expert", None),
        P("section", "expert", None),
        P("section", "expert", None, None),
        P("section", "expert", None, None),
        P("section", "expert", None),
        P("section", "expert", None),
        P("section", "expert"),
    )
    out_specs = (P("section", "expert", None), P("section", "expert", None))
    step = functools.partial(body, mesh.shape["section"], mesh.shape["expert"])
    return jax.shard_map(step, mesh=mesh, in_specs=in_specs, out_specs=out_specs, check_vma=False)
```
